32 devices in a mesh: member: 2 (over x), passage: 16 (over z, y, core).
Axes of the slice: x: 2, y: 2, z: 4, core: 2. Of those that a mesh axis runs over, the one named last changes fastest.
Arguments:
- states: bfloat16 [64, 5, 16, 2048], P('member', None, None, 'passage'), parts along dimension 0, may hold values from -6 to 6
- basis: bfloat16 [32, 5, 16, 2048], P(None, None, None, 'passage'), may hold values from -0.015625 to 0.015625
- snapshot_times: int32 [64], P('member'), parts along dimension 0, may hold values from 0 to 4095
- pert_ids: int32 [32], P(('member', 'passage')), parts along dimension 0, may hold values from 0 to 7
- pert_table: float32 [8, 16, 128], replicated, may hold values from 0 to 0.6
- cycle_ids: int32 [16, 2048], P(None, 'passage'), may hold values from 0 to 5
- groove_kernel: float32 [16], replicated, may hold values from -4 to 4
- groove_gain: float32 [5], replicated, may hold values from 0.5 to 1.5
- speed: float32 [16, 2048], P(None, 'passage'), may hold values from 0.2 to 1
- force_amp: float32 [16, 2048], P(None, 'passage'), may hold values from -6 to 6
- viscosity: float32 [5], replicated, may hold values from 0.02 to 0.2
- coupling: float32 [5, 5], replicated, may hold values from -2.5 to 2.5
Outputs:
- derivative: bfloat16 [64, 5, 16, 2048], P('member', None, None, 'passage'), parts along dimension 0
- reduced: float32 [64, 64], P(('member', 'passage')), parts along dimension 0
- operator: float32 [1120, 32], P('member'), parts along dimension 0
- fitted: float32 [64, 32], P(('member', 'passage')), parts along dimension 0
The draws below stay inside these ranges and needn't reach their ends.
There are 2 independent parts, one for each index of `member`. The reference program is written for one: setup_inputs(seed, part) draws one part's arguments, and reference() takes and returns one part's arrays. A program takes and returns all parts, laid end to end along the dimension named above; an argument that names none is the same for every part. Nothing has to cross between parts.
Inputs may be any that keep to these rules, and one draw needn't show every extreme that they name: `cycle_ids`: the value 5 marks a cell outside every groove cycle.
All inputs are finite; a program needn't handle non-finite values.
Results may differ from the reference program's by a relative error of at most 0.0031.
Values may be sent and summed in bfloat16 or wider, within the bound.
No kernel may reach another device: no remote copies, remote signals or barrier semaphores. Data moves between devices by JAX's collectives and lax.ppermute only.
A program may use at most 128 MiB of HBM per device.

```python
import math
import jax
import jax.numpy as jnp
import numpy as np
from jax import lax

NV = 5
NX = 16
TH_DEV = 128
R = 32
NRING = 5
NPERT = 8
NPASS = 16
NTH = 2048
K = 32
N_PASSAGE = 16


def place_ends(array, own_key, low, top_value):
    spot = [jax.random.randint(jax.random.fold_in(own_key, axis), (), 0, length) for axis, length in enumerate(array.shape)]
    widest = array.shape.index(max(array.shape))
    beside = spot[:widest] + [(spot[widest] + 1) % array.shape[widest]] + spot[widest + 1:]
    return array.at[tuple(spot)].set(low).at[tuple(beside)].set(top_value)


def block_levels(own_key, dims, split, low, high):
    gain = 1.0
    for axis_at, shards_of in split:
        draws = jax.random.uniform(jax.random.fold_in(jax.random.fold_in(own_key, 6), axis_at), (shards_of,), jnp.float32, low / len(split), high / len(split))
        gain = gain * jnp.repeat(jnp.exp(draws), dims[axis_at] // shards_of).reshape((-1,) + (1,) * (len(dims) - 1 - axis_at))
    return gain


def noise(own_key, dims, deviation, most, pieces=(), kind=jnp.bfloat16):
    values = deviation * jax.random.normal(own_key, dims, jnp.float32)
    if pieces:
        values = values * block_levels(own_key, dims, pieces, -0.22, 0.18)
    return jnp.clip(values, -most, most).astype(kind)


def setup_inputs(seed: int = 0, part: int = 0) -> dict:
    splits = jax.random.split(jax.random.key(seed), 13)
    part_splits = jax.random.split(jax.random.fold_in(splits[12], part), 13)
    states = noise(part_splits[0], (K, NV, NX, NTH), 1.0, 6.0, ((3, 16),))
    basis = noise(splits[1], (R, NV, NX, NTH), (NV * NX * NTH) ** -0.5, 0.015625, ((3, 16),))
    snapshot_times = place_ends(jax.random.randint(part_splits[2], (K,), 0, 4096), jax.random.fold_in(part_splits[2], 1), 0, 4095).astype(jnp.int32)
    pert_ids = place_ends(jax.random.randint(part_splits[3], (NPASS,), 0, NPERT), jax.random.fold_in(part_splits[3], 1), 0, NPERT - 1).astype(jnp.int32)
    pert_table = jnp.clip(jax.random.uniform(splits[4], (NPERT, NX, TH_DEV), jnp.float32, 0.0, 0.6), 0.0, 0.6)
    cycle_ids = place_ends(jax.random.randint(splits[5], (NX, NTH), 0, NRING + 1), jax.random.fold_in(splits[5], 1), 0, NRING).astype(jnp.int32)
    groove_kernel = noise(splits[6], (NPASS,), (max(NPASS // 8, 1)) ** -0.5, 4.0, (), jnp.float32)
    groove_gain = jnp.clip(jax.random.uniform(splits[7], (NV,), jnp.float32, 0.5, 1.5), 0.5, 1.5)
    speed = jnp.clip(0.2 + 0.8 * jax.random.uniform(splits[8], (NX, NTH), jnp.float32) ** block_levels(splits[8], (NX, NTH), ((1, 16),), -0.2, 0.2), 0.2, 1.0)
    force_amp = noise(splits[9], (NX, NTH), 1.0, 6.0, ((1, 16),), jnp.float32)
    viscosity = jnp.clip(jnp.exp(jax.random.uniform(splits[10], (NV,), jnp.float32, math.log(0.02), math.log(0.2))), 0.02, 0.2)
    coupling = noise(splits[11], (NV, NV), NV ** -0.5, 2.5, (), jnp.float32)
    return dict(states=states, basis=basis, snapshot_times=snapshot_times, pert_ids=pert_ids, pert_table=pert_table, cycle_ids=cycle_ids, groove_kernel=groove_kernel, groove_gain=groove_gain, speed=speed, force_amp=force_amp, viscosity=viscosity, coupling=coupling)


highest = lax.Precision.HIGHEST
time_step = 0.2
forcing_period = 37.0
ridge_factor = 1.0

def flux_rate(cell_values, groove, damping, speed, viscosity, coupling, groove_gain, forcing):
    east_side = jnp.roll(cell_values, -1, axis=3)
    west_side = jnp.roll(cell_values, 1, axis=3)
    padded_x = jnp.pad(cell_values, ((0, 0), (0, 0), (1, 1), (0, 0)))
    north_side = padded_x[:, :, 2:, :]
    south_side = padded_x[:, :, :-2, :]
    advection = -0.5 * speed * (east_side - west_side)
    diffusion = viscosity[None, :, None, None] * (east_side + west_side + north_side + south_side - 4.0 * cell_values)
    mixing = jnp.einsum('vw,kwxt->kvxt', coupling, cell_values, precision=highest)
    source = groove_gain[None, :, None, None] * groove[:, None] + forcing[:, None]
    return advection + diffusion + mixing - damping * cell_values + source

def reference(states, basis, snapshot_times, pert_ids, pert_table, cycle_ids, groove_kernel, groove_gain, speed, force_amp, viscosity, coupling):
    passages = N_PASSAGE
    cycle_mask = (cycle_ids[None] == jnp.arange(NRING, dtype=jnp.int32)[:, None, None]).astype(jnp.float32)
    mask_blocks = cycle_mask.reshape(NRING, NX, passages, TH_DEV)
    peer_ids = jnp.arange(passages, dtype=jnp.int32)
    circulant = groove_kernel[(peer_ids[:, None] - peer_ids[None, :]) % passages]
    damping = jnp.transpose(pert_table[pert_ids], (1, 0, 2)).reshape(NX, NTH)
    cosine = jnp.cos(2.0 * math.pi * snapshot_times.astype(jnp.float32) / forcing_period)
    forcing = force_amp[None] * cosine[:, None, None]
    cycle_scale = 1.0 / math.sqrt(NX * TH_DEV)

    def groove_of(cell_values):
        pressure = cell_values[:, NV - 1].reshape(K, NX, passages, TH_DEV)
        cycles = jnp.einsum('kxpt,gxpt->pkg', pressure, mask_blocks, precision=highest) * cycle_scale
        plenum = jnp.einsum('pq,qkg->pkg', circulant, cycles, precision=highest)
        return jnp.einsum('pkg,gxpt->kxpt', plenum, mask_blocks, precision=highest).reshape(K, NX, NTH)
    start_field = states.astype(jnp.float32)
    first_rate = flux_rate(start_field, groove_of(start_field), damping, speed, viscosity, coupling, groove_gain, forcing)
    middle = start_field + time_step * first_rate
    second_rate = flux_rate(middle, groove_of(middle), damping, speed, viscosity, coupling, groove_gain, forcing)
    derivative = (0.5 * (first_rate + second_rate)).astype(jnp.bfloat16)
    flat_basis = basis.reshape(R, -1)
    contract_dims = (((1,), (1,)), ((), ()))
    coordinates = lax.dot_general(states.reshape(K, -1).astype(jnp.float32), flat_basis.astype(jnp.float32), contract_dims, preferred_element_type=jnp.float32)
    rate_coords = lax.dot_general(derivative.reshape(K, -1).astype(jnp.float32), flat_basis.astype(jnp.float32), contract_dims, preferred_element_type=jnp.float32)
    reduced = jnp.concatenate([coordinates, rate_coords], axis=1)
    upper_first, upper_second = np.triu_indices(R)
    products = coordinates[:, upper_first] * coordinates[:, upper_second]
    design = jnp.concatenate([coordinates, products, rate_coords], axis=1)
    columns = design.shape[1]
    features = columns - R
    gram = jnp.dot(design.T, design, precision=highest) + ridge_factor * K * jnp.eye(columns, dtype=jnp.float32)
    factor_low = jnp.linalg.cholesky(gram)
    operator = lax.linalg.triangular_solve(factor_low[:features, :features], factor_low[features:, :features].T, left_side=True, lower=True, transpose_a=True)
    fitted = jnp.dot(design[:, :features], operator, precision=highest)
    return (derivative, reduced, operator, fitted)
```

```python
import functools
import math

import jax
import jax.numpy as jnp
import numpy as np
from jax import lax
from jax.experimental import pallas as pl
from jax.experimental.pallas import tpu as pltpu
from jax.sharding import PartitionSpec as P

F32 = jnp.float32
BF16 = jnp.bfloat16
NRING = 5
NV = 5
NX = 16
LANES = 128
PERIOD = 37
TIME_STEP = 0.2
RIDGE_FACTOR = 1.0
CHUNK = 32
BLOB = 16
EDGE = 48
ROWS = BLOB + 2 * EDGE

HIGH = lax.Precision.HIGHEST
NT = (((1,), (1,)), ((), ()))
VMEM = pl.BlockSpec(memory_space=pltpu.VMEM)
SMEM = pl.BlockSpec(memory_space=pltpu.SMEM)


def iota(shape, axis):
    return lax.broadcasted_iota(jnp.int32, shape, axis)


def roll(value, shift, axis):
    size = value.shape[axis]
    return pltpu.roll(value, shift % size if isinstance(shift, int) else shift, axis)


def split(value):
    high = value.astype(BF16).astype(F32)
    return high, (value - high).astype(BF16).astype(F32)


def north_south(u):
    row = iota(u.shape, 0)
    north = jnp.where(row == NX - 1, 0.0, roll(u, -1, 0))
    south = jnp.where(row == 0, 0.0, roll(u, 1, 0))
    return north + south


def cycle_masks(ids):
    return jnp.concatenate([jnp.where(ids == g, 1.0, 0.0) for g in range(NRING)], axis=0)


def lane_part():
    return iota((8, LANES), 1) % 4


def before_kernel(
    times, pert_ids, visc, coup, table, states, pert, ids_ref, speed_ref, force_ref, out, fields
):
    chunks = out.shape[0]
    speed = speed_ref[...]
    force = force_ref[...]
    damping = pert[pert_ids[0]]
    ids = ids_ref[...]
    visc_p = visc[NV - 1]
    lane = iota((NX, LANES), 1)
    half_speed = 0.5 * speed
    coef_east = jnp.where(lane == LANES - 1, 0.0, visc_p - half_speed)
    coef_west = jnp.where(lane == 0, 0.0, visc_p + half_speed)
    coef_own = coup[NV - 1, NV - 1] - 4.0 * visc_p - damping
    masks = cycle_masks(ids)
    masks_half = masks.astype(BF16)
    c8 = lane_part()
    row8 = iota((8, LANES), 0)
    quad = iota((NX, LANES), 1) // 4
    scale = 1.0 / math.sqrt(NX * LANES)

    def pieces(column):
        out16 = jnp.zeros((NX, LANES), F32)
        spot = 0
        for field in (speed, force, damping, ids.astype(F32)):
            for piece in split(field):
                moved = roll(piece, spot - column, 1)
                out16 = jnp.where(lane == spot, moved, out16)
                spot += 1
        return jnp.where(iota((8, LANES), 1) < 64, out16[:8], roll(out16[8:], 64, 1))

    params_right = pieces(LANES - 1)
    params_left = pieces(0)

    east_hi, east_lo = split(jnp.where(lane == LANES - 1, visc_p - half_speed, 0.0))
    west_hi, west_lo = split(jnp.where(lane == 0, visc_p + half_speed, 0.0))
    ids_f = ids.astype(F32)
    id_east = jnp.where(lane == LANES - 1, ids_f, 0.0)
    id_west = jnp.where(lane == 0, ids_f, 0.0)
    ones = jnp.ones((NX, LANES), BF16)
    filler = jnp.zeros((LANES - 32, LANES), F32)

    def as_rows(east, west):
        stacked = jnp.concatenate([east, west, filler], axis=0).astype(BF16)
        return lax.dot_general(ones, stacked, NT, preferred_element_type=F32)[:8]

    row_hi = as_rows(east_hi, west_hi)
    row_lo = as_rows(east_lo, west_lo)
    row_id = as_rows(id_east, id_west)
    counts = lax.dot_general(ones, masks_half, NT, preferred_element_type=F32)[:8]
    spread = jnp.where(
        iota((NRING * NX, LANES), 1) == 32 + iota((NRING * NX, LANES), 0) // NX, 1.0, 0.0
    )
    counts = jnp.dot(counts, spread, precision=HIGH, preferred_element_type=F32)
    count_hi, count_lo = split(counts)
    row_hi = row_hi + count_hi
    row_lo = row_lo + count_lo

    size = CHUNK * NX
    same_x = iota((NRING * NX, 3 * size), 0) % NX == iota((NRING * NX, 3 * size), 1) % NX
    snap_of_row = iota((size, LANES), 0) // NX == iota((size, LANES), 1) // 4
    part_of_lane = iota((size, LANES), 1) % 4
    to_start = jnp.where(snap_of_row & (part_of_lane < 2), scale, 0.0)
    to_rate = jnp.where(snap_of_row & (part_of_lane >= 2), scale, 0.0)

    def chunk_step(chunk, carry):
        first = chunk * CHUNK

        def snap(k, edges):
            u = [states[first + k, v].astype(F32) for v in range(NV)]
            p = u[NV - 1]
            cosine = table[lax.rem(times[first + k], PERIOD)]
            rate = coef_east * roll(p, -1, 1) + coef_west * roll(p, 1, 1)
            rate = rate + visc_p * north_south(p) + coef_own * p + cosine * force
            for v in range(NV - 1):
                rate = rate + coup[NV - 1, v] * u[v]
            high, low = split(rate)
            at = pl.multiple_of(k * NX, NX)
            fields[pl.ds(at, NX), :] = p.astype(BF16)
            fields[pl.ds(pl.multiple_of(size + at, NX), NX), :] = high.astype(BF16)
            fields[pl.ds(pl.multiple_of(2 * size + at, NX), NX), :] = low.astype(BF16)
            return tuple(
                jnp.where(quad == k, roll(u[v], 4 * k + 2, 1), edges[v]) for v in range(NV)
            )

        edges = tuple(jnp.zeros((NX, LANES), F32) for _ in range(NV))
        if chunks == 1:
            for k in range(CHUNK):
                edges = snap(k, edges)
        else:
            edges = lax.fori_loop(0, CHUNK, snap, edges)
        sums = lax.dot_general(masks_half, fields[...], NT, preferred_element_type=F32)
        sums = jnp.where(same_x, sums, 0.0)
        by_cycle = jnp.sum(sums.reshape(NRING, NX, 3 * size), axis=1)
        by_cycle = jnp.concatenate([by_cycle, jnp.zeros((3, 3 * size), F32)], axis=0)
        start = by_cycle[:, :size]
        rate = by_cycle[:, size : 2 * size] + by_cycle[:, 2 * size :]
        packed = jnp.dot(start, to_start, precision=HIGH, preferred_element_type=F32)
        packed += jnp.dot(rate, to_rate, precision=HIGH, preferred_element_type=F32)
        high, low = split(packed)
        packed = jnp.where(c8 % 2 == 0, high, low)
        packed = jnp.where(row8 < NRING, packed, 0.0)
        for at, row in ((5, row_hi), (6, row_lo), (7, row_id)):
            packed = jnp.where(row8 == at, row, packed)
        p_low, p_high = edges[NV - 1][:8], edges[NV - 1][8:]
        p_edges = jnp.where(
            (c8 == 1) | (c8 == 2), p_low, jnp.where(c8 == 3, roll(p_high, 1, 1), roll(p_high, -1, 1))
        )
        right = [jnp.where(c8 < 2, t[:8], roll(t[8:], 2, 1)) for t in edges]
        left = [jnp.where(c8 >= 2, t[:8], roll(t[8:], -2, 1)) for t in edges]
        rows = [packed, p_edges] + right + [params_right] + left + [params_left]
        out[chunk] = jnp.concatenate(rows, axis=0).astype(BF16)
        return carry

    if chunks == 1:
        chunk_step(0, 0)
    else:
        lax.fori_loop(0, chunks, chunk_step, 0)


def after_kernel(
    carries,
    times,
    pert_ids,
    place,
    kern,
    gain,
    visc,
    coup,
    table,
    states,
    basis,
    pert,
    ids_ref,
    speed_ref,
    force_ref,
    own_ref,
    near_ref,
    *rest,
):
    carry_refs = rest[:carries]
    low_ref, high_ref, deriv, partial, mixed, raw, cyc0, cyc1, grooves, halo0, halo1 = rest[carries:]
    chunks = own_ref.shape[0]
    passages = kern.shape[0]
    half = passages // 2
    me = place[0]
    odd = me % 2 == 1
    speed = speed_ref[...]
    force = force_ref[...]
    damping = pert[pert_ids[0]]
    ids = ids_ref[...]
    half_speed = 0.5 * speed
    lane = iota((NX, LANES), 1)
    c16 = lane % 4
    masks = cycle_masks(ids).astype(BF16)
    masks_twice = jnp.concatenate([masks, masks], axis=0)
    scale = 1.0 / math.sqrt(NX * LANES)
    size = CHUNK * NX

    src = iota((LANES, LANES), 0)
    dst = iota((LANES, LANES), 1) // 4 * 4
    mixers = [(src == dst) | (src == dst + 1), (src == dst + 2) | (src == dst + 3)]
    mixers += [src == dst + 2, src == dst + 1, src == dst + 3, src == dst]
    mix = jnp.concatenate([jnp.where(m, 1.0, 0.0).astype(BF16) for m in mixers], axis=1)
    pick_snap = jnp.where(iota((size, LANES), 1) == iota((size, LANES), 0) // NX * 4, 1.0, 0.0)
    pick_snap = pick_snap.astype(BF16)
    wide = 4 * NRING * NX
    same_x = iota((size, wide), 0) % NX == iota((size, wide), 1) % NX

    def unpack_right(t):
        return jnp.concatenate([t, roll(t, -2, 1)], axis=0)

    def unpack_left(t):
        return jnp.concatenate([t, roll(t, 2, 1)], axis=0)

    def chunk_step(chunk, carry):
        first = chunk * CHUNK
        raw[: half * BLOB, :] = low_ref[chunk, : half * BLOB, :].astype(F32)
        raw[half * BLOB :, :] = high_ref[chunk, : half * BLOB, :].astype(F32)
        mixed[...] = jnp.dot(raw[...].astype(BF16), mix, preferred_element_type=F32)

        def slot(offset):
            other = lax.rem(me + offset + passages, passages)
            return pl.multiple_of(jnp.bitwise_xor(me, other) * BLOB, BLOB)

        def load(offset, carry):
            cyc0[pl.ds(pl.multiple_of(offset * 8, 8), 8), :] = mixed[pl.ds(slot(offset), 8), :LANES]
            return carry

        lax.fori_loop(0, passages, load, 0, unroll=passages <= 16)

        def plenum0(offset):
            total = jnp.zeros((8, LANES), F32)
            if passages <= 16 and isinstance(offset, int):
                for other in range(passages):
                    total += kern[(offset - other) % passages] * cyc0[other * 8 : other * 8 + 8, :]
                return total

            def add(other, total):
                weight = kern[lax.rem(offset - other + 2 * passages, passages)]
                return total + weight * cyc0[pl.ds(pl.multiple_of(other * 8, 8), 8), :]

            return lax.fori_loop(0, passages, add, total)

        row8 = iota((8, LANES), 0)
        lane8 = iota((8, LANES), 1)

        def second(offset, total):
            own = slot(offset)
            east, west = slot(offset + 1), slot(offset - 1)
            coefs = raw[pl.ds(own, 8), :]
            id_row = coefs[7:8, :].astype(jnp.int32)
            hit = (id_row == row8) & (lane8 < 32)
            left = jnp.concatenate(
                [jnp.where(hit, coefs[5:6, :], 0.0), jnp.where(hit, coefs[6:7, :], 0.0)], axis=0
            )
            right = jnp.concatenate(
                [
                    mixed[pl.ds(pl.multiple_of(east + 8, 8), 8), 2 * LANES : 3 * LANES],
                    mixed[pl.ds(pl.multiple_of(east + 8, 8), 8), 4 * LANES : 5 * LANES],
                    mixed[pl.ds(pl.multiple_of(west + 8, 8), 8), 3 * LANES : 4 * LANES],
                    mixed[pl.ds(pl.multiple_of(west + 8, 8), 8), 5 * LANES :],
                    jnp.zeros((LANES - 32, LANES), F32),
                ],
                axis=0,
            )
            edge = jnp.dot(left.astype(BF16), right.astype(BF16), preferred_element_type=F32)
            edge = (edge[:8] + edge[8:]) * scale
            count = jnp.where(lane8 == 32 + row8, coefs[5:6, :] + coefs[6:7, :], 0.0)
            count = jnp.sum(count, axis=1, keepdims=True) * (scale * gain[NV - 1])
            rate = mixed[pl.ds(own, 8), LANES : 2 * LANES] + edge + count * plenum0(offset)
            if isinstance(offset, int):
                start = cyc0[offset * 8 : offset * 8 + 8, :]
                weight = kern[-offset % passages]
            else:
                start = cyc0[pl.ds(pl.multiple_of(offset * 8, 8), 8), :]
                weight = kern[lax.rem(passages - offset, passages)]
            return total + weight * (start + TIME_STEP * rate)

        total = jnp.zeros((8, LANES), F32)
        if passages <= 16:
            for offset in range(passages):
                total = second(offset, total)
        else:
            total = lax.fori_loop(0, passages, second, total)
        own0, own1 = plenum0(0), total
        west0, east0 = plenum0(passages - 1), plenum0(1)

        stack = []
        for tile in (own0, own1):
            for piece in split(tile):
                stack += [jnp.broadcast_to(piece[g : g + 1], (NX, LANES)) for g in range(NRING)]
        stack = jnp.concatenate(stack, axis=0).astype(BF16)
        picked = lax.dot_general(pick_snap, stack, NT, preferred_element_type=F32)
        picked = jnp.where(same_x, picked, 0.0).astype(BF16)
        for stage in range(2):
            grooves[stage] = jnp.dot(
                picked[:, stage * wide // 2 : (stage + 1) * wide // 2],
                masks_twice,
                preferred_element_type=F32,
            )

        far = carry_refs[-1][chunk, -EDGE:, :].astype(F32)
        for index in range(carries - 2, -1, -1):
            bit = jnp.bitwise_and(jnp.right_shift(me, index + 1), 1)
            arrived = (bit == 1) != odd
            far = jnp.where(arrived, carry_refs[index][chunk, -EDGE:, :].astype(F32), far)
        near = near_ref[chunk].astype(F32)
        own = own_ref[chunk].astype(F32)
        west = jnp.where(odd, near[BLOB : BLOB + EDGE], far)
        east = jnp.where(odd, far, near[BLOB + EDGE :])

        def param(side, index):
            t = side[40:48]
            low = t[:, index : index + 1] + t[:, index + 1 : index + 2]
            high = t[:, 64 + index : 65 + index] + t[:, 65 + index : 66 + index]
            return jnp.broadcast_to(jnp.concatenate([low, high], axis=0), (NX, LANES))

        speed_h, force_h, damp_h, ids_h = (
            jnp.where(c16 < 2, param(west, 2 * i), param(east, 2 * i)) for i in range(4)
        )
        groove_h = jnp.zeros((NX, LANES), F32)
        for g in range(NRING):
            value = jnp.where(c16 < 2, west0[g : g + 1], east0[g : g + 1])
            groove_h = jnp.where(ids_h == g, value, groove_h)
        cos_h = jnp.zeros((NX, LANES), F32)
        for k in range(CHUNK):
            cos_h = jnp.where(lane // 4 == k, table[lax.rem(times[first + k], PERIOD)], cos_h)
        halo = []
        ours = []
        for v in range(NV):
            at = slice(8 * v, 8 * v + 8)
            halo.append(jnp.where(c16 < 2, unpack_right(west[at]), unpack_left(east[at])))
            mine = slice(BLOB + 8 * v, BLOB + 8 * v + 8)
            mine_left = slice(BLOB + EDGE + 8 * v, BLOB + EDGE + 8 * v + 8)
            ours.append(jnp.where(c16 < 2, unpack_right(own[mine]), unpack_left(own[mine_left])))
        for v in range(NV):
            h = halo[v]
            e = roll(jnp.where(c16 == 3, h, ours[v]), -1, 1)
            w = roll(jnp.where(c16 == 0, h, ours[v]), 1, 1)
            rate = visc[v] * (e + w + north_south(h) - 4.0 * h) - 0.5 * speed_h * (e - w)
            rate = rate - damp_h * h + gain[v] * groove_h + force_h * cos_h
            for other in range(NV):
                rate = rate + coup[v, other] * halo[other]
            halo0[v] = h
            halo1[v] = h + TIME_STEP * rate

        def flux(u, halos, source, spread):
            result = []
            for v in range(NV):
                h = roll(halos[v], spread, 1)
                e = roll(jnp.where(lane == 0, h, u[v]), -1, 1)
                w = roll(jnp.where(lane == LANES - 1, h, u[v]), 1, 1)
                rate = visc[v] * (e + w + north_south(u[v])) - half_speed * (e - w)
                rate = rate + (coup[v, v] - 4.0 * visc[v] - damping) * u[v]
                for other in range(NV):
                    if other != v:
                        rate = rate + coup[v, other] * u[other]
                result.append(rate + gain[v] * source[0] + source[1])
            return result

        def snap(k, carry):
            u = [states[first + k, v].astype(F32) for v in range(NV)]
            drive = table[lax.rem(times[first + k], PERIOD)] * force
            at = pl.multiple_of(k * NX, NX)
            spread = -(4 * k + 2) if isinstance(k, int) else 2 * LANES - 4 * k - 2
            rate0 = flux(u, halo0, (grooves[0, pl.ds(at, NX), :], drive), spread)
            middle = [u[v] + TIME_STEP * rate0[v] for v in range(NV)]
            rate1 = flux(middle, halo1, (grooves[1, pl.ds(at, NX), :], drive), spread)
            for v in range(NV):
                deriv[first + k, v] = (0.5 * (rate0[v] + rate1[v])).astype(BF16)
            return carry

        if chunks == 1:
            for k in range(CHUNK):
                snap(k, 0)
        else:
            lax.fori_loop(0, CHUNK, snap, 0)

        modes = basis.shape[0]
        flat_basis = jnp.concatenate(
            [basis[:, v].reshape(modes * NX, LANES) for v in range(NV)], axis=1
        )
        diagonal = (
            iota((size, modes * NX), 0) % NX == iota((size, modes * NX), 1) % NX
        )
        mode_of = iota((modes * NX, 2 * modes), 0) // NX
        column = iota((modes * NX, 2 * modes), 1)
        total = jnp.zeros((CHUNK, 2 * modes), F32)
        for part, source in ((0, states), (1, deriv)):
            rows = jnp.concatenate(
                [source[pl.ds(first, CHUNK), v].reshape(size, LANES) for v in range(NV)], axis=1
            )
            pairs = lax.dot_general(rows, flat_basis, NT, preferred_element_type=F32)
            pairs = jnp.where(diagonal, pairs, 0.0)
            pairs = jnp.sum(pairs.reshape(CHUNK, NX, modes * NX), axis=1)
            gather = jnp.where(mode_of + part * modes == column, 1.0, 0.0)
            total += jnp.dot(pairs, gather, precision=HIGH, preferred_element_type=F32)
        partial[pl.ds(pl.multiple_of(first, CHUNK), CHUNK), :] = total
        return carry

    if chunks == 1:
        chunk_step(0, 0)
    else:
        lax.fori_loop(0, chunks, chunk_step, 0)


def fit_kernel(ridge, place, red_ref, first_ref, second_ref, lin_ref, reduced, operator, fitted, full):
    snaps, modes = red_ref.shape[0], red_ref.shape[1] // 2
    red = red_ref[...]
    coords = red[:, :modes]
    rates = red[:, modes:]
    dot = functools.partial(
        lax.dot_general, precision=HIGH, preferred_element_type=F32
    )
    gram = dot(coords, coords, NT)
    squares = coords * coords
    kernel = gram + 0.5 * (gram * gram + dot(squares, squares, NT))
    eye = jnp.where(iota((snaps, snaps), 0) == iota((snaps, snaps), 1), ridge, 0.0)
    system = jnp.concatenate([kernel + eye, rates], axis=1)
    width = snaps + modes
    row = iota((snaps, width), 0)
    for j in range(snaps):
        pivot = system[j : j + 1, :] / system[j : j + 1, j : j + 1]
        factor = jnp.where(row == j, 0.0, jnp.broadcast_to(system[:, j : j + 1], (snaps, width)))
        system = jnp.where(row == j, pivot, system - factor * pivot)
    solved = system[:, snaps:]
    one = (((1,), (0,)), ((), ()))
    design = dot(coords, first_ref[...], one) * (dot(coords, second_ref[...], one) + lin_ref[...])
    operator[...] = dot(design, solved, (((0,), (0,)), ((), ())))
    full[...] = dot(kernel, solved, one)
    each = fitted.shape[0]
    for i in range(each):
        fitted[i : i + 1, :] = full[pl.ds(place[0] * each + i, 1), :]
        reduced[i : i + 1, :] = red_ref[pl.ds(place[0] * each + i, 1), :]


def body(
    states,
    basis,
    snapshot_times,
    pert_ids,
    pert_table,
    cycle_ids,
    groove_kernel,
    groove_gain,
    speed,
    force_amp,
    viscosity,
    coupling,
):
    snaps = states.shape[0]
    modes = basis.shape[0]
    chunks = snaps // CHUNK
    passages = lax.axis_size("passage")
    rounds = passages.bit_length() - 1
    position = lax.axis_index("passage")
    place = position.reshape(1).astype(jnp.int32)
    angles = 2.0 * math.pi * np.arange(PERIOD) / PERIOD
    table = jnp.asarray(np.cos(angles).astype(np.float32))

    def swap(value, mask):
        pairs = [(i, i ^ mask) for i in range(passages)]
        return lax.ppermute(value, "passage", pairs)

    first = pl.pallas_call(
        before_kernel,
        out_shape=jax.ShapeDtypeStruct((chunks, ROWS, LANES), BF16),
        in_specs=[SMEM] * 5 + [VMEM] * 5,
        out_specs=VMEM,
        scratch_shapes=[pltpu.VMEM((3 * CHUNK * NX, LANES), BF16)],
        compiler_params=pltpu.CompilerParams(vmem_limit_bytes=40 * 2**20),
        name="before",
    )(
        snapshot_times,
        pert_ids,
        viscosity,
        coupling,
        table,
        states,
        pert_table,
        cycle_ids,
        speed,
        force_amp,
    )
    near = swap(first, 1)
    group = jnp.concatenate([first[:, :BLOB], near[:, :BLOB]], axis=1)
    odd = position % 2
    carry = lax.dynamic_slice_in_dim(near, BLOB + EDGE * odd, EDGE, axis=1)
    carries = []
    for r in range(1, rounds):
        message = jnp.concatenate([group, carry], axis=1)
        if r > 1:
            carries.append(message)
        got = swap(message, 1 << r)
        carry = got[:, -EDGE:]
        if r < rounds - 1:
            group = jnp.concatenate([group, got[:, :-EDGE]], axis=1)
    carries.append(got)

    derivative, partial = pl.pallas_call(
        functools.partial(after_kernel, len(carries)),
        out_shape=(
            jax.ShapeDtypeStruct(states.shape, BF16),
            jax.ShapeDtypeStruct((snaps, 2 * modes), F32),
        ),
        in_specs=[SMEM] * 8 + [VMEM] * (10 + len(carries)),
        out_specs=(VMEM, VMEM),
        scratch_shapes=[
            pltpu.VMEM((passages * BLOB, 6 * LANES), F32),
            pltpu.VMEM((passages * BLOB, LANES), F32),
            pltpu.VMEM((passages * 8, LANES), F32),
            pltpu.VMEM((passages * 8, LANES), F32),
            pltpu.VMEM((2, CHUNK * NX, LANES), F32),
            pltpu.VMEM((NV, NX, LANES), F32),
            pltpu.VMEM((NV, NX, LANES), F32),
        ],
        compiler_params=pltpu.CompilerParams(vmem_limit_bytes=48 * 2**20),
        name="after",
    )(
        snapshot_times,
        pert_ids,
        place,
        groove_kernel,
        groove_gain,
        viscosity,
        coupling,
        table,
        states,
        basis,
        pert_table,
        cycle_ids,
        speed,
        force_amp,
        first,
        near,
        *carries,
        message,
        got,
    )
    total = partial
    for r in range(rounds):
        total = total + swap(total, 1 << r)

    upper_first, upper_second = np.triu_indices(modes)
    features = modes + len(upper_first)
    pick_first = np.zeros((modes, features), np.float32)
    pick_second = np.zeros((modes, features), np.float32)
    linear = np.zeros((1, features), np.float32)
    pick_first[np.arange(modes), np.arange(modes)] = 1.0
    linear[0, :modes] = 1.0
    pick_first[upper_first, modes + np.arange(len(upper_first))] = 1.0
    pick_second[upper_second, modes + np.arange(len(upper_first))] = 1.0
    each = snaps // passages
    reduced, operator, fitted = pl.pallas_call(
        functools.partial(fit_kernel, RIDGE_FACTOR * snaps),
        out_shape=(
            jax.ShapeDtypeStruct((each, 2 * modes), F32),
            jax.ShapeDtypeStruct((features, modes), F32),
            jax.ShapeDtypeStruct((each, modes), F32),
        ),
        in_specs=[SMEM] + [VMEM] * 4,
        out_specs=(VMEM, VMEM, VMEM),
        scratch_shapes=[pltpu.VMEM((snaps, modes), F32)],
        compiler_params=pltpu.CompilerParams(vmem_limit_bytes=16 * 2**20),
        name="fit",
    )(place, total, jnp.asarray(pick_first), jnp.asarray(pick_second), jnp.asarray(linear))
    return derivative, reduced, operator, fitted


def solution(mesh):
    in_specs = (
        P("member", None, None, "passage"),
        P(None, None, None, "passage"),
        P("member"),
        P(("member", "passage")),
        P(),
        P(None, "passage"),
        P(),
        P(),
        P(None, "passage"),
        P(None, "passage"),
        P(),
        P(),
    )
    out_specs = (
        P("member", None, None, "passage"),
        P(("member", "passage"), None),
        P("member", None),
        P(("member", "passage"), None),
    )
    return jax.shard_map(body, mesh=mesh, in_specs=in_specs, out_specs=out_specs, check_vma=False)
```

```python
import functools
import math

import jax
import jax.numpy as jnp
import numpy as np
from jax import lax
from jax.experimental import pallas as pl
from jax.experimental.pallas import tpu as pltpu
from jax.sharding import PartitionSpec as P

F32 = jnp.float32
BF16 = jnp.bfloat16
NRING = 5
NV = 5
NX = 16
LANES = 128
PERIOD = 37
TIME_STEP = 0.2
RIDGE_FACTOR = 1.0
UNROLL = 4
CHUNK = 32
BLOB = 16
COORD = 16
EDGE = 48
ROWS = BLOB + COORD + 2 * EDGE
RIGHT = slice(BLOB + COORD, BLOB + COORD + EDGE)
LEFT = slice(BLOB + COORD + EDGE, ROWS)

HIGH = lax.Precision.HIGHEST
NT = (((1,), (1,)), ((), ()))
VMEM = pl.BlockSpec(memory_space=pltpu.VMEM)
HBM = pl.BlockSpec(memory_space=pltpu.HBM)
SMEM = pl.BlockSpec(memory_space=pltpu.SMEM)


def iota(shape, axis):
    return lax.broadcasted_iota(jnp.int32, shape, axis)


def roll(value, shift, axis):
    size = value.shape[axis]
    return pltpu.roll(value, shift % size if isinstance(shift, int) else shift, axis)


def split(value):
    high = value.astype(BF16).astype(F32)
    return high, (value - high).astype(BF16).astype(F32)


def north_south(u):
    row = iota(u.shape, 0)
    north = jnp.where(row == NX - 1, 0.0, roll(u, -1, 0))
    south = jnp.where(row == 0, 0.0, roll(u, 1, 0))
    return north + south


def cycle_masks(ids):
    return jnp.concatenate([jnp.where(ids == g, 1.0, 0.0) for g in range(NRING)], axis=0)


def lane_part():
    return iota((8, LANES), 1) % 4


def flat(ref, first, count):
    parts = [ref[pl.ds(first, count), v].reshape(count * NX, LANES) for v in range(NV)]
    return jnp.concatenate(parts, axis=1)


def project(rows, modes_flat):
    width = modes_flat.shape[0]
    size = rows.shape[0]
    pairs = lax.dot_general(rows, modes_flat, NT, preferred_element_type=F32)
    diagonal = iota((size, width), 0) % NX == iota((size, width), 1) % NX
    pairs = jnp.where(diagonal, pairs, 0.0)
    pairs = jnp.sum(pairs.reshape(size // NX, NX, width), axis=1)
    high, low = split(pairs)
    modes = width // NX
    mode_of = iota((width, LANES), 0) // NX
    column = iota((width, LANES), 1)
    total = jnp.zeros((8, LANES), F32)
    for j in range(CHUNK // 8):
        pick = jnp.where(mode_of + j * modes == column, 1.0, 0.0).astype(BF16)
        both = jnp.concatenate([high[8 * j : 8 * j + 8], low[8 * j : 8 * j + 8]], axis=0)
        both = jnp.dot(both.astype(BF16), pick, preferred_element_type=F32)
        total += both[:8] + both[8:]
    return total


def unpack(ref, modes):
    rows = []
    for chunk in range(ref.shape[0]):
        tile = ref[chunk]
        rows += [tile[:, j * modes : (j + 1) * modes] for j in range(CHUNK // 8)]
    return jnp.concatenate(rows, axis=0)


def before_kernel(*refs):
    count = 11
    sources, out, targets = refs[:count], refs[count], refs[count + 1 : 2 * count + 1]
    fields, sems = refs[2 * count + 1 :]
    copies = [
        pltpu.make_async_copy(source, target, sems.at[i])
        for i, (source, target) in enumerate(zip(sources, targets))
    ]
    for copy in copies:
        copy.start()
    times, pert_ids, visc, coup, table, pert, ids_ref, speed_ref, force_ref, states, basis = targets
    for copy in copies[:-2]:
        copy.wait()
    chunks = out.shape[0]
    speed = speed_ref[...]
    force = force_ref[...]
    damping = pert[pert_ids[0]]
    ids = ids_ref[...]
    visc_p = visc[NV - 1]
    lane = iota((NX, LANES), 1)
    half_speed = 0.5 * speed
    coef_east = jnp.where(lane == LANES - 1, 0.0, visc_p - half_speed)
    coef_west = jnp.where(lane == 0, 0.0, visc_p + half_speed)
    coef_own = coup[NV - 1, NV - 1] - 4.0 * visc_p - damping
    masks = cycle_masks(ids)
    masks_half = masks.astype(BF16)
    c8 = lane_part()
    row8 = iota((8, LANES), 0)
    quad = iota((NX, LANES), 1) // 4
    scale = 1.0 / math.sqrt(NX * LANES)

    def pieces(column):
        out16 = jnp.zeros((NX, LANES), F32)
        spot = 0
        for field in (speed, force, damping, ids.astype(F32)):
            for piece in split(field):
                moved = roll(piece, spot - column, 1)
                out16 = jnp.where(lane == spot, moved, out16)
                spot += 1
        return jnp.where(iota((8, LANES), 1) < 64, out16[:8], roll(out16[8:], 64, 1))

    params_right = pieces(LANES - 1)
    params_left = pieces(0)

    east_hi, east_lo = split(jnp.where(lane == LANES - 1, visc_p - half_speed, 0.0))
    west_hi, west_lo = split(jnp.where(lane == 0, visc_p + half_speed, 0.0))
    ids_f = ids.astype(F32)
    id_east = jnp.where(lane == LANES - 1, ids_f, 0.0)
    id_west = jnp.where(lane == 0, ids_f, 0.0)
    ones = jnp.ones((NX, LANES), BF16)
    filler = jnp.zeros((LANES - 32, LANES), F32)

    def as_rows(east, west):
        stacked = jnp.concatenate([east, west, filler], axis=0).astype(BF16)
        return lax.dot_general(ones, stacked, NT, preferred_element_type=F32)[:8]

    row_hi = as_rows(east_hi, west_hi)
    row_lo = as_rows(east_lo, west_lo)
    row_id = as_rows(id_east, id_west)
    counts = lax.dot_general(ones, masks_half, NT, preferred_element_type=F32)[:8]
    spread = jnp.where(
        iota((NRING * NX, LANES), 1) == 32 + iota((NRING * NX, LANES), 0) // NX, 1.0, 0.0
    )
    counts = jnp.dot(counts, spread, precision=HIGH, preferred_element_type=F32)
    count_hi, count_lo = split(counts)
    row_hi = row_hi + count_hi
    row_lo = row_lo + count_lo

    size = CHUNK * NX
    same_x = iota((NRING * NX, 3 * size), 0) % NX == iota((NRING * NX, 3 * size), 1) % NX
    snap_of_row = iota((size, LANES), 0) // NX == iota((size, LANES), 1) // 4
    part_of_lane = iota((size, LANES), 1) % 4
    to_start = jnp.where(snap_of_row & (part_of_lane < 2), scale, 0.0)
    to_rate = jnp.where(snap_of_row & (part_of_lane >= 2), scale, 0.0)
    copies[-2].wait()
    copies[-1].wait()
    flat_basis = flat(basis, 0, basis.shape[0])

    def chunk_step(chunk, carry):
        first = chunk * CHUNK

        def snap(k, edges):
            u = [states[first + k, v].astype(F32) for v in range(NV)]
            p = u[NV - 1]
            cosine = table[lax.rem(times[first + k], PERIOD)]
            rate = coef_east * roll(p, -1, 1) + coef_west * roll(p, 1, 1)
            rate = rate + visc_p * north_south(p) + coef_own * p + cosine * force
            for v in range(NV - 1):
                rate = rate + coup[NV - 1, v] * u[v]
            high, low = split(rate)
            at = pl.multiple_of(k * NX, NX)
            fields[pl.ds(at, NX), :] = p.astype(BF16)
            fields[pl.ds(pl.multiple_of(size + at, NX), NX), :] = high.astype(BF16)
            fields[pl.ds(pl.multiple_of(2 * size + at, NX), NX), :] = low.astype(BF16)
            return tuple(
                jnp.where(quad == k, roll(u[v], 4 * k + 2, 1), edges[v]) for v in range(NV)
            )

        edges = tuple(jnp.zeros((NX, LANES), F32) for _ in range(NV))
        if chunks == 1:
            for k in range(CHUNK):
                edges = snap(k, edges)
        else:
            edges = lax.fori_loop(0, CHUNK, snap, edges)
        sums = lax.dot_general(masks_half, fields[...], NT, preferred_element_type=F32)
        sums = jnp.where(same_x, sums, 0.0)
        by_cycle = jnp.sum(sums.reshape(NRING, NX, 3 * size), axis=1)
        by_cycle = jnp.concatenate([by_cycle, jnp.zeros((3, 3 * size), F32)], axis=0)
        start = by_cycle[:, :size]
        rate = by_cycle[:, size : 2 * size] + by_cycle[:, 2 * size :]
        packed = jnp.dot(start, to_start, precision=HIGH, preferred_element_type=F32)
        packed += jnp.dot(rate, to_rate, precision=HIGH, preferred_element_type=F32)
        high, low = split(packed)
        packed = jnp.where(c8 % 2 == 0, high, low)
        packed = jnp.where(row8 < NRING, packed, 0.0)
        for at, row in ((5, row_hi), (6, row_lo), (7, row_id)):
            packed = jnp.where(row8 == at, row, packed)
        p_low, p_high = edges[NV - 1][:8], edges[NV - 1][8:]
        p_edges = jnp.where(
            (c8 == 1) | (c8 == 2), p_low, jnp.where(c8 == 3, roll(p_high, 1, 1), roll(p_high, -1, 1))
        )
        right = [jnp.where(c8 < 2, t[:8], roll(t[8:], 2, 1)) for t in edges]
        left = [jnp.where(c8 >= 2, t[:8], roll(t[8:], -2, 1)) for t in edges]
        coords = split(project(flat(states, first, CHUNK), flat_basis))
        rows = [packed, p_edges, *coords, *right, params_right, *left, params_left]
        out[chunk] = jnp.concatenate(rows, axis=0).astype(BF16)
        return carry

    if chunks == 1:
        chunk_step(0, 0)
    else:
        lax.fori_loop(0, chunks, chunk_step, 0)


def after_kernel(
    times,
    pert_ids,
    place,
    kern,
    gain,
    visc,
    coup,
    table,
    states,
    basis_hbm,
    pert,
    ids_ref,
    speed_ref,
    force_ref,
    own_ref,
    near_ref,
    far_ref,
    last_ref,
    deriv,
    partial,
    coords,
    mixed,
    raw,
    cyc0,
    grooves,
    halo0,
    halo1,
    east_coef,
    west_coef,
    basis,
    sem,
):
    fetch = pltpu.make_async_copy(basis_hbm, basis, sem)
    fetch.start()
    chunks = own_ref.shape[0]
    passages = kern.shape[0]
    me = place[0]
    base = me - lax.rem(me, 2)
    odd = me % 2 == 1
    speed = speed_ref[...]
    force = force_ref[...]
    damping = pert[pert_ids[0]]
    ids = ids_ref[...]
    half_speed = 0.5 * speed
    lane = iota((NX, LANES), 1)
    c16 = lane % 4
    masks = cycle_masks(ids).astype(BF16)
    masks_twice = jnp.concatenate([masks, masks], axis=0)
    scale = 1.0 / math.sqrt(NX * LANES)
    size = CHUNK * NX

    src = iota((LANES, LANES), 0)
    dst = iota((LANES, LANES), 1) // 4 * 4
    mixers = [(src == dst) | (src == dst + 1), (src == dst + 2) | (src == dst + 3)]
    mixers += [src == dst + 2, src == dst + 1, src == dst + 3, src == dst]
    mix = jnp.concatenate([jnp.where(m, 1.0, 0.0).astype(BF16) for m in mixers], axis=1)
    pick_snap = jnp.where(iota((size, LANES), 1) == iota((size, LANES), 0) // NX * 4, 1.0, 0.0)
    pick_snap = pick_snap.astype(BF16)
    wide = 4 * NRING * NX
    same_x = iota((size, wide), 0) % NX == iota((size, wide), 1) % NX

    for v in range(NV):
        east_coef[v] = visc[v] - half_speed
        west_coef[v] = visc[v] + half_speed
    deep = NV * NX
    col = iota((NX, 3 * deep), 1)
    col_var, col_x = col % deep // NX, col % NX
    row_x = iota((NX, 3 * deep), 0)
    beside = jnp.abs(row_x - col_x) == 1
    blocks = []
    for v in range(NV):
        weight = jnp.zeros((NX, 3 * deep), F32)
        for other in range(NV):
            value = coup[v, other] - (4.0 * visc[v] if other == v else 0.0)
            weight = jnp.where((col_var == other) & (row_x == col_x), value, weight)
        blocks.append(jnp.where((col_var == v) & beside, visc[v], weight))
    high, low = split(jnp.concatenate(blocks, axis=0))
    col = iota((deep, 3 * deep), 1)
    mixer = jnp.where((col < deep) | (col >= 2 * deep), high, low).astype(BF16)

    def flat_basis():
        if chunks == 1:
            fetch.wait()
        return flat(basis, 0, basis.shape[0])

    def unpack_right(t):
        return jnp.concatenate([t, roll(t, -2, 1)], axis=0)

    def unpack_left(t):
        return jnp.concatenate([t, roll(t, 2, 1)], axis=0)

    def chunk_step(chunk, carry):
        first = chunk * CHUNK
        final = last_ref[chunk].astype(F32)
        raw[...] = final[: passages * BLOB]
        mixed[...] = jnp.dot(
            final[: passages * BLOB].astype(BF16), mix, preferred_element_type=F32
        )
        summed = final[passages * BLOB : passages * BLOB + COORD]
        coords[chunk] = summed[:8] + summed[8:]

        def slot(offset):
            other = lax.rem(me + offset + passages, passages)
            return pl.multiple_of(jnp.bitwise_xor(base, other) * BLOB, BLOB)

        def load(offset, carry):
            cyc0[pl.ds(pl.multiple_of(offset * 8, 8), 8), :] = mixed[pl.ds(slot(offset), 8), :LANES]
            return carry

        lax.fori_loop(0, passages, load, 0, unroll=passages <= 16)

        def plenum0(offset):
            total = jnp.zeros((8, LANES), F32)
            if passages <= 16 and isinstance(offset, int):
                for other in range(passages):
                    total += kern[(offset - other) % passages] * cyc0[other * 8 : other * 8 + 8, :]
                return total

            def add(other, total):
                weight = kern[lax.rem(offset - other + 2 * passages, passages)]
                return total + weight * cyc0[pl.ds(pl.multiple_of(other * 8, 8), 8), :]

            return lax.fori_loop(0, passages, add, total)

        row8 = iota((8, LANES), 0)
        lane8 = iota((8, LANES), 1)

        def second(offset, total):
            own = slot(offset)
            east, west = slot(offset + 1), slot(offset - 1)
            coefs = raw[pl.ds(own, 8), :]
            id_row = coefs[7:8, :].astype(jnp.int32)
            hit = (id_row == row8) & (lane8 < 32)
            left = jnp.concatenate(
                [jnp.where(hit, coefs[5:6, :], 0.0), jnp.where(hit, coefs[6:7, :], 0.0)], axis=0
            )
            right = jnp.concatenate(
                [
                    mixed[pl.ds(pl.multiple_of(east + 8, 8), 8), 2 * LANES : 3 * LANES],
                    mixed[pl.ds(pl.multiple_of(east + 8, 8), 8), 4 * LANES : 5 * LANES],
                    mixed[pl.ds(pl.multiple_of(west + 8, 8), 8), 3 * LANES : 4 * LANES],
                    mixed[pl.ds(pl.multiple_of(west + 8, 8), 8), 5 * LANES :],
                    jnp.zeros((LANES - 32, LANES), F32),
                ],
                axis=0,
            )
            edge = jnp.dot(left.astype(BF16), right.astype(BF16), preferred_element_type=F32)
            edge = (edge[:8] + edge[8:]) * scale
            count = jnp.where(lane8 == 32 + row8, coefs[5:6, :] + coefs[6:7, :], 0.0)
            count = jnp.sum(count, axis=1, keepdims=True) * (scale * gain[NV - 1])
            rate = mixed[pl.ds(own, 8), LANES : 2 * LANES] + edge + count * plenum0(offset)
            if isinstance(offset, int):
                start = cyc0[offset * 8 : offset * 8 + 8, :]
                weight = kern[-offset % passages]
            else:
                start = cyc0[pl.ds(pl.multiple_of(offset * 8, 8), 8), :]
                weight = kern[lax.rem(passages - offset, passages)]
            return total + weight * (start + TIME_STEP * rate)

        total = jnp.zeros((8, LANES), F32)
        if passages <= 16:
            for offset in range(passages):
                total = second(offset, total)
        else:
            total = lax.fori_loop(0, passages, second, total)
        own0, own1 = plenum0(0), total
        west0, east0 = plenum0(passages - 1), plenum0(1)

        stack = []
        for tile in (own0, own1):
            for piece in split(tile):
                stack += [jnp.broadcast_to(piece[g : g + 1], (NX, LANES)) for g in range(NRING)]
        stack = jnp.concatenate(stack, axis=0).astype(BF16)
        picked = lax.dot_general(pick_snap, stack, NT, preferred_element_type=F32)
        picked = jnp.where(same_x, picked, 0.0).astype(BF16)
        for stage in range(2):
            grooves[stage] = jnp.dot(
                picked[:, stage * wide // 2 : (stage + 1) * wide // 2],
                masks_twice,
                preferred_element_type=F32,
            )

        near = near_ref[chunk].astype(F32)
        own = own_ref[chunk].astype(F32)
        far = far_ref[chunk].astype(F32)
        west = jnp.where(odd, near[RIGHT], far)
        east = jnp.where(odd, far, near[LEFT])

        def param(side, index):
            t = side[40:48]
            low = t[:, index : index + 1] + t[:, index + 1 : index + 2]
            high = t[:, 64 + index : 65 + index] + t[:, 65 + index : 66 + index]
            return jnp.broadcast_to(jnp.concatenate([low, high], axis=0), (NX, LANES))

        speed_h, force_h, damp_h, ids_h = (
            jnp.where(c16 < 2, param(west, 2 * i), param(east, 2 * i)) for i in range(4)
        )
        groove_h = jnp.zeros((NX, LANES), F32)
        for g in range(NRING):
            value = jnp.where(c16 < 2, west0[g : g + 1], east0[g : g + 1])
            groove_h = jnp.where(ids_h == g, value, groove_h)
        cos_h = jnp.zeros((NX, LANES), F32)
        for k in range(CHUNK):
            cos_h = jnp.where(lane // 4 == k, table[lax.rem(times[first + k], PERIOD)], cos_h)
        halo = []
        ours = []
        for v in range(NV):
            at = slice(8 * v, 8 * v + 8)
            halo.append(jnp.where(c16 < 2, unpack_right(west[at]), unpack_left(east[at])))
            ours.append(
                jnp.where(c16 < 2, unpack_right(own[RIGHT][at]), unpack_left(own[LEFT][at]))
            )
        for v in range(NV):
            h = halo[v]
            e = roll(jnp.where(c16 == 3, h, ours[v]), -1, 1)
            w = roll(jnp.where(c16 == 0, h, ours[v]), 1, 1)
            rate = visc[v] * (e + w + north_south(h) - 4.0 * h) - 0.5 * speed_h * (e - w)
            rate = rate - damp_h * h + gain[v] * groove_h + force_h * cos_h
            for other in range(NV):
                rate = rate + coup[v, other] * halo[other]
            halo0[v] = h
            halo1[v] = h + TIME_STEP * rate

        def flux(u, mixed_u, halos, source, spread):
            result = []
            for v in range(NV):
                h = roll(halos[v], spread, 1)
                e = roll(jnp.where(lane == 0, h, u[v]), -1, 1)
                w = roll(jnp.where(lane == LANES - 1, h, u[v]), 1, 1)
                rate = mixed_u[NX * v : NX * v + NX] + east_coef[v] * e + west_coef[v] * w
                result.append(rate - damping * u[v] + gain[v] * source[0] + source[1])
            return result

        def snap(k):
            half = states[first + k].reshape(NV * NX, LANES)
            u = [states[first + k, v].astype(F32) for v in range(NV)]
            drive = table[lax.rem(times[first + k], PERIOD)] * force
            at = pl.multiple_of(k * NX, NX)
            spread = 2 * LANES - 4 * k - 2
            mixed0 = jnp.dot(
                mixer[:, : 2 * NV * NX],
                jnp.concatenate([half, half], axis=0),
                preferred_element_type=F32,
            )
            rate0 = flux(u, mixed0, halo0, (grooves[0, pl.ds(at, NX), :], drive), spread)
            middle = [u[v] + TIME_STEP * rate0[v] for v in range(NV)]
            stack = jnp.concatenate(middle, axis=0)
            high = stack.astype(BF16)
            low = (stack - high.astype(F32)).astype(BF16)
            mixed1 = jnp.dot(
                mixer, jnp.concatenate([high, high, low], axis=0), preferred_element_type=F32
            )
            rate1 = flux(middle, mixed1, halo1, (grooves[1, pl.ds(at, NX), :], drive), spread)
            for v in range(NV):
                deriv[first + k, v] = (0.5 * (rate0[v] + rate1[v])).astype(BF16)

        def snaps(step, carry):
            for i in range(UNROLL):
                snap(step * UNROLL + i)
            return carry

        lax.fori_loop(0, CHUNK // UNROLL, snaps, 0)
        partial[chunk] = project(flat(deriv, first, CHUNK), flat_basis())
        return carry

    if chunks == 1:
        chunk_step(0, 0)
    else:
        fetch.wait()
        lax.fori_loop(0, chunks, chunk_step, 0)


def eliminate(system, columns):
    row = iota(system.shape, 0)
    for j in columns:
        pivot = system[j : j + 1, :] / system[j : j + 1, j : j + 1]
        factor = jnp.where(row == j, 0.0, jnp.broadcast_to(system[:, j : j + 1], system.shape))
        system = jnp.where(row == j, pivot, system - factor * pivot)
    return system


highest = functools.partial(lax.dot_general, precision=HIGH, preferred_element_type=F32)
NN = (((1,), (0,)), ((), ()))


def system_kernel(ridge, modes, coords_ref, kernel_ref, system_ref):
    coords = unpack(coords_ref, modes)
    snaps = coords.shape[0]
    gram = highest(coords, coords, NT)
    squares = coords * coords
    kernel = gram + 0.5 * (gram * gram + highest(squares, squares, NT))
    kernel_ref[...] = kernel
    same = iota((snaps, snaps), 0) == iota((snaps, snaps), 1)
    eye = jnp.where(same, 1.0, 0.0)
    system = jnp.concatenate([kernel + ridge * eye, eye], axis=1)
    system_ref[...] = eliminate(system, range(snaps * 3 // 8))


def invert_kernel(modes, system_ref, inverse_ref):
    snaps = system_ref.shape[0]
    system = eliminate(system_ref[...], range(snaps * 3 // 8, snaps))
    inverse_ref[...] = system[:, snaps:]


def weight_kernel(
    coords_ref, kernel_ref, inverse_ref, first_ref, second_ref, lin_ref, weights, fit
):
    coords = unpack(coords_ref, first_ref.shape[0])
    design = highest(coords, first_ref[...], NN)
    design = design * (highest(coords, second_ref[...], NN) + lin_ref[...])
    weights[...] = highest(inverse_ref[...], design, NN)
    fit[...] = highest(kernel_ref[...], inverse_ref[...], NN)


def fit_kernel(
    place, rates_ref, coords_ref, weights, fit, reduced, operator, fitted, full, red
):
    modes = operator.shape[0]
    rates = unpack(rates_ref, modes)
    operator[...] = highest(rates, weights[...], (((0,), (0,)), ((), ())))
    full[...] = highest(fit[...], rates, NN)
    red[...] = jnp.concatenate([unpack(coords_ref, modes), rates], axis=1)
    each = fitted.shape[0]
    for i in range(each):
        at = pl.ds(place[0] * each + i, 1)
        fitted[i : i + 1, :] = full[at, :]
        reduced[i : i + 1, :] = red[at, :]


def body(
    states,
    basis,
    snapshot_times,
    pert_ids,
    pert_table,
    cycle_ids,
    groove_kernel,
    groove_gain,
    speed,
    force_amp,
    viscosity,
    coupling,
):
    snaps = states.shape[0]
    modes = basis.shape[0]
    chunks = snaps // CHUNK
    passages = lax.axis_size("passage")
    rounds = passages.bit_length() - 1
    position = lax.axis_index("passage")
    place = position.reshape(1).astype(jnp.int32)
    angles = 2.0 * math.pi * np.arange(PERIOD) / PERIOD
    table = jnp.asarray(np.cos(angles).astype(np.float32))

    def swap(value, mask):
        pairs = [(i, i ^ mask) for i in range(passages)]
        return lax.ppermute(value, "passage", pairs)

    def swap_chip(value, mask):
        return swap(value, mask + 1)

    def add_pieces(one, two):
        total = one[:, :8].astype(F32) + one[:, 8:].astype(F32)
        total += two[:, :8].astype(F32) + two[:, 8:].astype(F32)
        high = lax.reduce_precision(total, 8, 7)
        return jnp.concatenate([high, total - high], axis=1).astype(BF16)

    operands = (
        snapshot_times,
        pert_ids,
        viscosity,
        coupling,
        table,
        pert_table,
        cycle_ids,
        speed,
        force_amp,
        states,
        basis,
    )
    first = pl.pallas_call(
        before_kernel,
        out_shape=jax.ShapeDtypeStruct((chunks, ROWS, LANES), BF16),
        in_specs=[HBM] * len(operands),
        out_specs=VMEM,
        scratch_shapes=[pltpu.SMEM(x.shape, x.dtype) for x in operands[:5]]
        + [pltpu.VMEM(x.shape, x.dtype) for x in operands[5:]]
        + [
            pltpu.VMEM((3 * CHUNK * NX, LANES), BF16),
            pltpu.SemaphoreType.DMA((len(operands),)),
        ],
        compiler_params=pltpu.CompilerParams(vmem_limit_bytes=60 * 2**20),
        name="before",
    )(*operands)
    near = swap(first, 1)
    odd = position % 2 == 1
    low, high = jnp.where(odd, near, first), jnp.where(odd, first, near)
    group = jnp.concatenate([low[:, :BLOB], high[:, :BLOB]], axis=1)
    coords = add_pieces(first[:, BLOB : BLOB + COORD], near[:, BLOB : BLOB + COORD])
    right, left = high[:, RIGHT], low[:, LEFT]
    far_right, far_left = [], []
    for r in range(1, rounds):
        got = swap_chip(jnp.concatenate([group, coords, right, left], axis=1), 1 << r)
        rows = group.shape[1]
        group = jnp.concatenate([group, got[:, :rows]], axis=1)
        coords = add_pieces(coords, got[:, rows : rows + COORD])
        right, left = got[:, rows + COORD : rows + COORD + EDGE], got[:, rows + COORD + EDGE :]
        far_right.append(right)
        far_left.append(left)
    for r in range(rounds - 2, 0, -1):
        bit = (position >> r) & 1
        right = jnp.where(bit == 1, far_right[r - 1], right)
        left = jnp.where(bit == 0, far_left[r - 1], left)
    far = jnp.where(odd, left, right)
    last = jnp.concatenate([group, coords], axis=1)

    tile = jax.ShapeDtypeStruct((chunks, 8, LANES), F32)
    derivative, partial, coords = pl.pallas_call(
        after_kernel,
        out_shape=(jax.ShapeDtypeStruct(states.shape, BF16), tile, tile),
        in_specs=[SMEM] * 8 + [VMEM, HBM] + [VMEM] * 8,
        out_specs=(VMEM, VMEM, VMEM),
        scratch_shapes=[
            pltpu.VMEM((passages * BLOB, 6 * LANES), F32),
            pltpu.VMEM((passages * BLOB, LANES), F32),
            pltpu.VMEM((passages * 8, LANES), F32),
            pltpu.VMEM((2, CHUNK * NX, LANES), F32),
            pltpu.VMEM((NV, NX, LANES), F32),
            pltpu.VMEM((NV, NX, LANES), F32),
            pltpu.VMEM((NV, NX, LANES), F32),
            pltpu.VMEM((NV, NX, LANES), F32),
            pltpu.VMEM(basis.shape, BF16),
            pltpu.SemaphoreType.DMA,
        ],
        compiler_params=pltpu.CompilerParams(vmem_limit_bytes=32 * 2**20),
        name="after",
    )(
        snapshot_times,
        pert_ids,
        place,
        groove_kernel,
        groove_gain,
        viscosity,
        coupling,
        table,
        states,
        basis,
        pert_table,
        cycle_ids,
        speed,
        force_amp,
        first,
        near,
        far,
        last,
    )

    upper_first, upper_second = np.triu_indices(modes)
    features = modes + len(upper_first)
    pick_first = np.zeros((modes, features), np.float32)
    pick_second = np.zeros((modes, features), np.float32)
    linear = np.zeros((1, features), np.float32)
    pick_first[np.arange(modes), np.arange(modes)] = 1.0
    linear[0, :modes] = 1.0
    pick_first[upper_first, modes + np.arange(len(upper_first))] = 1.0
    pick_second[upper_second, modes + np.arange(len(upper_first))] = 1.0

    def small(kernel, name, outs, *args):
        return pl.pallas_call(
            kernel,
            out_shape=tuple(jax.ShapeDtypeStruct(shape, F32) for shape in outs),
            in_specs=[VMEM] * len(args),
            out_specs=tuple(VMEM for _ in outs),
            cost_estimate=pl.CostEstimate(flops=10**8, bytes_accessed=2**20, transcendentals=0),
            compiler_params=pltpu.CompilerParams(vmem_limit_bytes=16 * 2**20),
            name=name,
        )(*args)

    total = partial + swap(partial, 1)
    kernel, system = small(
        functools.partial(system_kernel, RIDGE_FACTOR * snaps, modes),
        "system",
        [(snaps, snaps), (snaps, 2 * snaps)],
        coords,
    )
    for r in range(1, rounds):
        got = swap_chip(total, 1 << r)
        if r == 1:
            total, kernel, system = lax.optimization_barrier((total + got, kernel, system))
            (inverse,) = small(
                functools.partial(invert_kernel, modes), "invert", [(snaps, snaps)], system
            )
        elif r == 2:
            total, inverse = lax.optimization_barrier((total + got, inverse))
            weights, fit = small(
                weight_kernel,
                "weights",
                [(snaps, features), (snaps, snaps)],
                coords,
                kernel,
                inverse,
                jnp.asarray(pick_first),
                jnp.asarray(pick_second),
                jnp.asarray(linear),
            )
        else:
            total = total + got
    each = snaps // passages
    reduced, operator, fitted = pl.pallas_call(
        fit_kernel,
        out_shape=(
            jax.ShapeDtypeStruct((each, 2 * modes), F32),
            jax.ShapeDtypeStruct((modes, features), F32),
            jax.ShapeDtypeStruct((each, modes), F32),
        ),
        in_specs=[SMEM] + [VMEM] * 4,
        out_specs=(VMEM, VMEM, VMEM),
        scratch_shapes=[pltpu.VMEM((snaps, modes), F32), pltpu.VMEM((snaps, 2 * modes), F32)],
        compiler_params=pltpu.CompilerParams(vmem_limit_bytes=16 * 2**20),
        name="fit",
    )(place, total, coords, weights, fit)
    return derivative, reduced, operator.T, fitted


def solution(mesh):
    in_specs = (
        P("member", None, None, "passage"),
        P(None, None, None, "passage"),
        P("member"),
        P(("member", "passage")),
        P(),
        P(None, "passage"),
        P(),
        P(),
        P(None, "passage"),
        P(None, "passage"),
        P(),
        P(),
    )
    out_specs = (
        P("member", None, None, "passage"),
        P(("member", "passage"), None),
        P("member", None),
        P(("member", "passage"), None),
    )
    return jax.shard_map(body, mesh=mesh, in_specs=in_specs, out_specs=out_specs, check_vma=False)
```

```python
import functools
import math

import jax
import jax.numpy as jnp
import numpy as np
from jax import lax
from jax.experimental import pallas as pl
from jax.experimental.pallas import tpu as pltpu
from jax.sharding import PartitionSpec as P

F32 = jnp.float32
BF16 = jnp.bfloat16
NRING = 5
NV = 5
NX = 16
LANES = 128
PERIOD = 37
TIME_STEP = 0.2
RIDGE_FACTOR = 1.0
UNROLL = 4
CHUNK = 32
BLOB = 16
COORD = 16
EDGE = 48
ROWS = BLOB + COORD + 2 * EDGE
RIGHT = slice(BLOB + COORD, BLOB + COORD + EDGE)
LEFT = slice(BLOB + COORD + EDGE, ROWS)

HIGH = lax.Precision.HIGHEST
NT = (((1,), (1,)), ((), ()))
VMEM = pl.BlockSpec(memory_space=pltpu.VMEM)
HBM = pl.BlockSpec(memory_space=pltpu.HBM)
SMEM = pl.BlockSpec(memory_space=pltpu.SMEM)


def iota(shape, axis):
    return lax.broadcasted_iota(jnp.int32, shape, axis)


def roll(value, shift, axis):
    size = value.shape[axis]
    return pltpu.roll(value, shift % size if isinstance(shift, int) else shift, axis)


def split(value):
    high = value.astype(BF16).astype(F32)
    return high, (value - high).astype(BF16).astype(F32)


def north_south(u):
    row = iota(u.shape, 0)
    north = jnp.where(row == NX - 1, 0.0, roll(u, -1, 0))
    south = jnp.where(row == 0, 0.0, roll(u, 1, 0))
    return north + south


def cycle_masks(ids):
    return jnp.concatenate([jnp.where(ids == g, 1.0, 0.0) for g in range(NRING)], axis=0)


def lane_part():
    return iota((8, LANES), 1) % 4


def flat(ref, first, count):
    parts = [ref[pl.ds(first, count), v].reshape(count * NX, LANES) for v in range(NV)]
    return jnp.concatenate(parts, axis=1)


def project(rows, modes_flat):
    width = modes_flat.shape[0]
    size = rows.shape[0]
    pairs = lax.dot_general(rows, modes_flat, NT, preferred_element_type=F32)
    diagonal = iota((size, width), 0) % NX == iota((size, width), 1) % NX
    pairs = jnp.where(diagonal, pairs, 0.0)
    pairs = jnp.sum(pairs.reshape(size // NX, NX, width), axis=1)
    high, low = split(pairs)
    modes = width // NX
    mode_of = iota((width, LANES), 0) // NX
    column = iota((width, LANES), 1)
    total = jnp.zeros((8, LANES), F32)
    for j in range(CHUNK // 8):
        pick = jnp.where(mode_of + j * modes == column, 1.0, 0.0).astype(BF16)
        both = jnp.concatenate([high[8 * j : 8 * j + 8], low[8 * j : 8 * j + 8]], axis=0)
        both = jnp.dot(both.astype(BF16), pick, preferred_element_type=F32)
        total += both[:8] + both[8:]
    return total


def unpack(ref, modes):
    rows = []
    for chunk in range(ref.shape[0]):
        tile = ref[chunk]
        rows += [tile[:, j * modes : (j + 1) * modes] for j in range(CHUNK // 8)]
    return jnp.concatenate(rows, axis=0)


def before_kernel(*refs):
    count = 11
    sources, out, targets = refs[:count], refs[count], refs[count + 1 : 2 * count + 1]
    fields, sems = refs[2 * count + 1 :]
    copies = [
        pltpu.make_async_copy(source, target, sems.at[i])
        for i, (source, target) in enumerate(zip(sources, targets))
    ]
    for copy in copies:
        copy.start()
    times, pert_ids, visc, coup, table, pert, ids_ref, speed_ref, force_ref, states, basis = targets
    for copy in copies[:-2]:
        copy.wait()
    chunks = out.shape[0]
    speed = speed_ref[...]
    force = force_ref[...]
    damping = pert[pert_ids[0]]
    ids = ids_ref[...]
    visc_p = visc[NV - 1]
    lane = iota((NX, LANES), 1)
    half_speed = 0.5 * speed
    coef_east = jnp.where(lane == LANES - 1, 0.0, visc_p - half_speed)
    coef_west = jnp.where(lane == 0, 0.0, visc_p + half_speed)
    coef_own = coup[NV - 1, NV - 1] - 4.0 * visc_p - damping
    masks = cycle_masks(ids)
    masks_half = masks.astype(BF16)
    c8 = lane_part()
    row8 = iota((8, LANES), 0)
    quad = iota((NX, LANES), 1) // 4
    scale = 1.0 / math.sqrt(NX * LANES)

    def pieces(column):
        out16 = jnp.zeros((NX, LANES), F32)
        spot = 0
        for field in (speed, force, damping, ids.astype(F32)):
            for piece in split(field):
                moved = roll(piece, spot - column, 1)
                out16 = jnp.where(lane == spot, moved, out16)
                spot += 1
        return jnp.where(iota((8, LANES), 1) < 64, out16[:8], roll(out16[8:], 64, 1))

    params_right = pieces(LANES - 1)
    params_left = pieces(0)

    east_hi, east_lo = split(jnp.where(lane == LANES - 1, visc_p - half_speed, 0.0))
    west_hi, west_lo = split(jnp.where(lane == 0, visc_p + half_speed, 0.0))
    ids_f = ids.astype(F32)
    id_east = jnp.where(lane == LANES - 1, ids_f, 0.0)
    id_west = jnp.where(lane == 0, ids_f, 0.0)
    ones = jnp.ones((NX, LANES), BF16)
    filler = jnp.zeros((LANES - 32, LANES), F32)

    def as_rows(east, west):
        stacked = jnp.concatenate([east, west, filler], axis=0).astype(BF16)
        return lax.dot_general(ones, stacked, NT, preferred_element_type=F32)[:8]

    row_hi = as_rows(east_hi, west_hi)
    row_lo = as_rows(east_lo, west_lo)
    row_id = as_rows(id_east, id_west)
    counts = lax.dot_general(ones, masks_half, NT, preferred_element_type=F32)[:8]
    spread = jnp.where(
        iota((NRING * NX, LANES), 1) == 32 + iota((NRING * NX, LANES), 0) // NX, 1.0, 0.0
    )
    counts = jnp.dot(counts, spread, precision=HIGH, preferred_element_type=F32)
    count_hi, count_lo = split(counts)
    row_hi = row_hi + count_hi
    row_lo = row_lo + count_lo

    size = CHUNK * NX
    same_x = iota((NRING * NX, 3 * size), 0) % NX == iota((NRING * NX, 3 * size), 1) % NX
    snap_of_row = iota((size, LANES), 0) // NX == iota((size, LANES), 1) // 4
    part_of_lane = iota((size, LANES), 1) % 4
    to_start = jnp.where(snap_of_row & (part_of_lane < 2), scale, 0.0)
    to_rate = jnp.where(snap_of_row & (part_of_lane >= 2), scale, 0.0)
    copies[-2].wait()
    if chunks > 1:
        copies[-1].wait()

    def chunk_step(chunk, carry):
        first = chunk * CHUNK

        def snap(k, edges):
            u = [states[first + k, v].astype(F32) for v in range(NV)]
            p = u[NV - 1]
            cosine = table[lax.rem(times[first + k], PERIOD)]
            rate = coef_east * roll(p, -1, 1) + coef_west * roll(p, 1, 1)
            rate = rate + visc_p * north_south(p) + coef_own * p + cosine * force
            for v in range(NV - 1):
                rate = rate + coup[NV - 1, v] * u[v]
            high, low = split(rate)
            at = pl.multiple_of(k * NX, NX)
            fields[pl.ds(at, NX), :] = p.astype(BF16)
            fields[pl.ds(pl.multiple_of(size + at, NX), NX), :] = high.astype(BF16)
            fields[pl.ds(pl.multiple_of(2 * size + at, NX), NX), :] = low.astype(BF16)
            return tuple(
                jnp.where(quad == k, roll(u[v], 4 * k + 2, 1), edges[v]) for v in range(NV)
            )

        edges = tuple(jnp.zeros((NX, LANES), F32) for _ in range(NV))
        if chunks == 1:
            for k in range(CHUNK):
                edges = snap(k, edges)
        else:
            edges = lax.fori_loop(0, CHUNK, snap, edges)
        sums = lax.dot_general(masks_half, fields[...], NT, preferred_element_type=F32)
        sums = jnp.where(same_x, sums, 0.0)
        by_cycle = jnp.sum(sums.reshape(NRING, NX, 3 * size), axis=1)
        by_cycle = jnp.concatenate([by_cycle, jnp.zeros((3, 3 * size), F32)], axis=0)
        start = by_cycle[:, :size]
        rate = by_cycle[:, size : 2 * size] + by_cycle[:, 2 * size :]
        packed = jnp.dot(start, to_start, precision=HIGH, preferred_element_type=F32)
        packed += jnp.dot(rate, to_rate, precision=HIGH, preferred_element_type=F32)
        high, low = split(packed)
        packed = jnp.where(c8 % 2 == 0, high, low)
        packed = jnp.where(row8 < NRING, packed, 0.0)
        for at, row in ((5, row_hi), (6, row_lo), (7, row_id)):
            packed = jnp.where(row8 == at, row, packed)
        p_low, p_high = edges[NV - 1][:8], edges[NV - 1][8:]
        p_edges = jnp.where(
            (c8 == 1) | (c8 == 2), p_low, jnp.where(c8 == 3, roll(p_high, 1, 1), roll(p_high, -1, 1))
        )
        right = [jnp.where(c8 < 2, t[:8], roll(t[8:], 2, 1)) for t in edges]
        left = [jnp.where(c8 >= 2, t[:8], roll(t[8:], -2, 1)) for t in edges]
        if chunks == 1:
            copies[-1].wait()
        flat_basis = flat(basis, 0, basis.shape[0])
        coords = split(project(flat(states, first, CHUNK), flat_basis))
        rows = [packed, p_edges, *coords, *right, params_right, *left, params_left]
        out[chunk] = jnp.concatenate(rows, axis=0).astype(BF16)
        return carry

    if chunks == 1:
        chunk_step(0, 0)
    else:
        lax.fori_loop(0, chunks, chunk_step, 0)


def start_kernel(top, place, first, near, out, edges):
    odd = place[0] % 2 == 1
    for chunk in range(out.shape[0]):
        mine, other = first[chunk].astype(F32), near[chunk].astype(F32)
        low, high = jnp.where(odd, other, mine), jnp.where(odd, mine, other)
        total = mine[BLOB : BLOB + COORD] + other[BLOB : BLOB + COORD]
        right, left = high[RIGHT], low[LEFT]
        edges[chunk] = jnp.concatenate([right, left], axis=0).astype(BF16)
        payload = jnp.where(goes_right(place[0], top), right, left)
        rows = [payload, *split(total[:8] + total[8:]), low[:BLOB], high[:BLOB]]
        out[chunk] = jnp.concatenate(rows, axis=0).astype(BF16)


def goes_right(me, bit):
    if bit == 0:
        return me % 2 == 1
    lower = jnp.bitwise_and(jnp.right_shift(me, 1), (1 << bit) - 1)
    return lower == (1 << bit) - 1


def goes_left(me, bit):
    lower = jnp.bitwise_and(jnp.right_shift(me, 1), (1 << bit) - 1)
    return lower == 0


def next_kernel(bit, place, sent, got, edges, out, new_edges):
    me = place[0]
    for chunk in range(out.shape[0]):
        mine, other = sent[chunk].astype(F32), got[chunk].astype(F32)
        both = edges[chunk].astype(F32)
        right = jnp.where(goes_right(me, bit + 1), other[:EDGE], both[:EDGE])
        left = jnp.where(goes_left(me, bit + 1), other[:EDGE], both[EDGE:])
        new_edges[chunk] = jnp.concatenate([right, left], axis=0).astype(BF16)
        payload = jnp.where(goes_right(me, bit), right, left)
        total = mine[EDGE : EDGE + COORD] + other[EDGE : EDGE + COORD]
        rows = [payload, *split(total[:8] + total[8:]), mine[EDGE + COORD :], other[EDGE + COORD :]]
        out[chunk] = jnp.concatenate(rows, axis=0).astype(BF16)


def after_kernel(
    times,
    pert_ids,
    place,
    kern,
    gain,
    visc,
    coup,
    table,
    states_hbm,
    basis_hbm,
    pert,
    ids_ref,
    speed_ref,
    force_ref,
    own_ref,
    near_ref,
    sent_ref,
    last_ref,
    deriv,
    partial,
    coords,
    mixed,
    raw,
    cyc0,
    grooves,
    halo0,
    halo1,
    east_coef,
    west_coef,
    basis,
    states,
    sems,
):
    fetch_states = pltpu.make_async_copy(states_hbm, states, sems.at[0])
    fetch = pltpu.make_async_copy(basis_hbm, basis, sems.at[1])
    fetch_states.start()
    fetch.start()
    chunks = own_ref.shape[0]
    passages = kern.shape[0]
    me = place[0]
    base = me - lax.rem(me, 2)
    bits = passages.bit_length() - 2
    odd = me % 2 == 1
    speed = speed_ref[...]
    force = force_ref[...]
    damping = pert[pert_ids[0]]
    ids = ids_ref[...]
    half_speed = 0.5 * speed
    lane = iota((NX, LANES), 1)
    c16 = lane % 4
    masks = cycle_masks(ids).astype(BF16)
    masks_twice = jnp.concatenate([masks, masks], axis=0)
    scale = 1.0 / math.sqrt(NX * LANES)
    size = CHUNK * NX

    src = iota((LANES, LANES), 0)
    dst = iota((LANES, LANES), 1) // 4 * 4
    mixers = [(src == dst) | (src == dst + 1), (src == dst + 2) | (src == dst + 3)]
    mixers += [src == dst + 2, src == dst + 1, src == dst + 3, src == dst]
    mix = jnp.concatenate([jnp.where(m, 1.0, 0.0).astype(BF16) for m in mixers], axis=1)
    pick_snap = jnp.where(iota((size, LANES), 1) == iota((size, LANES), 0) // NX * 4, 1.0, 0.0)
    pick_snap = pick_snap.astype(BF16)
    wide = 4 * NRING * NX
    same_x = iota((size, wide), 0) % NX == iota((size, wide), 1) % NX

    for v in range(NV):
        east_coef[v] = visc[v] - half_speed
        west_coef[v] = visc[v] + half_speed
    deep = NV * NX
    col = iota((NX, 3 * deep), 1)
    col_var, col_x = col % deep // NX, col % NX
    row_x = iota((NX, 3 * deep), 0)
    beside = jnp.abs(row_x - col_x) == 1
    blocks = []
    for v in range(NV):
        weight = jnp.zeros((NX, 3 * deep), F32)
        for other in range(NV):
            value = coup[v, other] - (4.0 * visc[v] if other == v else 0.0)
            weight = jnp.where((col_var == other) & (row_x == col_x), value, weight)
        blocks.append(jnp.where((col_var == v) & beside, visc[v], weight))
    high, low = split(jnp.concatenate(blocks, axis=0))
    col = iota((deep, 3 * deep), 1)
    mixer = jnp.where((col < deep) | (col >= 2 * deep), high, low).astype(BF16)

    def flat_basis():
        if chunks == 1:
            fetch.wait()
        return flat(basis, 0, basis.shape[0])

    def unpack_right(t):
        return jnp.concatenate([t, roll(t, -2, 1)], axis=0)

    def unpack_left(t):
        return jnp.concatenate([t, roll(t, 2, 1)], axis=0)

    def chunk_step(chunk, carry):
        first = chunk * CHUNK
        head = EDGE + COORD
        half = passages // 2 * BLOB
        raw[:half, :] = sent_ref[chunk, head:, :].astype(F32)
        raw[half:, :] = last_ref[chunk, head:, :].astype(F32)
        summed = sent_ref[chunk, EDGE:head, :].astype(F32)
        summed += last_ref[chunk, EDGE:head, :].astype(F32)
        coords[chunk] = summed[:8] + summed[8:]
        mixed[...] = jnp.dot(raw[...].astype(BF16), mix, preferred_element_type=F32)

        def slot(offset):
            other = lax.rem(me + offset + passages, passages)
            flips = jnp.bitwise_xor(base, other)
            index = jnp.bitwise_and(flips, 1)
            for bit in range(bits):
                moved = jnp.bitwise_and(jnp.right_shift(flips, bit + 1), 1)
                index = index + jnp.left_shift(moved, bits - bit)
            return pl.multiple_of(index * BLOB, BLOB)

        def load(offset, carry):
            cyc0[pl.ds(pl.multiple_of(offset * 8, 8), 8), :] = mixed[pl.ds(slot(offset), 8), :LANES]
            return carry

        lax.fori_loop(0, passages, load, 0, unroll=passages <= 16)

        def plenum0(offset):
            total = jnp.zeros((8, LANES), F32)
            if passages <= 16 and isinstance(offset, int):
                for other in range(passages):
                    total += kern[(offset - other) % passages] * cyc0[other * 8 : other * 8 + 8, :]
                return total

            def add(other, total):
                weight = kern[lax.rem(offset - other + 2 * passages, passages)]
                return total + weight * cyc0[pl.ds(pl.multiple_of(other * 8, 8), 8), :]

            return lax.fori_loop(0, passages, add, total)

        row8 = iota((8, LANES), 0)
        lane8 = iota((8, LANES), 1)

        def second(offset, total):
            own = slot(offset)
            east, west = slot(offset + 1), slot(offset - 1)
            coefs = raw[pl.ds(own, 8), :]
            id_row = coefs[7:8, :].astype(jnp.int32)
            hit = (id_row == row8) & (lane8 < 32)
            left = jnp.concatenate(
                [jnp.where(hit, coefs[5:6, :], 0.0), jnp.where(hit, coefs[6:7, :], 0.0)], axis=0
            )
            right = jnp.concatenate(
                [
                    mixed[pl.ds(pl.multiple_of(east + 8, 8), 8), 2 * LANES : 3 * LANES],
                    mixed[pl.ds(pl.multiple_of(east + 8, 8), 8), 4 * LANES : 5 * LANES],
                    mixed[pl.ds(pl.multiple_of(west + 8, 8), 8), 3 * LANES : 4 * LANES],
                    mixed[pl.ds(pl.multiple_of(west + 8, 8), 8), 5 * LANES :],
                    jnp.zeros((LANES - 32, LANES), F32),
                ],
                axis=0,
            )
            edge = jnp.dot(left.astype(BF16), right.astype(BF16), preferred_element_type=F32)
            edge = (edge[:8] + edge[8:]) * scale
            count = jnp.where(lane8 == 32 + row8, coefs[5:6, :] + coefs[6:7, :], 0.0)
            count = jnp.sum(count, axis=1, keepdims=True) * (scale * gain[NV - 1])
            rate = mixed[pl.ds(own, 8), LANES : 2 * LANES] + edge + count * plenum0(offset)
            if isinstance(offset, int):
                start = cyc0[offset * 8 : offset * 8 + 8, :]
                weight = kern[-offset % passages]
            else:
                start = cyc0[pl.ds(pl.multiple_of(offset * 8, 8), 8), :]
                weight = kern[lax.rem(passages - offset, passages)]
            return total + weight * (start + TIME_STEP * rate)

        total = jnp.zeros((8, LANES), F32)
        if passages <= 16:
            for offset in range(passages):
                total = second(offset, total)
        else:
            total = lax.fori_loop(0, passages, second, total)
        own0, own1 = plenum0(0), total
        west0, east0 = plenum0(passages - 1), plenum0(1)

        stack = []
        for tile in (own0, own1):
            for piece in split(tile):
                stack += [jnp.broadcast_to(piece[g : g + 1], (NX, LANES)) for g in range(NRING)]
        stack = jnp.concatenate(stack, axis=0).astype(BF16)
        picked = lax.dot_general(pick_snap, stack, NT, preferred_element_type=F32)
        picked = jnp.where(same_x, picked, 0.0).astype(BF16)
        for stage in range(2):
            grooves[stage] = jnp.dot(
                picked[:, stage * wide // 2 : (stage + 1) * wide // 2],
                masks_twice,
                preferred_element_type=F32,
            )

        near = near_ref[chunk].astype(F32)
        own = own_ref[chunk].astype(F32)
        far = last_ref[chunk, :EDGE, :].astype(F32)
        west = jnp.where(odd, near[RIGHT], far)
        east = jnp.where(odd, far, near[LEFT])

        def param(side, index):
            t = side[40:48]
            low = t[:, index : index + 1] + t[:, index + 1 : index + 2]
            high = t[:, 64 + index : 65 + index] + t[:, 65 + index : 66 + index]
            return jnp.broadcast_to(jnp.concatenate([low, high], axis=0), (NX, LANES))

        speed_h, force_h, damp_h, ids_h = (
            jnp.where(c16 < 2, param(west, 2 * i), param(east, 2 * i)) for i in range(4)
        )
        groove_h = jnp.zeros((NX, LANES), F32)
        for g in range(NRING):
            value = jnp.where(c16 < 2, west0[g : g + 1], east0[g : g + 1])
            groove_h = jnp.where(ids_h == g, value, groove_h)
        cos_h = jnp.zeros((NX, LANES), F32)
        for k in range(CHUNK):
            cos_h = jnp.where(lane // 4 == k, table[lax.rem(times[first + k], PERIOD)], cos_h)
        halo = []
        ours = []
        for v in range(NV):
            at = slice(8 * v, 8 * v + 8)
            halo.append(jnp.where(c16 < 2, unpack_right(west[at]), unpack_left(east[at])))
            ours.append(
                jnp.where(c16 < 2, unpack_right(own[RIGHT][at]), unpack_left(own[LEFT][at]))
            )
        for v in range(NV):
            h = halo[v]
            e = roll(jnp.where(c16 == 3, h, ours[v]), -1, 1)
            w = roll(jnp.where(c16 == 0, h, ours[v]), 1, 1)
            rate = visc[v] * (e + w + north_south(h) - 4.0 * h) - 0.5 * speed_h * (e - w)
            rate = rate - damp_h * h + gain[v] * groove_h + force_h * cos_h
            for other in range(NV):
                rate = rate + coup[v, other] * halo[other]
            halo0[v] = h
            halo1[v] = h + TIME_STEP * rate

        def flux(u, mixed_u, halos, source, spread):
            result = []
            for v in range(NV):
                h = roll(halos[v], spread, 1)
                e = roll(jnp.where(lane == 0, h, u[v]), -1, 1)
                w = roll(jnp.where(lane == LANES - 1, h, u[v]), 1, 1)
                rate = mixed_u[NX * v : NX * v + NX] + east_coef[v] * e + west_coef[v] * w
                result.append(rate - damping * u[v] + gain[v] * source[0] + source[1])
            return result

        def snap(k):
            half = states[first + k].reshape(NV * NX, LANES)
            u = [states[first + k, v].astype(F32) for v in range(NV)]
            drive = table[lax.rem(times[first + k], PERIOD)] * force
            at = pl.multiple_of(k * NX, NX)
            spread = 2 * LANES - 4 * k - 2
            mixed0 = jnp.dot(
                mixer[:, : 2 * NV * NX],
                jnp.concatenate([half, half], axis=0),
                preferred_element_type=F32,
            )
            rate0 = flux(u, mixed0, halo0, (grooves[0, pl.ds(at, NX), :], drive), spread)
            middle = [u[v] + TIME_STEP * rate0[v] for v in range(NV)]
            stack = jnp.concatenate(middle, axis=0)
            high = stack.astype(BF16)
            low = (stack - high.astype(F32)).astype(BF16)
            mixed1 = jnp.dot(
                mixer, jnp.concatenate([high, high, low], axis=0), preferred_element_type=F32
            )
            rate1 = flux(middle, mixed1, halo1, (grooves[1, pl.ds(at, NX), :], drive), spread)
            for v in range(NV):
                deriv[first + k, v] = (0.5 * (rate0[v] + rate1[v])).astype(BF16)

        def snaps(step, carry):
            for i in range(UNROLL):
                snap(step * UNROLL + i)
            return carry

        if chunks == 1:
            fetch_states.wait()
        lax.fori_loop(0, CHUNK // UNROLL, snaps, 0)
        partial[chunk] = project(flat(deriv, first, CHUNK), flat_basis())
        return carry

    if chunks == 1:
        chunk_step(0, 0)
    else:
        fetch_states.wait()
        fetch.wait()
        lax.fori_loop(0, chunks, chunk_step, 0)


def eliminate(system, columns):
    row = iota(system.shape, 0)
    for j in columns:
        pivot = system[j : j + 1, :] / system[j : j + 1, j : j + 1]
        factor = jnp.where(row == j, 0.0, jnp.broadcast_to(system[:, j : j + 1], system.shape))
        system = jnp.where(row == j, pivot, system - factor * pivot)
    return system


highest = functools.partial(lax.dot_general, precision=HIGH, preferred_element_type=F32)
NN = (((1,), (0,)), ((), ()))


def system_kernel(ridge, modes, coords_ref, kernel_ref, system_ref):
    coords = unpack(coords_ref, modes)
    snaps = coords.shape[0]
    gram = highest(coords, coords, NT)
    squares = coords * coords
    kernel = gram + 0.5 * (gram * gram + highest(squares, squares, NT))
    kernel_ref[...] = kernel
    same = iota((snaps, snaps), 0) == iota((snaps, snaps), 1)
    eye = jnp.where(same, 1.0, 0.0)
    system = jnp.concatenate([kernel + ridge * eye, eye], axis=1)
    system_ref[...] = eliminate(system, range(snaps * 3 // 8))


def invert_kernel(modes, system_ref, inverse_ref):
    snaps = system_ref.shape[0]
    system = eliminate(system_ref[...], range(snaps * 3 // 8, snaps))
    inverse_ref[...] = system[:, snaps:]


def weight_kernel(
    coords_ref, kernel_ref, inverse_ref, first_ref, second_ref, lin_ref, weights, fit
):
    coords = unpack(coords_ref, first_ref.shape[0])
    design = highest(coords, first_ref[...], NN)
    design = design * (highest(coords, second_ref[...], NN) + lin_ref[...])
    weights[...] = highest(inverse_ref[...], design, NN)
    fit[...] = highest(kernel_ref[...], inverse_ref[...], NN)


def fit_kernel(
    place, rates_ref, coords_ref, weights, fit, reduced, operator, fitted, full, red
):
    modes = operator.shape[0]
    rates = unpack(rates_ref, modes)
    operator[...] = highest(rates, weights[...], (((0,), (0,)), ((), ())))
    full[...] = highest(fit[...], rates, NN)
    red[...] = jnp.concatenate([unpack(coords_ref, modes), rates], axis=1)
    each = fitted.shape[0]
    for i in range(each):
        at = pl.ds(place[0] * each + i, 1)
        fitted[i : i + 1, :] = full[at, :]
        reduced[i : i + 1, :] = red[at, :]


def body(
    states,
    basis,
    snapshot_times,
    pert_ids,
    pert_table,
    cycle_ids,
    groove_kernel,
    groove_gain,
    speed,
    force_amp,
    viscosity,
    coupling,
):
    snaps = states.shape[0]
    modes = basis.shape[0]
    chunks = snaps // CHUNK
    passages = lax.axis_size("passage")
    rounds = passages.bit_length() - 1
    position = lax.axis_index("passage")
    place = position.reshape(1).astype(jnp.int32)
    angles = 2.0 * math.pi * np.arange(PERIOD) / PERIOD
    table = jnp.asarray(np.cos(angles).astype(np.float32))

    def swap(value, mask):
        pairs = [(i, i ^ mask) for i in range(passages)]
        return lax.ppermute(value, "passage", pairs)

    def swap_chip(value, mask):
        return swap(value, mask + 1)

    operands = (
        snapshot_times,
        pert_ids,
        viscosity,
        coupling,
        table,
        pert_table,
        cycle_ids,
        speed,
        force_amp,
        states,
        basis,
    )
    first = pl.pallas_call(
        before_kernel,
        out_shape=jax.ShapeDtypeStruct((chunks, ROWS, LANES), BF16),
        in_specs=[HBM] * len(operands),
        out_specs=VMEM,
        scratch_shapes=[pltpu.SMEM(x.shape, x.dtype) for x in operands[:5]]
        + [pltpu.VMEM(x.shape, x.dtype) for x in operands[5:]]
        + [
            pltpu.VMEM((3 * CHUNK * NX, LANES), BF16),
            pltpu.SemaphoreType.DMA((len(operands),)),
        ],
        compiler_params=pltpu.CompilerParams(vmem_limit_bytes=24 * 2**20),
        name="before",
    )(*(x if x is pert_ids else pltpu.with_memory_space_constraint(x, pltpu.HBM) for x in operands))
    near = swap(first, 1)
    bits = rounds - 1
    edges_shape = jax.ShapeDtypeStruct((chunks, 2 * EDGE, LANES), BF16)
    head = EDGE + COORD

    def glue(kernel, name, rows, *args):
        return pl.pallas_call(
            kernel,
            out_shape=(jax.ShapeDtypeStruct((chunks, rows, LANES), BF16), edges_shape),
            in_specs=[SMEM] + [VMEM] * len(args),
            out_specs=(VMEM, VMEM),
            compiler_params=pltpu.CompilerParams(vmem_limit_bytes=16 * 2**20),
            name=name,
        )(place, *args)

    start = functools.partial(start_kernel, bits - 1)
    message, edges = glue(start, "start", head + 2 * BLOB, first, near)
    for bit in range(bits - 1, -1, -1):
        got = swap_chip(message, 2 << bit)
        if bit:
            rows = 2 * message.shape[1] - head
            step = functools.partial(next_kernel, bit - 1)
            message, edges = glue(step, "next", rows, message, got, edges)

    tile = jax.ShapeDtypeStruct((chunks, 8, LANES), F32)
    derivative, partial, coords = pl.pallas_call(
        after_kernel,
        out_shape=(jax.ShapeDtypeStruct(states.shape, BF16), tile, tile),
        in_specs=[SMEM] * 8 + [HBM, HBM] + [VMEM] * 8,
        out_specs=(VMEM, VMEM, VMEM),
        scratch_shapes=[
            pltpu.VMEM((passages * BLOB, 6 * LANES), F32),
            pltpu.VMEM((passages * BLOB, LANES), F32),
            pltpu.VMEM((passages * 8, LANES), F32),
            pltpu.VMEM((2, CHUNK * NX, LANES), F32),
            pltpu.VMEM((NV, NX, LANES), F32),
            pltpu.VMEM((NV, NX, LANES), F32),
            pltpu.VMEM((NV, NX, LANES), F32),
            pltpu.VMEM((NV, NX, LANES), F32),
            pltpu.VMEM(basis.shape, BF16),
            pltpu.VMEM(states.shape, BF16),
            pltpu.SemaphoreType.DMA((2,)),
        ],
        compiler_params=pltpu.CompilerParams(vmem_limit_bytes=32 * 2**20),
        name="after",
    )(
        snapshot_times,
        pert_ids,
        place,
        groove_kernel,
        groove_gain,
        viscosity,
        coupling,
        table,
        pltpu.with_memory_space_constraint(states, pltpu.HBM),
        pltpu.with_memory_space_constraint(basis, pltpu.HBM),
        pert_table,
        cycle_ids,
        speed,
        force_amp,
        first,
        near,
        message,
        got,
    )

    upper_first, upper_second = np.triu_indices(modes)
    features = modes + len(upper_first)
    pick_first = np.zeros((modes, features), np.float32)
    pick_second = np.zeros((modes, features), np.float32)
    linear = np.zeros((1, features), np.float32)
    pick_first[np.arange(modes), np.arange(modes)] = 1.0
    linear[0, :modes] = 1.0
    pick_first[upper_first, modes + np.arange(len(upper_first))] = 1.0
    pick_second[upper_second, modes + np.arange(len(upper_first))] = 1.0

    def small(kernel, name, outs, *args):
        return pl.pallas_call(
            kernel,
            out_shape=tuple(jax.ShapeDtypeStruct(shape, F32) for shape in outs),
            in_specs=[VMEM] * len(args),
            out_specs=tuple(VMEM for _ in outs),
            cost_estimate=pl.CostEstimate(flops=10**8, bytes_accessed=2**20, transcendentals=0),
            compiler_params=pltpu.CompilerParams(vmem_limit_bytes=16 * 2**20),
            name=name,
        )(*args)

    total = partial + swap(partial, 1)
    kernel, system = small(
        functools.partial(system_kernel, RIDGE_FACTOR * snaps, modes),
        "system",
        [(snaps, snaps), (snaps, 2 * snaps)],
        coords,
    )
    for r in range(1, rounds):
        got = swap_chip(total, 1 << r)
        if r == 1:
            total, kernel, system = lax.optimization_barrier((total + got, kernel, system))
            (inverse,) = small(
                functools.partial(invert_kernel, modes), "invert", [(snaps, snaps)], system
            )
        elif r == 2:
            total, inverse = lax.optimization_barrier((total + got, inverse))
            weights, fit = small(
                weight_kernel,
                "weights",
                [(snaps, features), (snaps, snaps)],
                coords,
                kernel,
                inverse,
                jnp.asarray(pick_first),
                jnp.asarray(pick_second),
                jnp.asarray(linear),
            )
        else:
            total = total + got
    each = snaps // passages
    reduced, operator, fitted = pl.pallas_call(
        fit_kernel,
        out_shape=(
            jax.ShapeDtypeStruct((each, 2 * modes), F32),
            jax.ShapeDtypeStruct((modes, features), F32),
            jax.ShapeDtypeStruct((each, modes), F32),
        ),
        in_specs=[SMEM] + [VMEM] * 4,
        out_specs=(VMEM, VMEM, VMEM),
        scratch_shapes=[pltpu.VMEM((snaps, modes), F32), pltpu.VMEM((snaps, 2 * modes), F32)],
        compiler_params=pltpu.CompilerParams(vmem_limit_bytes=16 * 2**20),
        name="fit",
    )(place, total, coords, weights, fit)
    return derivative, reduced, operator.T, fitted


def solution(mesh):
    in_specs = (
        P("member", None, None, "passage"),
        P(None, None, None, "passage"),
        P("member"),
        P(("member", "passage")),
        P(),
        P(None, "passage"),
        P(),
        P(),
        P(None, "passage"),
        P(None, "passage"),
        P(),
        P(),
    )
    out_specs = (
        P("member", None, None, "passage"),
        P(("member", "passage"), None),
        P("member", None),
        P(("member", "passage"), None),
    )
    return jax.shard_map(body, mesh=mesh, in_specs=in_specs, out_specs=out_specs, check_vma=False)
```

```python
import functools
import math

import jax
import jax.numpy as jnp
import numpy as np
from jax import lax
from jax.experimental import pallas as pl
from jax.experimental.pallas import tpu as pltpu
from jax.sharding import PartitionSpec as P

F32 = jnp.float32
BF16 = jnp.bfloat16
NRING = 5
NV = 5
NX = 16
LANES = 128
PERIOD = 37
TIME_STEP = 0.2
RIDGE_FACTOR = 1.0
UNROLL = 4
CHUNK = 32
BLOB = 16
COORD = 16
EDGE = 48
ROWS = BLOB + 2 * EDGE
RIGHT = slice(BLOB, BLOB + EDGE)
LEFT = slice(BLOB + EDGE, ROWS)

HIGH = lax.Precision.HIGHEST
NT = (((1,), (1,)), ((), ()))
VMEM = pl.BlockSpec(memory_space=pltpu.VMEM)
HBM = pl.BlockSpec(memory_space=pltpu.HBM)
SMEM = pl.BlockSpec(memory_space=pltpu.SMEM)


def iota(shape, axis):
    return lax.broadcasted_iota(jnp.int32, shape, axis)


def roll(value, shift, axis):
    size = value.shape[axis]
    return pltpu.roll(value, shift % size if isinstance(shift, int) else shift, axis)


def split(value):
    high = value.astype(BF16).astype(F32)
    return high, (value - high).astype(BF16).astype(F32)


def north_south(u):
    row = iota(u.shape, 0)
    north = jnp.where(row == NX - 1, 0.0, roll(u, -1, 0))
    south = jnp.where(row == 0, 0.0, roll(u, 1, 0))
    return north + south


def cycle_masks(ids):
    return jnp.concatenate([jnp.where(ids == g, 1.0, 0.0) for g in range(NRING)], axis=0)


def lane_part():
    return iota((8, LANES), 1) % 4


def flat(ref, first, count):
    parts = [ref[pl.ds(first, count), v].reshape(count * NX, LANES) for v in range(NV)]
    return jnp.concatenate(parts, axis=1)


def project(rows, modes_flat):
    width = modes_flat.shape[0]
    size = rows.shape[0]
    pairs = lax.dot_general(rows, modes_flat, NT, preferred_element_type=F32)
    diagonal = iota((size, width), 0) % NX == iota((size, width), 1) % NX
    pairs = jnp.where(diagonal, pairs, 0.0)
    pairs = jnp.sum(pairs.reshape(size // NX, NX, width), axis=1)
    high, low = split(pairs)
    modes = width // NX
    mode_of = iota((width, LANES), 0) // NX
    column = iota((width, LANES), 1)
    total = jnp.zeros((8, LANES), F32)
    for j in range(CHUNK // 8):
        pick = jnp.where(mode_of + j * modes == column, 1.0, 0.0).astype(BF16)
        both = jnp.concatenate([high[8 * j : 8 * j + 8], low[8 * j : 8 * j + 8]], axis=0)
        both = jnp.dot(both.astype(BF16), pick, preferred_element_type=F32)
        total += both[:8] + both[8:]
    return total


def unpack(ref, modes):
    rows = []
    for chunk in range(ref.shape[0]):
        tile = ref[chunk]
        rows += [tile[:, j * modes : (j + 1) * modes] for j in range(CHUNK // 8)]
    return jnp.concatenate(rows, axis=0)


def before_kernel(*refs):
    count = 11
    sources = refs[:count]
    out, states, basis, cells, cosines, cos_lanes = refs[count : count + 6]
    targets = (*refs[count + 6 : 2 * count + 4], states, basis)
    fields, sems = refs[2 * count + 4 :]
    copies = [
        pltpu.make_async_copy(source, target, sems.at[i])
        for i, (source, target) in enumerate(zip(sources, targets))
    ]
    for copy in copies:
        copy.start()
    times, pert_ids, visc, coup, table, pert, ids_ref, speed_ref, force_ref = targets[:-2]
    for copy in copies[:-2]:
        copy.wait()
    chunks = out.shape[0]
    speed = speed_ref[...]
    force = force_ref[...]
    damping = pert[pert_ids[0]]
    ids = ids_ref[...]
    visc_p = visc[NV - 1]
    lane = iota((NX, LANES), 1)
    half_speed = 0.5 * speed
    coef_east = jnp.where(lane == LANES - 1, 0.0, visc_p - half_speed)
    coef_west = jnp.where(lane == 0, 0.0, visc_p + half_speed)
    coef_own = coup[NV - 1, NV - 1] - 4.0 * visc_p - damping
    masks = cycle_masks(ids)
    masks_half = masks.astype(BF16)
    c8 = lane_part()
    row8 = iota((8, LANES), 0)
    quad = iota((NX, LANES), 1) // 4
    for index, field in enumerate((speed, force, damping, ids.astype(F32))):
        cells[index] = field
    scale = 1.0 / math.sqrt(NX * LANES)

    def pieces(column):
        out16 = jnp.zeros((NX, LANES), F32)
        spot = 0
        for field in (speed, force, damping, ids.astype(F32)):
            for piece in split(field):
                moved = roll(piece, spot - column, 1)
                out16 = jnp.where(lane == spot, moved, out16)
                spot += 1
        return jnp.where(iota((8, LANES), 1) < 64, out16[:8], roll(out16[8:], 64, 1))

    params_right = pieces(LANES - 1)
    params_left = pieces(0)

    east_hi, east_lo = split(jnp.where(lane == LANES - 1, visc_p - half_speed, 0.0))
    west_hi, west_lo = split(jnp.where(lane == 0, visc_p + half_speed, 0.0))
    ids_f = ids.astype(F32)
    id_east = jnp.where(lane == LANES - 1, ids_f, 0.0)
    id_west = jnp.where(lane == 0, ids_f, 0.0)
    ones = jnp.ones((NX, LANES), BF16)
    filler = jnp.zeros((LANES - 32, LANES), F32)

    def as_rows(east, west):
        stacked = jnp.concatenate([east, west, filler], axis=0).astype(BF16)
        return lax.dot_general(ones, stacked, NT, preferred_element_type=F32)[:8]

    row_hi = as_rows(east_hi, west_hi)
    row_lo = as_rows(east_lo, west_lo)
    row_id = as_rows(id_east, id_west)
    counts = lax.dot_general(ones, masks_half, NT, preferred_element_type=F32)[:8]
    spread = jnp.where(
        iota((NRING * NX, LANES), 1) == 32 + iota((NRING * NX, LANES), 0) // NX, 1.0, 0.0
    )
    counts = jnp.dot(counts, spread, precision=HIGH, preferred_element_type=F32)
    count_hi, count_lo = split(counts)
    row_hi = row_hi + count_hi
    row_lo = row_lo + count_lo

    size = CHUNK * NX
    same_x = iota((NRING * NX, 3 * size), 0) % NX == iota((NRING * NX, 3 * size), 1) % NX
    snap_of_row = iota((size, LANES), 0) // NX == iota((size, LANES), 1) // 4
    part_of_lane = iota((size, LANES), 1) % 4
    to_start = jnp.where(snap_of_row & (part_of_lane < 2), scale, 0.0)
    to_rate = jnp.where(snap_of_row & (part_of_lane >= 2), scale, 0.0)
    copies[-2].wait()

    def chunk_step(chunk, carry):
        first = chunk * CHUNK

        def snap(k, carried):
            edges, cos_row = carried
            u = [states[first + k, v].astype(F32) for v in range(NV)]
            p = u[NV - 1]
            cosine = table[lax.rem(times[first + k], PERIOD)]
            cosines[pl.ds(first + k, 1), :] = jnp.full((1, LANES), cosine, F32)
            cos_row = jnp.where(quad[:8] == k, cosine, cos_row)
            rate = coef_east * roll(p, -1, 1) + coef_west * roll(p, 1, 1)
            rate = rate + visc_p * north_south(p) + coef_own * p + cosine * force
            for v in range(NV - 1):
                rate = rate + coup[NV - 1, v] * u[v]
            high, low = split(rate)
            at = pl.multiple_of(k * NX, NX)
            fields[pl.ds(at, NX), :] = p.astype(BF16)
            fields[pl.ds(pl.multiple_of(size + at, NX), NX), :] = high.astype(BF16)
            fields[pl.ds(pl.multiple_of(2 * size + at, NX), NX), :] = low.astype(BF16)
            edges = tuple(
                jnp.where(quad == k, roll(u[v], 4 * k + 2, 1), edges[v]) for v in range(NV)
            )
            return edges, cos_row

        carried = tuple(jnp.zeros((NX, LANES), F32) for _ in range(NV)), jnp.zeros((8, LANES), F32)
        if chunks == 1:
            for k in range(CHUNK):
                carried = snap(k, carried)
        else:
            carried = lax.fori_loop(0, CHUNK, snap, carried)
        edges, cos_lanes[chunk] = carried
        sums = lax.dot_general(masks_half, fields[...], NT, preferred_element_type=F32)
        sums = jnp.where(same_x, sums, 0.0)
        by_cycle = jnp.sum(sums.reshape(NRING, NX, 3 * size), axis=1)
        by_cycle = jnp.concatenate([by_cycle, jnp.zeros((3, 3 * size), F32)], axis=0)
        start = by_cycle[:, :size]
        rate = by_cycle[:, size : 2 * size] + by_cycle[:, 2 * size :]
        packed = jnp.dot(start, to_start, precision=HIGH, preferred_element_type=F32)
        packed += jnp.dot(rate, to_rate, precision=HIGH, preferred_element_type=F32)
        high, low = split(packed)
        packed = jnp.where(c8 % 2 == 0, high, low)
        packed = jnp.where(row8 < NRING, packed, 0.0)
        for at, row in ((5, row_hi), (6, row_lo), (7, row_id)):
            packed = jnp.where(row8 == at, row, packed)
        p_low, p_high = edges[NV - 1][:8], edges[NV - 1][8:]
        p_edges = jnp.where(
            (c8 == 1) | (c8 == 2), p_low, jnp.where(c8 == 3, roll(p_high, 1, 1), roll(p_high, -1, 1))
        )
        right = [jnp.where(c8 < 2, t[:8], roll(t[8:], 2, 1)) for t in edges]
        left = [jnp.where(c8 >= 2, t[:8], roll(t[8:], -2, 1)) for t in edges]
        rows = [packed, p_edges, *right, params_right, *left, params_left]
        out[chunk] = jnp.concatenate(rows, axis=0).astype(BF16)
        return carry

    if chunks == 1:
        chunk_step(0, 0)
    else:
        lax.fori_loop(0, chunks, chunk_step, 0)
    copies[-1].wait()


def coords_kernel(states, basis, after, out):
    flat_basis = flat(basis, 0, basis.shape[0])
    if out.shape[0] == 1:
        out[0] = project(flat(states, 0, CHUNK), flat_basis)
        return

    def chunk_step(chunk, carry):
        out[chunk] = project(flat(states, chunk * CHUNK, CHUNK), flat_basis)
        return carry

    lax.fori_loop(0, out.shape[0], chunk_step, 0)


def start_kernel(top, place, first, near, coords, out, edges):
    odd = place[0] % 2 == 1
    for chunk in range(out.shape[0]):
        mine, other = first[chunk].astype(F32), near[chunk].astype(F32)
        low, high = jnp.where(odd, other, mine), jnp.where(odd, mine, other)
        right, left = high[RIGHT], low[LEFT]
        edges[chunk] = jnp.concatenate([right, left], axis=0).astype(BF16)
        payload = jnp.where(goes_right(place[0], top), right, left)
        rows = [payload, *split(coords[chunk]), low[:BLOB], high[:BLOB]]
        out[chunk] = jnp.concatenate(rows, axis=0).astype(BF16)


def goes_right(me, bit):
    if bit == 0:
        return me % 2 == 1
    lower = jnp.bitwise_and(jnp.right_shift(me, 1), (1 << bit) - 1)
    return lower == (1 << bit) - 1


def goes_left(me, bit):
    lower = jnp.bitwise_and(jnp.right_shift(me, 1), (1 << bit) - 1)
    return lower == 0


def next_kernel(bit, place, sent, got, edges, out, new_edges=None):
    me = place[0]
    for chunk in range(out.shape[0]):
        mine, other = sent[chunk].astype(F32), got[chunk].astype(F32)
        both = edges[chunk].astype(F32)
        right = jnp.where(goes_right(me, bit + 1), other[:EDGE], both[:EDGE])
        left = jnp.where(goes_left(me, bit + 1), other[:EDGE], both[EDGE:])
        if new_edges is not None:
            new_edges[chunk] = jnp.concatenate([right, left], axis=0).astype(BF16)
        payload = jnp.where(goes_right(me, bit), right, left)
        total = mine[EDGE : EDGE + COORD] + other[EDGE : EDGE + COORD]
        rows = [payload, *split(total[:8] + total[8:]), mine[EDGE + COORD :], other[EDGE + COORD :]]
        out[chunk] = jnp.concatenate(rows, axis=0).astype(BF16)


def prepare_kernel(visc, coup, kern, gain, cells, after, mixer, east_coef, west_coef):
    half_speed = 0.5 * cells[0]
    lane = iota((NX, LANES), 1)
    for v in range(NV):
        east_coef[v] = jnp.where(lane == LANES - 1, 0.0, visc[v] - half_speed)
        west_coef[v] = jnp.where(lane == 0, 0.0, visc[v] + half_speed)
    deep = NV * NX
    col = iota((NX, 3 * deep), 1)
    col_var, col_x = col % deep // NX, col % NX
    row_x = iota((NX, 3 * deep), 0)
    beside = jnp.abs(row_x - col_x) == 1
    blocks = []
    for v in range(NV):
        weight = jnp.zeros((NX, 3 * deep), F32)
        for other in range(NV):
            value = coup[v, other] - (4.0 * visc[v] if other == v else 0.0)
            weight = jnp.where((col_var == other) & (row_x == col_x), value, weight)
        blocks.append(jnp.where((col_var == v) & beside, visc[v], weight))
    high, low = split(jnp.concatenate(blocks, axis=0))
    col = iota((deep, 3 * deep), 1)
    mixer[...] = jnp.where((col < deep) | (col >= 2 * deep), high, low).astype(BF16)


def local_kernel(
    offset,
    states,
    cells,
    cosines,
    mixer_ref,
    east_coef,
    west_coef,
    after,
    out,
):
    count = out.shape[0]
    deep = NV * NX
    force = cells[1]
    damping = cells[2]
    mixer = mixer_ref[...]

    def linear(u, mixed):
        result = []
        for v in range(NV):
            rate = mixed[NX * v : NX * v + NX] - damping * u[v]
            rate = rate + east_coef[v] * roll(u[v], -1, 1) + west_coef[v] * roll(u[v], 1, 1)
            result.append(rate)
        return result

    def snap(k):
        half = states[offset + k].reshape(deep, LANES)
        u = [states[offset + k, v].astype(F32) for v in range(NV)]
        drive = cosines[pl.ds(offset + k, 1), :] * force
        mixed = jnp.dot(
            mixer[:, : 2 * deep],
            jnp.concatenate([half, half], axis=0),
            preferred_element_type=F32,
        )
        rate = [r + drive for r in linear(u, mixed)]
        stack = jnp.concatenate(rate, axis=0)
        high = stack.astype(BF16)
        low = (stack - high.astype(F32)).astype(BF16)
        mixed = jnp.dot(
            mixer, jnp.concatenate([high, high, low], axis=0), preferred_element_type=F32
        )
        again = linear(rate, mixed)
        for v in range(NV):
            out[k, v] = rate[v] + 0.5 * TIME_STEP * again[v]

    def snaps(step, carry):
        for i in range(UNROLL):
            snap(step * UNROLL + i)
        return carry

    lax.fori_loop(0, count // UNROLL, snaps, 0)


def after_kernel(parts, *refs):
    place, kern, gain, visc, coup, basis, cells, cos_lanes = refs[:8]
    own_ref, near_ref, sent_ref, last_ref = refs[8:12]
    bases = refs[12 : 12 + parts]
    deriv, partial, mixed, raw, cyc0, grooves, ends = refs[12 + parts :]
    chunks = own_ref.shape[0]
    passages = kern.shape[0]
    me = place[0]
    base = me - lax.rem(me, 2)
    bits = passages.bit_length() - 2
    odd = me % 2 == 1
    speed = cells[0]
    damping = cells[2]
    ids = cells[3]
    half_speed = 0.5 * speed
    lane = iota((NX, LANES), 1)
    c16 = lane % 4
    masks = cycle_masks(ids).astype(BF16)
    masks_twice = jnp.concatenate([masks, masks], axis=0)
    scale = 1.0 / math.sqrt(NX * LANES)
    size = CHUNK * NX

    src = iota((LANES, LANES), 0)
    dst = iota((LANES, LANES), 1) // 4 * 4
    mixers = [(src == dst) | (src == dst + 1), (src == dst + 2) | (src == dst + 3)]
    mixers += [src == dst + 2, src == dst + 1, src == dst + 3, src == dst]
    mix = jnp.concatenate([jnp.where(m, 1.0, 0.0).astype(BF16) for m in mixers], axis=1)
    pick_snap = jnp.where(iota((size, LANES), 1) == iota((size, LANES), 0) // NX * 4, 1.0, 0.0)
    pick_snap = pick_snap.astype(BF16)
    wide = 4 * NRING * NX
    same_x = iota((size, wide), 0) % NX == iota((size, wide), 1) % NX

    def flat_basis():
        return flat(basis, 0, basis.shape[0])

    def unpack_right(t):
        return jnp.concatenate([t, roll(t, -2, 1)], axis=0)

    def unpack_left(t):
        return jnp.concatenate([t, roll(t, 2, 1)], axis=0)

    def chunk_step(chunk, carry):
        first = chunk * CHUNK
        head = EDGE + COORD
        half = passages // 2 * BLOB
        raw[:half, :] = sent_ref[chunk, head:, :].astype(F32)
        raw[half:, :] = last_ref[chunk, head:, :].astype(F32)
        summed = sent_ref[chunk, EDGE:head, :].astype(F32)
        summed += last_ref[chunk, EDGE:head, :].astype(F32)
        partial[chunk, :8, :] = summed[:8] + summed[8:]
        mixed[...] = jnp.dot(raw[...].astype(BF16), mix, preferred_element_type=F32)

        def slot(offset):
            other = lax.rem(me + offset + passages, passages)
            flips = jnp.bitwise_xor(base, other)
            index = jnp.bitwise_and(flips, 1)
            for bit in range(bits):
                moved = jnp.bitwise_and(jnp.right_shift(flips, bit + 1), 1)
                index = index + jnp.left_shift(moved, bits - bit)
            return pl.multiple_of(index * BLOB, BLOB)

        def load(offset, carry):
            cyc0[pl.ds(pl.multiple_of(offset * 8, 8), 8), :] = mixed[pl.ds(slot(offset), 8), :LANES]
            return carry

        lax.fori_loop(0, passages, load, 0, unroll=passages <= 16)

        def plenum0(offset):
            total = jnp.zeros((8, LANES), F32)
            if passages <= 16 and isinstance(offset, int):
                for other in range(passages):
                    total += kern[(offset - other) % passages] * cyc0[other * 8 : other * 8 + 8, :]
                return total

            def add(other, total):
                weight = kern[lax.rem(offset - other + 2 * passages, passages)]
                return total + weight * cyc0[pl.ds(pl.multiple_of(other * 8, 8), 8), :]

            return lax.fori_loop(0, passages, add, total)

        row8 = iota((8, LANES), 0)
        lane8 = iota((8, LANES), 1)

        def second(offset, total):
            own = slot(offset)
            east, west = slot(offset + 1), slot(offset - 1)
            coefs = raw[pl.ds(own, 8), :]
            id_row = coefs[7:8, :].astype(jnp.int32)
            hit = (id_row == row8) & (lane8 < 32)
            left = jnp.concatenate(
                [jnp.where(hit, coefs[5:6, :], 0.0), jnp.where(hit, coefs[6:7, :], 0.0)], axis=0
            )
            right = jnp.concatenate(
                [
                    mixed[pl.ds(pl.multiple_of(east + 8, 8), 8), 2 * LANES : 3 * LANES],
                    mixed[pl.ds(pl.multiple_of(east + 8, 8), 8), 4 * LANES : 5 * LANES],
                    mixed[pl.ds(pl.multiple_of(west + 8, 8), 8), 3 * LANES : 4 * LANES],
                    mixed[pl.ds(pl.multiple_of(west + 8, 8), 8), 5 * LANES :],
                    jnp.zeros((LANES - 32, LANES), F32),
                ],
                axis=0,
            )
            edge = jnp.dot(left.astype(BF16), right.astype(BF16), preferred_element_type=F32)
            edge = (edge[:8] + edge[8:]) * scale
            count = jnp.where(lane8 == 32 + row8, coefs[5:6, :] + coefs[6:7, :], 0.0)
            count = jnp.sum(count, axis=1, keepdims=True) * (scale * gain[NV - 1])
            rate = mixed[pl.ds(own, 8), LANES : 2 * LANES] + edge + count * plenum0(offset)
            if isinstance(offset, int):
                start = cyc0[offset * 8 : offset * 8 + 8, :]
                weight = kern[-offset % passages]
            else:
                start = cyc0[pl.ds(pl.multiple_of(offset * 8, 8), 8), :]
                weight = kern[lax.rem(passages - offset, passages)]
            return total + weight * (start + TIME_STEP * rate)

        total = jnp.zeros((8, LANES), F32)
        if passages <= 16:
            for offset in range(passages):
                total = second(offset, total)
        else:
            total = lax.fori_loop(0, passages, second, total)
        own0, own1 = plenum0(0), total
        west0, east0 = plenum0(passages - 1), plenum0(1)

        stack = []
        for tile in (own0, own1):
            for piece in split(tile):
                stack += [jnp.broadcast_to(piece[g : g + 1], (NX, LANES)) for g in range(NRING)]
        stack = jnp.concatenate(stack, axis=0).astype(BF16)
        picked = lax.dot_general(pick_snap, stack, NT, preferred_element_type=F32)
        picked = jnp.where(same_x, picked, 0.0).astype(BF16)
        for stage in range(2):
            grooves[stage] = jnp.dot(
                picked[:, stage * wide // 2 : (stage + 1) * wide // 2],
                masks_twice,
                preferred_element_type=F32,
            )

        near = near_ref[chunk].astype(F32)
        own = own_ref[chunk].astype(F32)
        far = last_ref[chunk, :EDGE, :].astype(F32)
        west = jnp.where(odd, near[RIGHT], far)
        east = jnp.where(odd, far, near[LEFT])

        def param(side, index):
            t = side[40:48]
            low = t[:, index : index + 1] + t[:, index + 1 : index + 2]
            high = t[:, 64 + index : 65 + index] + t[:, 65 + index : 66 + index]
            return jnp.broadcast_to(jnp.concatenate([low, high], axis=0), (NX, LANES))

        speed_h, force_h, damp_h, ids_h = (
            jnp.where(c16 < 2, param(west, 2 * i), param(east, 2 * i)) for i in range(4)
        )
        groove_h = jnp.zeros((NX, LANES), F32)
        for g in range(NRING):
            value = jnp.where(c16 < 2, west0[g : g + 1], east0[g : g + 1])
            groove_h = jnp.where(ids_h == g, value, groove_h)
        cos_h = jnp.concatenate([cos_lanes[chunk]] * 2, axis=0)
        halo, ours, rates = [], [], []
        for v in range(NV):
            at = slice(8 * v, 8 * v + 8)
            halo.append(jnp.where(c16 < 2, unpack_right(west[at]), unpack_left(east[at])))
            ours.append(
                jnp.where(c16 < 2, unpack_right(own[RIGHT][at]), unpack_left(own[LEFT][at]))
            )
        for v in range(NV):
            h = halo[v]
            e = roll(jnp.where(c16 == 3, h, ours[v]), -1, 1)
            w = roll(jnp.where(c16 == 0, h, ours[v]), 1, 1)
            rate = visc[v] * (e + w + north_south(h) - 4.0 * h) - 0.5 * speed_h * (e - w)
            rate = rate - damp_h * h + gain[v] * groove_h + force_h * cos_h
            for other in range(NV):
                rate = rate + coup[v, other] * halo[other]
            rates.append(rate)

        def columns(field):
            tiles = [
                jnp.broadcast_to(field[:, c : c + 1], (NX, LANES))
                for c in (LANES - 2, LANES - 1, 0, 1)
            ]
            return jnp.where(
                c16 < 2,
                jnp.where(c16 == 0, tiles[0], tiles[1]),
                jnp.where(c16 == 2, tiles[2], tiles[3]),
            )

        def across(t):
            return jnp.where(c16 == 2, roll(t, 1, 1), roll(t, -1, 1))

        inner = (c16 == 1) | (c16 == 2)
        signed_speed = columns(half_speed) * jnp.where(c16 < 2, -1.0, 1.0)
        damp_e = columns(damping)
        half_step = 0.5 * TIME_STEP
        shifts = [
            jnp.where(inner, (visc[v] + signed_speed) * across(halo[v]), 0.0) for v in range(NV)
        ]
        for v in range(NV):
            change = shifts[v]
            rate = visc[v] * (north_south(change) - 4.0 * change) - damp_e * change
            for other in range(NV):
                rate = rate + coup[v, other] * shifts[other]
            rate = rate + (visc[v] + signed_speed) * across(rates[v])
            beside = jnp.where(c16 == 0, roll(change, -1, 1), roll(change, 1, 1))
            outer = (visc[v] + signed_speed) * beside
            ends[v] = jnp.where(inner, change + half_step * rate, half_step * outer)

        at_ends = (lane < 2) | (lane >= LANES - 2)
        damp_step = half_step * damping
        speed_step = half_step * half_speed
        diffuse = [half_step * visc[v] * gain[v] for v in range(NV)]
        couple = []
        for v in range(NV):
            total = coup[v, 0] * gain[0]
            for other in range(1, NV):
                total = total + coup[v, other] * gain[other]
            couple.append(half_step * total)

        def snap(k, share, index):
            at = pl.ds(pl.multiple_of(k * NX, NX), NX)
            m0, m1 = grooves[0, at, :], grooves[1, at, :]
            e = jnp.where(lane == LANES - 1, 0.0, roll(m0, -1, 1))
            w = jnp.where(lane == 0, 0.0, roll(m0, 1, 1))
            spread = 2 * LANES - 4 * k - 2
            lap = e + w + north_south(m0) - 4.0 * m0
            own = 0.5 * (m0 + m1) - speed_step * (e - w) - damp_step * m0
            for v in range(NV):
                total = share[index, v] + gain[v] * own + diffuse[v] * lap + couple[v] * m0
                total = total + jnp.where(at_ends, roll(ends[v], spread, 1), 0.0)
                deriv[first + k, v] = total.astype(BF16)

        done = 0
        for share in bases:
            count = share.shape[0] if chunks == 1 else CHUNK

            def snaps(step, carry, share=share, done=done):
                for i in range(UNROLL):
                    k = step * UNROLL + i
                    snap(done + k, share, k if chunks == 1 else first + k)
                return carry

            lax.fori_loop(0, count // UNROLL, snaps, 0)
            done += count
        partial[chunk, 8:, :] = project(flat(deriv, first, CHUNK), flat_basis())
        return carry

    if chunks == 1:
        chunk_step(0, 0)
    else:
        lax.fori_loop(0, chunks, chunk_step, 0)


def eliminate(system, columns):
    row = iota(system.shape, 0)
    for j in columns:
        pivot = system[j : j + 1, :] / system[j : j + 1, j : j + 1]
        factor = jnp.where(row == j, 0.0, jnp.broadcast_to(system[:, j : j + 1], system.shape))
        system = jnp.where(row == j, pivot, system - factor * pivot)
    return system


highest = functools.partial(lax.dot_general, precision=HIGH, preferred_element_type=F32)
NN = (((1,), (0,)), ((), ()))


def system_kernel(ridge, modes, coords_ref, deriv, kernel_ref, system_ref, deriv_out, sem):
    write = pltpu.make_async_copy(deriv, deriv_out, sem)
    write.start()
    coords = unpack(coords_ref, modes)
    snaps = coords.shape[0]
    gram = highest(coords, coords, NT)
    squares = coords * coords
    kernel = gram + 0.5 * (gram * gram + highest(squares, squares, NT))
    kernel_ref[...] = kernel
    same = iota((snaps, snaps), 0) == iota((snaps, snaps), 1)
    eye = jnp.where(same, 1.0, 0.0)
    system = jnp.concatenate([kernel + ridge * eye, eye], axis=1)
    system_ref[...] = eliminate(system, range(snaps // 4))
    write.wait()


def invert_kernel(system_ref, out_ref):
    snaps = system_ref.shape[0]
    out_ref[...] = eliminate(system_ref[...], range(snaps // 4, snaps * 5 // 8))


def weight_kernel(
    coords_ref, kernel_ref, system_ref, first_ref, second_ref, lin_ref, weights, fit
):
    snaps = kernel_ref.shape[0]
    inverse = eliminate(system_ref[...], range(snaps * 5 // 8, snaps))[:, snaps:]
    coords = unpack(coords_ref, first_ref.shape[0])
    design = highest(coords, first_ref[...], NN)
    design = design * (highest(coords, second_ref[...], NN) + lin_ref[...])
    weights[...] = highest(inverse, design, NN)
    fit[...] = highest(kernel_ref[...], inverse, NN)


def fit_kernel(
    place, rates_ref, coords_ref, weights, fit, reduced, operator, fitted, full, red
):
    modes = operator.shape[0]
    rates = unpack(rates_ref, modes)
    operator[...] = highest(rates, weights[...], (((0,), (0,)), ((), ())))
    full[...] = highest(fit[...], rates, NN)
    red[...] = jnp.concatenate([unpack(coords_ref, modes), rates], axis=1)
    each = fitted.shape[0]
    for i in range(each):
        at = pl.ds(place[0] * each + i, 1)
        fitted[i : i + 1, :] = full[at, :]
        reduced[i : i + 1, :] = red[at, :]


def body(
    states,
    basis,
    snapshot_times,
    pert_ids,
    pert_table,
    cycle_ids,
    groove_kernel,
    groove_gain,
    speed,
    force_amp,
    viscosity,
    coupling,
):
    snaps = states.shape[0]
    modes = basis.shape[0]
    chunks = snaps // CHUNK
    passages = lax.axis_size("passage")
    rounds = passages.bit_length() - 1
    position = lax.axis_index("passage")
    place = position.reshape(1).astype(jnp.int32)
    angles = 2.0 * math.pi * np.arange(PERIOD) / PERIOD
    table = jnp.asarray(np.cos(angles).astype(np.float32))

    def swap(value, mask):
        pairs = [(i, i ^ mask) for i in range(passages)]
        return lax.ppermute(value, "passage", pairs)

    def swap_chip(value, mask):
        return swap(value, mask + 1)

    operands = (
        snapshot_times,
        pert_ids,
        viscosity,
        coupling,
        table,
        pert_table,
        cycle_ids,
        speed,
        force_amp,
        states,
        basis,
    )
    first, held, held_basis, cells, cosines, cos_lanes = pl.pallas_call(
        before_kernel,
        out_shape=(
            jax.ShapeDtypeStruct((chunks, ROWS, LANES), BF16),
            jax.ShapeDtypeStruct(states.shape, BF16),
            jax.ShapeDtypeStruct(basis.shape, BF16),
            jax.ShapeDtypeStruct((4, NX, LANES), F32),
            jax.ShapeDtypeStruct((snaps, LANES), F32),
            jax.ShapeDtypeStruct((chunks, 8, LANES), F32),
        ),
        in_specs=[HBM] * len(operands),
        out_specs=(VMEM,) * 6,
        scratch_shapes=[pltpu.SMEM(x.shape, x.dtype) for x in operands[:5]]
        + [pltpu.VMEM(x.shape, x.dtype) for x in operands[5:9]]
        + [
            pltpu.VMEM((3 * CHUNK * NX, LANES), BF16),
            pltpu.SemaphoreType.DMA((len(operands),)),
        ],
        compiler_params=pltpu.CompilerParams(vmem_limit_bytes=24 * 2**20),
        name="before",
    )(*(x if x is pert_ids else pltpu.with_memory_space_constraint(x, pltpu.HBM) for x in operands))
    near = swap(first, 1)
    bits = rounds - 1
    edges_shape = jax.ShapeDtypeStruct((chunks, 2 * EDGE, LANES), BF16)
    head = EDGE + COORD

    def glue(kernel, name, rows, *args, more=True):
        outs = (jax.ShapeDtypeStruct((chunks, rows, LANES), BF16), edges_shape)
        return pl.pallas_call(
            kernel,
            out_shape=outs if more else outs[:1],
            in_specs=[SMEM] + [VMEM] * len(args),
            out_specs=(VMEM, VMEM) if more else (VMEM,),
            compiler_params=pltpu.CompilerParams(vmem_limit_bytes=16 * 2**20),
            name=name,
        )(place, *args)

    hidden = pl.CostEstimate(flops=2 * 10**9, bytes_accessed=2**20, transcendentals=0)
    anywhere = pl.BlockSpec(memory_space=pl.ANY)
    tile = jax.ShapeDtypeStruct((chunks, 8, LANES), F32)
    coords = pl.pallas_call(
        coords_kernel,
        out_shape=tile,
        in_specs=[VMEM, VMEM, anywhere],
        out_specs=VMEM,
        cost_estimate=hidden,
        compiler_params=pltpu.CompilerParams(vmem_limit_bytes=24 * 2**20),
        name="coords",
    )(held, held_basis, first)
    near, coords = lax.optimization_barrier((near, coords))

    def local(offset, count, after):
        return pl.pallas_call(
            functools.partial(local_kernel, offset),
            out_shape=jax.ShapeDtypeStruct((count,) + states.shape[1:], F32),
            in_specs=[VMEM] * 6 + [anywhere],
            out_specs=VMEM,
            cost_estimate=hidden,
            compiler_params=pltpu.CompilerParams(vmem_limit_bytes=24 * 2**20),
            name="local",
        )(
            held,
            cells,
            cosines,
            mixer,
            east_coef,
            west_coef,
            after,
        )

    start = functools.partial(start_kernel, bits - 1)
    message, edges = glue(start, "start", head + 2 * BLOB, first, near, coords)
    mixer, east_coef, west_coef = pl.pallas_call(
        prepare_kernel,
        out_shape=(
            jax.ShapeDtypeStruct((NV * NX, 3 * NV * NX), BF16),
            jax.ShapeDtypeStruct((NV, NX, LANES), F32),
            jax.ShapeDtypeStruct((NV, NX, LANES), F32),
        ),
        in_specs=[SMEM] * 4 + [VMEM, anywhere],
        out_specs=(VMEM, VMEM, VMEM),
        cost_estimate=hidden,
        compiler_params=pltpu.CompilerParams(vmem_limit_bytes=16 * 2**20),
        name="prepare",
    )(viscosity, coupling, groove_kernel, groove_gain, cells, message)
    shares = [4, 12, 16] if chunks == 1 and bits == 3 else [snaps]
    bases, offset = [], 0
    for bit in range(bits - 1, -1, -1):
        got = swap_chip(message, 2 << bit)
        if shares:
            count = shares.pop(0)
            base = local(offset, count, message)
            got, base = lax.optimization_barrier((got, base))
            bases.append(base)
            offset += count
        if bit:
            rows = 2 * message.shape[1] - head
            step = functools.partial(next_kernel, bit - 1)
            message, *edges = glue(step, "next", rows, message, got, edges, more=bit > 1)
            edges = edges[0] if edges else None

    derivative, partial = pl.pallas_call(
        functools.partial(after_kernel, len(bases)),
        out_shape=(
            jax.ShapeDtypeStruct(states.shape, BF16),
            jax.ShapeDtypeStruct((chunks, 16, LANES), F32),
        ),
        in_specs=[SMEM] * 5 + [VMEM] * (7 + len(bases)),
        out_specs=(VMEM, VMEM),
        scratch_shapes=[
            pltpu.VMEM((passages * BLOB, 6 * LANES), F32),
            pltpu.VMEM((passages * BLOB, LANES), F32),
            pltpu.VMEM((passages * 8, LANES), F32),
            pltpu.VMEM((2, CHUNK * NX, LANES), F32),
            pltpu.VMEM((NV, NX, LANES), F32),
        ],
        compiler_params=pltpu.CompilerParams(vmem_limit_bytes=32 * 2**20),
        name="after",
    )(
        place,
        groove_kernel,
        groove_gain,
        viscosity,
        coupling,
        held_basis,
        cells,
        cos_lanes,
        first,
        near,
        message,
        got,
        *bases,
    )

    upper_first, upper_second = np.triu_indices(modes)
    features = modes + len(upper_first)
    pick_first = np.zeros((modes, features), np.float32)
    pick_second = np.zeros((modes, features), np.float32)
    linear = np.zeros((1, features), np.float32)
    pick_first[np.arange(modes), np.arange(modes)] = 1.0
    linear[0, :modes] = 1.0
    pick_first[upper_first, modes + np.arange(len(upper_first))] = 1.0
    pick_second[upper_second, modes + np.arange(len(upper_first))] = 1.0

    def small(kernel, name, outs, *args):
        return pl.pallas_call(
            kernel,
            out_shape=tuple(jax.ShapeDtypeStruct(shape, F32) for shape in outs),
            in_specs=[VMEM] * len(args),
            out_specs=tuple(VMEM for _ in outs),
            cost_estimate=hidden,
            compiler_params=pltpu.CompilerParams(vmem_limit_bytes=16 * 2**20),
            name=name,
        )(*args)

    total = partial + swap(partial, 1)
    coords, total, derivative = lax.optimization_barrier((total[:, :8], total[:, 8:], derivative))
    kernel, system, derivative = pl.pallas_call(
        functools.partial(system_kernel, RIDGE_FACTOR * snaps, modes),
        out_shape=(
            jax.ShapeDtypeStruct((snaps, snaps), F32),
            jax.ShapeDtypeStruct((snaps, 2 * snaps), F32),
            jax.ShapeDtypeStruct(states.shape, BF16),
        ),
        in_specs=[VMEM, VMEM],
        out_specs=(VMEM, VMEM, HBM),
        scratch_shapes=[pltpu.SemaphoreType.DMA],
        cost_estimate=hidden,
        compiler_params=pltpu.CompilerParams(vmem_limit_bytes=16 * 2**20),
        name="system",
    )(coords, derivative)
    for r in range(1, rounds):
        got = swap_chip(total, 1 << r)
        if r == 1:
            got, kernel, system = lax.optimization_barrier((got, kernel, system))
            total = total + got
            (inverse,) = small(invert_kernel, "invert", [(snaps, 2 * snaps)], system)
        elif r == 2:
            total, inverse = lax.optimization_barrier((total + got, inverse))
            weights, fit = small(
                weight_kernel,
                "weights",
                [(snaps, features), (snaps, snaps)],
                coords,
                kernel,
                inverse,
                jnp.asarray(pick_first),
                jnp.asarray(pick_second),
                jnp.asarray(linear),
            )
        else:
            total = total + got
    each = snaps // passages
    reduced, operator, fitted = pl.pallas_call(
        fit_kernel,
        out_shape=(
            jax.ShapeDtypeStruct((each, 2 * modes), F32),
            jax.ShapeDtypeStruct((modes, features), F32),
            jax.ShapeDtypeStruct((each, modes), F32),
        ),
        in_specs=[SMEM] + [VMEM] * 4,
        out_specs=(VMEM, VMEM, VMEM),
        scratch_shapes=[pltpu.VMEM((snaps, modes), F32), pltpu.VMEM((snaps, 2 * modes), F32)],
        compiler_params=pltpu.CompilerParams(vmem_limit_bytes=16 * 2**20),
        name="fit",
    )(place, total, coords, weights, fit)
    return derivative, reduced, operator.T, fitted


def solution(mesh):
    in_specs = (
        P("member", None, None, "passage"),
        P(None, None, None, "passage"),
        P("member"),
        P(("member", "passage")),
        P(),
        P(None, "passage"),
        P(),
        P(),
        P(None, "passage"),
        P(None, "passage"),
        P(),
        P(),
    )
    out_specs = (
        P("member", None, None, "passage"),
        P(("member", "passage"), None),
        P("member", None),
        P(("member", "passage"), None),
    )
    return jax.shard_map(body, mesh=mesh, in_specs=in_specs, out_specs=out_specs, check_vma=False)
```

```python
import functools
import math

import jax
import jax.numpy as jnp
import numpy as np
from jax import lax
from jax.experimental import pallas as pl
from jax.experimental.pallas import tpu as pltpu
from jax.sharding import PartitionSpec as P

F32 = jnp.float32
BF16 = jnp.bfloat16
NRING = 5
NV = 5
NX = 16
LANES = 128
PERIOD = 37
TIME_STEP = 0.2
RIDGE_FACTOR = 1.0
UNROLL = 4
CHUNK = 32
BLOB = 16
COORD = 16
EDGE = 48
ROWS = BLOB + 2 * EDGE
RIGHT = slice(BLOB, BLOB + EDGE)
LEFT = slice(BLOB + EDGE, ROWS)

HIGH = lax.Precision.HIGHEST
NT = (((1,), (1,)), ((), ()))
VMEM = pl.BlockSpec(memory_space=pltpu.VMEM)
HBM = pl.BlockSpec(memory_space=pltpu.HBM)
SMEM = pl.BlockSpec(memory_space=pltpu.SMEM)


def iota(shape, axis):
    return lax.broadcasted_iota(jnp.int32, shape, axis)


def roll(value, shift, axis):
    size = value.shape[axis]
    return pltpu.roll(value, shift % size if isinstance(shift, int) else shift, axis)


def split(value):
    high = value.astype(BF16).astype(F32)
    return high, (value - high).astype(BF16).astype(F32)


def north_south(u):
    row = iota(u.shape, 0)
    north = jnp.where(row == NX - 1, 0.0, roll(u, -1, 0))
    south = jnp.where(row == 0, 0.0, roll(u, 1, 0))
    return north + south


def cycle_masks(ids):
    return jnp.concatenate([jnp.where(ids == g, 1.0, 0.0) for g in range(NRING)], axis=0)


def lane_part():
    return iota((8, LANES), 1) % 4


def flat(ref, first, count):
    parts = [ref[pl.ds(first, count), v].reshape(count * NX, LANES) for v in range(NV)]
    return jnp.concatenate(parts, axis=1)


def project(rows, modes_flat):
    width = modes_flat.shape[0]
    size = rows.shape[0]
    pairs = lax.dot_general(rows, modes_flat, NT, preferred_element_type=F32)
    diagonal = iota((size, width), 0) % NX == iota((size, width), 1) % NX
    pairs = jnp.where(diagonal, pairs, 0.0)
    pairs = jnp.sum(pairs.reshape(size // NX, NX, width), axis=1)
    high, low = split(pairs)
    modes = width // NX
    mode_of = iota((width, LANES), 0) // NX
    column = iota((width, LANES), 1)
    total = jnp.zeros((8, LANES), F32)
    for j in range(CHUNK // 8):
        pick = jnp.where(mode_of + j * modes == column, 1.0, 0.0).astype(BF16)
        both = jnp.concatenate([high[8 * j : 8 * j + 8], low[8 * j : 8 * j + 8]], axis=0)
        both = jnp.dot(both.astype(BF16), pick, preferred_element_type=F32)
        total += both[:8] + both[8:]
    return total


def unpack(ref, modes):
    rows = []
    for chunk in range(ref.shape[0]):
        tile = ref[chunk]
        rows += [tile[:, j * modes : (j + 1) * modes] for j in range(CHUNK // 8)]
    return jnp.concatenate(rows, axis=0)


def before_kernel(*refs):
    count = 11
    sources = refs[:count]
    out, states, basis, cells, cosines, cos_lanes = refs[count : count + 6]
    targets = (*refs[count + 6 : 2 * count + 4], states, basis)
    fields, sems = refs[2 * count + 4 :]
    copies = [
        pltpu.make_async_copy(source, target, sems.at[i])
        for i, (source, target) in enumerate(zip(sources, targets))
    ]
    for copy in copies:
        copy.start()
    times, pert_ids, visc, coup, table, pert, ids_ref, speed_ref, force_ref = targets[:-2]
    for copy in copies[:-2]:
        copy.wait()
    chunks = out.shape[0]
    speed = speed_ref[...]
    force = force_ref[...]
    damping = pert[pert_ids[0]]
    ids = ids_ref[...]
    visc_p = visc[NV - 1]
    lane = iota((NX, LANES), 1)
    half_speed = 0.5 * speed
    coef_east = jnp.where(lane == LANES - 1, 0.0, visc_p - half_speed)
    coef_west = jnp.where(lane == 0, 0.0, visc_p + half_speed)
    coef_own = coup[NV - 1, NV - 1] - 4.0 * visc_p - damping
    masks = cycle_masks(ids)
    masks_half = masks.astype(BF16)
    c8 = lane_part()
    row8 = iota((8, LANES), 0)
    quad = iota((NX, LANES), 1) // 4
    for index, field in enumerate((speed, force, damping, ids.astype(F32))):
        cells[index] = field
    scale = 1.0 / math.sqrt(NX * LANES)

    def pieces(column):
        out16 = jnp.zeros((NX, LANES), F32)
        spot = 0
        for field in (speed, force, damping, ids.astype(F32)):
            for piece in split(field):
                moved = roll(piece, spot - column, 1)
                out16 = jnp.where(lane == spot, moved, out16)
                spot += 1
        return jnp.where(iota((8, LANES), 1) < 64, out16[:8], roll(out16[8:], 64, 1))

    params_right = pieces(LANES - 1)
    params_left = pieces(0)

    east_hi, east_lo = split(jnp.where(lane == LANES - 1, visc_p - half_speed, 0.0))
    west_hi, west_lo = split(jnp.where(lane == 0, visc_p + half_speed, 0.0))
    ids_f = ids.astype(F32)
    id_east = jnp.where(lane == LANES - 1, ids_f, 0.0)
    id_west = jnp.where(lane == 0, ids_f, 0.0)
    ones = jnp.ones((NX, LANES), BF16)
    filler = jnp.zeros((LANES - 32, LANES), F32)

    def as_rows(east, west):
        stacked = jnp.concatenate([east, west, filler], axis=0).astype(BF16)
        return lax.dot_general(ones, stacked, NT, preferred_element_type=F32)[:8]

    row_hi = as_rows(east_hi, west_hi)
    row_lo = as_rows(east_lo, west_lo)
    row_id = as_rows(id_east, id_west)
    counts = lax.dot_general(ones, masks_half, NT, preferred_element_type=F32)[:8]
    spread = jnp.where(
        iota((NRING * NX, LANES), 1) == 32 + iota((NRING * NX, LANES), 0) // NX, 1.0, 0.0
    )
    counts = jnp.dot(counts, spread, precision=HIGH, preferred_element_type=F32)
    count_hi, count_lo = split(counts)
    row_hi = row_hi + count_hi
    row_lo = row_lo + count_lo

    size = CHUNK * NX
    same_x = iota((NRING * NX, 3 * size), 0) % NX == iota((NRING * NX, 3 * size), 1) % NX
    snap_of_row = iota((size, LANES), 0) // NX == iota((size, LANES), 1) // 4
    part_of_lane = iota((size, LANES), 1) % 4
    to_start = jnp.where(snap_of_row & (part_of_lane < 2), scale, 0.0)
    to_rate = jnp.where(snap_of_row & (part_of_lane >= 2), scale, 0.0)
    copies[-2].wait()

    def chunk_step(chunk, carry):
        first = chunk * CHUNK

        def snap(k, carried):
            edges, cos_row = carried
            u = [states[first + k, v].astype(F32) for v in range(NV)]
            p = u[NV - 1]
            cosine = table[lax.rem(times[first + k], PERIOD)]
            cosines[pl.ds(first + k, 1), :] = jnp.full((1, LANES), cosine, F32)
            cos_row = jnp.where(quad[:8] == k, cosine, cos_row)
            rate = coef_east * roll(p, -1, 1) + coef_west * roll(p, 1, 1)
            rate = rate + visc_p * north_south(p) + coef_own * p + cosine * force
            for v in range(NV - 1):
                rate = rate + coup[NV - 1, v] * u[v]
            high, low = split(rate)
            at = pl.multiple_of(k * NX, NX)
            fields[pl.ds(at, NX), :] = p.astype(BF16)
            fields[pl.ds(pl.multiple_of(size + at, NX), NX), :] = high.astype(BF16)
            fields[pl.ds(pl.multiple_of(2 * size + at, NX), NX), :] = low.astype(BF16)
            edges = tuple(
                jnp.where(quad == k, roll(u[v], 4 * k + 2, 1), edges[v]) for v in range(NV)
            )
            return edges, cos_row

        carried = tuple(jnp.zeros((NX, LANES), F32) for _ in range(NV)), jnp.zeros((8, LANES), F32)
        if chunks == 1:
            for k in range(CHUNK):
                carried = snap(k, carried)
        else:
            carried = lax.fori_loop(0, CHUNK, snap, carried)
        edges, cos_lanes[chunk] = carried
        sums = lax.dot_general(masks_half, fields[...], NT, preferred_element_type=F32)
        sums = jnp.where(same_x, sums, 0.0)
        by_cycle = jnp.sum(sums.reshape(NRING, NX, 3 * size), axis=1)
        by_cycle = jnp.concatenate([by_cycle, jnp.zeros((3, 3 * size), F32)], axis=0)
        start = by_cycle[:, :size]
        rate = by_cycle[:, size : 2 * size] + by_cycle[:, 2 * size :]
        packed = jnp.dot(start, to_start, precision=HIGH, preferred_element_type=F32)
        packed += jnp.dot(rate, to_rate, precision=HIGH, preferred_element_type=F32)
        high, low = split(packed)
        packed = jnp.where(c8 % 2 == 0, high, low)
        packed = jnp.where(row8 < NRING, packed, 0.0)
        for at, row in ((5, row_hi), (6, row_lo), (7, row_id)):
            packed = jnp.where(row8 == at, row, packed)
        p_low, p_high = edges[NV - 1][:8], edges[NV - 1][8:]
        p_edges = jnp.where(
            (c8 == 1) | (c8 == 2), p_low, jnp.where(c8 == 3, roll(p_high, 1, 1), roll(p_high, -1, 1))
        )
        right = [jnp.where(c8 < 2, t[:8], roll(t[8:], 2, 1)) for t in edges]
        left = [jnp.where(c8 >= 2, t[:8], roll(t[8:], -2, 1)) for t in edges]
        rows = [packed, p_edges, *right, params_right, *left, params_left]
        out[chunk] = jnp.concatenate(rows, axis=0).astype(BF16)
        return carry

    if chunks == 1:
        chunk_step(0, 0)
    else:
        lax.fori_loop(0, chunks, chunk_step, 0)
    copies[-1].wait()


def coords_kernel(states, basis, after, out):
    flat_basis = flat(basis, 0, basis.shape[0])
    if out.shape[0] == 1:
        out[0] = project(flat(states, 0, CHUNK), flat_basis)
        return

    def chunk_step(chunk, carry):
        out[chunk] = project(flat(states, chunk * CHUNK, CHUNK), flat_basis)
        return carry

    lax.fori_loop(0, out.shape[0], chunk_step, 0)


def start_kernel(top, place, first, near, coords, out, edges):
    odd = place[0] % 2 == 1
    for chunk in range(out.shape[0]):
        mine, other = first[chunk].astype(F32), near[chunk].astype(F32)
        low, high = jnp.where(odd, other, mine), jnp.where(odd, mine, other)
        right, left = high[RIGHT], low[LEFT]
        edges[chunk] = jnp.concatenate([right, left], axis=0).astype(BF16)
        payload = jnp.where(goes_right(place[0], top), right, left)
        rows = [payload, *split(coords[chunk]), low[:BLOB], high[:BLOB]]
        out[chunk] = jnp.concatenate(rows, axis=0).astype(BF16)


def goes_right(me, bit):
    if bit == 0:
        return me % 2 == 1
    lower = jnp.bitwise_and(jnp.right_shift(me, 1), (1 << bit) - 1)
    return lower == (1 << bit) - 1


def goes_left(me, bit):
    lower = jnp.bitwise_and(jnp.right_shift(me, 1), (1 << bit) - 1)
    return lower == 0


def next_kernel(bit, place, sent, got, edges, out, new_edges=None):
    me = place[0]
    for chunk in range(out.shape[0]):
        mine, other = sent[chunk].astype(F32), got[chunk].astype(F32)
        both = edges[chunk].astype(F32)
        right = jnp.where(goes_right(me, bit + 1), other[:EDGE], both[:EDGE])
        left = jnp.where(goes_left(me, bit + 1), other[:EDGE], both[EDGE:])
        if new_edges is not None:
            new_edges[chunk] = jnp.concatenate([right, left], axis=0).astype(BF16)
        payload = jnp.where(goes_right(me, bit), right, left)
        total = mine[EDGE : EDGE + COORD] + other[EDGE : EDGE + COORD]
        rows = [payload, *split(total[:8] + total[8:]), mine[EDGE + COORD :], other[EDGE + COORD :]]
        out[chunk] = jnp.concatenate(rows, axis=0).astype(BF16)


def prepare_kernel(visc, coup, kern, gain, cells, after, mixer, east_coef, west_coef):
    half_speed = 0.5 * cells[0]
    lane = iota((NX, LANES), 1)
    for v in range(NV):
        east_coef[v] = jnp.where(lane == LANES - 1, 0.0, visc[v] - half_speed)
        west_coef[v] = jnp.where(lane == 0, 0.0, visc[v] + half_speed)
    deep = NV * NX
    col = iota((NX, 3 * deep), 1)
    col_var, col_x = col % deep // NX, col % NX
    row_x = iota((NX, 3 * deep), 0)
    beside = jnp.abs(row_x - col_x) == 1
    blocks = []
    for v in range(NV):
        weight = jnp.zeros((NX, 3 * deep), F32)
        for other in range(NV):
            value = coup[v, other] - (4.0 * visc[v] if other == v else 0.0)
            weight = jnp.where((col_var == other) & (row_x == col_x), value, weight)
        blocks.append(jnp.where((col_var == v) & beside, visc[v], weight))
    high, low = split(jnp.concatenate(blocks, axis=0))
    col = iota((deep, 3 * deep), 1)
    mixer[...] = jnp.where((col < deep) | (col >= 2 * deep), high, low).astype(BF16)


def local_kernel(
    offset,
    states,
    cells,
    cosines,
    mixer_ref,
    east_coef,
    west_coef,
    after,
    out,
):
    count = out.shape[0]
    deep = NV * NX
    force = cells[1]
    damping = cells[2]
    mixer = mixer_ref[...]

    def linear(u, mixed):
        result = []
        for v in range(NV):
            rate = mixed[NX * v : NX * v + NX] - damping * u[v]
            rate = rate + east_coef[v] * roll(u[v], -1, 1) + west_coef[v] * roll(u[v], 1, 1)
            result.append(rate)
        return result

    def snap(k):
        half = states[offset + k].reshape(deep, LANES)
        u = [states[offset + k, v].astype(F32) for v in range(NV)]
        drive = cosines[pl.ds(offset + k, 1), :] * force
        mixed = jnp.dot(
            mixer[:, : 2 * deep],
            jnp.concatenate([half, half], axis=0),
            preferred_element_type=F32,
        )
        rate = [r + drive for r in linear(u, mixed)]
        stack = jnp.concatenate(rate, axis=0)
        high = stack.astype(BF16)
        low = (stack - high.astype(F32)).astype(BF16)
        mixed = jnp.dot(
            mixer, jnp.concatenate([high, high, low], axis=0), preferred_element_type=F32
        )
        again = linear(rate, mixed)
        for v in range(NV):
            out[k, v] = rate[v] + 0.5 * TIME_STEP * again[v]

    def snaps(step, carry):
        for i in range(8):
            snap(step * 8 + i)
        return carry

    lax.fori_loop(0, count // 8, snaps, 0)


def after_kernel(parts, *refs):
    place, kern, gain, visc, coup, basis, cells, cos_lanes = refs[:8]
    own_ref, near_ref, sent_ref, last_ref = refs[8:12]
    bases = refs[12 : 12 + parts]
    deriv, partial, mixed, raw, cyc0, grooves, ends = refs[12 + parts :]
    chunks = own_ref.shape[0]
    passages = kern.shape[0]
    me = place[0]
    base = me - lax.rem(me, 2)
    bits = passages.bit_length() - 2
    odd = me % 2 == 1
    speed = cells[0]
    damping = cells[2]
    ids = cells[3]
    half_speed = 0.5 * speed
    lane = iota((NX, LANES), 1)
    c16 = lane % 4
    masks = cycle_masks(ids).astype(BF16)
    masks_twice = jnp.concatenate([masks, masks], axis=0)
    scale = 1.0 / math.sqrt(NX * LANES)
    size = CHUNK * NX

    src = iota((LANES, LANES), 0)
    dst = iota((LANES, LANES), 1) // 4 * 4
    mixers = [(src == dst) | (src == dst + 1), (src == dst + 2) | (src == dst + 3)]
    mixers += [src == dst + 2, src == dst + 1, src == dst + 3, src == dst]
    mix = jnp.concatenate([jnp.where(m, 1.0, 0.0).astype(BF16) for m in mixers], axis=1)
    pick_snap = jnp.where(iota((size, LANES), 1) == iota((size, LANES), 0) // NX * 4, 1.0, 0.0)
    pick_snap = pick_snap.astype(BF16)
    wide = 4 * NRING * NX
    same_x = iota((size, wide), 0) % NX == iota((size, wide), 1) % NX

    def flat_basis():
        return flat(basis, 0, basis.shape[0])

    def unpack_right(t):
        return jnp.concatenate([t, roll(t, -2, 1)], axis=0)

    def unpack_left(t):
        return jnp.concatenate([t, roll(t, 2, 1)], axis=0)

    def chunk_step(chunk, carry):
        first = chunk * CHUNK
        head = EDGE + COORD
        half = passages // 2 * BLOB
        raw[:half, :] = sent_ref[chunk, head:, :].astype(F32)
        raw[half:, :] = last_ref[chunk, head:, :].astype(F32)
        summed = sent_ref[chunk, EDGE:head, :].astype(F32)
        summed += last_ref[chunk, EDGE:head, :].astype(F32)
        partial[chunk, :8, :] = summed[:8] + summed[8:]
        mixed[...] = jnp.dot(raw[...].astype(BF16), mix, preferred_element_type=F32)

        def slot(offset):
            other = lax.rem(me + offset + passages, passages)
            flips = jnp.bitwise_xor(base, other)
            index = jnp.bitwise_and(flips, 1)
            for bit in range(bits):
                moved = jnp.bitwise_and(jnp.right_shift(flips, bit + 1), 1)
                index = index + jnp.left_shift(moved, bits - bit)
            return pl.multiple_of(index * BLOB, BLOB)

        def load(offset, carry):
            cyc0[pl.ds(pl.multiple_of(offset * 8, 8), 8), :] = mixed[pl.ds(slot(offset), 8), :LANES]
            return carry

        lax.fori_loop(0, passages, load, 0, unroll=passages <= 16)

        def plenum0(offset):
            total = jnp.zeros((8, LANES), F32)
            if passages <= 16 and isinstance(offset, int):
                for other in range(passages):
                    total += kern[(offset - other) % passages] * cyc0[other * 8 : other * 8 + 8, :]
                return total

            def add(other, total):
                weight = kern[lax.rem(offset - other + 2 * passages, passages)]
                return total + weight * cyc0[pl.ds(pl.multiple_of(other * 8, 8), 8), :]

            return lax.fori_loop(0, passages, add, total)

        row8 = iota((8, LANES), 0)
        lane8 = iota((8, LANES), 1)

        def second(offset, total):
            own = slot(offset)
            east, west = slot(offset + 1), slot(offset - 1)
            coefs = raw[pl.ds(own, 8), :]
            id_row = coefs[7:8, :].astype(jnp.int32)
            hit = (id_row == row8) & (lane8 < 32)
            left = jnp.concatenate(
                [jnp.where(hit, coefs[5:6, :], 0.0), jnp.where(hit, coefs[6:7, :], 0.0)], axis=0
            )
            right = jnp.concatenate(
                [
                    mixed[pl.ds(pl.multiple_of(east + 8, 8), 8), 2 * LANES : 3 * LANES],
                    mixed[pl.ds(pl.multiple_of(east + 8, 8), 8), 4 * LANES : 5 * LANES],
                    mixed[pl.ds(pl.multiple_of(west + 8, 8), 8), 3 * LANES : 4 * LANES],
                    mixed[pl.ds(pl.multiple_of(west + 8, 8), 8), 5 * LANES :],
                    jnp.zeros((LANES - 32, LANES), F32),
                ],
                axis=0,
            )
            edge = jnp.dot(left.astype(BF16), right.astype(BF16), preferred_element_type=F32)
            edge = (edge[:8] + edge[8:]) * scale
            count = jnp.where(lane8 == 32 + row8, coefs[5:6, :] + coefs[6:7, :], 0.0)
            count = jnp.sum(count, axis=1, keepdims=True) * (scale * gain[NV - 1])
            rate = mixed[pl.ds(own, 8), LANES : 2 * LANES] + edge + count * plenum0(offset)
            if isinstance(offset, int):
                start = cyc0[offset * 8 : offset * 8 + 8, :]
                weight = kern[-offset % passages]
            else:
                start = cyc0[pl.ds(pl.multiple_of(offset * 8, 8), 8), :]
                weight = kern[lax.rem(passages - offset, passages)]
            return total + weight * (start + TIME_STEP * rate)

        total = jnp.zeros((8, LANES), F32)
        if passages <= 16:
            for offset in range(passages):
                total = second(offset, total)
        else:
            total = lax.fori_loop(0, passages, second, total)
        own0, own1 = plenum0(0), total
        west0, east0 = plenum0(passages - 1), plenum0(1)

        stack = []
        for tile in (own0, own1):
            for piece in split(tile):
                stack += [jnp.broadcast_to(piece[g : g + 1], (NX, LANES)) for g in range(NRING)]
        stack = jnp.concatenate(stack, axis=0).astype(BF16)
        picked = lax.dot_general(pick_snap, stack, NT, preferred_element_type=F32)
        picked = jnp.where(same_x, picked, 0.0).astype(BF16)
        for stage in range(2):
            grooves[stage] = jnp.dot(
                picked[:, stage * wide // 2 : (stage + 1) * wide // 2],
                masks_twice,
                preferred_element_type=F32,
            )

        near = near_ref[chunk].astype(F32)
        own = own_ref[chunk].astype(F32)
        far = last_ref[chunk, :EDGE, :].astype(F32)
        west = jnp.where(odd, near[RIGHT], far)
        east = jnp.where(odd, far, near[LEFT])

        def param(side, index):
            t = side[40:48]
            low = t[:, index : index + 1] + t[:, index + 1 : index + 2]
            high = t[:, 64 + index : 65 + index] + t[:, 65 + index : 66 + index]
            return jnp.broadcast_to(jnp.concatenate([low, high], axis=0), (NX, LANES))

        speed_h, force_h, damp_h, ids_h = (
            jnp.where(c16 < 2, param(west, 2 * i), param(east, 2 * i)) for i in range(4)
        )
        groove_h = jnp.zeros((NX, LANES), F32)
        for g in range(NRING):
            value = jnp.where(c16 < 2, west0[g : g + 1], east0[g : g + 1])
            groove_h = jnp.where(ids_h == g, value, groove_h)
        cos_h = jnp.concatenate([cos_lanes[chunk]] * 2, axis=0)
        halo, ours, rates = [], [], []
        for v in range(NV):
            at = slice(8 * v, 8 * v + 8)
            halo.append(jnp.where(c16 < 2, unpack_right(west[at]), unpack_left(east[at])))
            ours.append(
                jnp.where(c16 < 2, unpack_right(own[RIGHT][at]), unpack_left(own[LEFT][at]))
            )
        for v in range(NV):
            h = halo[v]
            e = roll(jnp.where(c16 == 3, h, ours[v]), -1, 1)
            w = roll(jnp.where(c16 == 0, h, ours[v]), 1, 1)
            rate = visc[v] * (e + w + north_south(h) - 4.0 * h) - 0.5 * speed_h * (e - w)
            rate = rate - damp_h * h + gain[v] * groove_h + force_h * cos_h
            for other in range(NV):
                rate = rate + coup[v, other] * halo[other]
            rates.append(rate)

        def columns(field):
            tiles = [
                jnp.broadcast_to(field[:, c : c + 1], (NX, LANES))
                for c in (LANES - 2, LANES - 1, 0, 1)
            ]
            return jnp.where(
                c16 < 2,
                jnp.where(c16 == 0, tiles[0], tiles[1]),
                jnp.where(c16 == 2, tiles[2], tiles[3]),
            )

        def across(t):
            return jnp.where(c16 == 2, roll(t, 1, 1), roll(t, -1, 1))

        inner = (c16 == 1) | (c16 == 2)
        signed_speed = columns(half_speed) * jnp.where(c16 < 2, -1.0, 1.0)
        damp_e = columns(damping)
        half_step = 0.5 * TIME_STEP
        shifts = [
            jnp.where(inner, (visc[v] + signed_speed) * across(halo[v]), 0.0) for v in range(NV)
        ]
        for v in range(NV):
            change = shifts[v]
            rate = visc[v] * (north_south(change) - 4.0 * change) - damp_e * change
            for other in range(NV):
                rate = rate + coup[v, other] * shifts[other]
            rate = rate + (visc[v] + signed_speed) * across(rates[v])
            beside = jnp.where(c16 == 0, roll(change, -1, 1), roll(change, 1, 1))
            outer = (visc[v] + signed_speed) * beside
            ends[v] = jnp.where(inner, change + half_step * rate, half_step * outer)

        at_ends = (lane < 2) | (lane >= LANES - 2)
        damp_step = half_step * damping
        speed_step = half_step * half_speed
        diffuse = [half_step * visc[v] * gain[v] for v in range(NV)]
        couple = []
        for v in range(NV):
            total = coup[v, 0] * gain[0]
            for other in range(1, NV):
                total = total + coup[v, other] * gain[other]
            couple.append(half_step * total)

        def snap(k, share, index):
            at = pl.ds(pl.multiple_of(k * NX, NX), NX)
            m0, m1 = grooves[0, at, :], grooves[1, at, :]
            e = jnp.where(lane == LANES - 1, 0.0, roll(m0, -1, 1))
            w = jnp.where(lane == 0, 0.0, roll(m0, 1, 1))
            spread = 2 * LANES - 4 * k - 2
            lap = e + w + north_south(m0) - 4.0 * m0
            own = 0.5 * (m0 + m1) - speed_step * (e - w) - damp_step * m0
            for v in range(NV):
                total = share[index, v] + gain[v] * own + diffuse[v] * lap + couple[v] * m0
                total = total + jnp.where(at_ends, roll(ends[v], spread, 1), 0.0)
                deriv[first + k, v] = total.astype(BF16)

        done = 0
        for share in bases:
            count = share.shape[0] if chunks == 1 else CHUNK

            def snaps(step, carry, share=share, done=done):
                for i in range(count):
                    k = step * count + i
                    snap(done + k, share, k if chunks == 1 else first + k)
                return carry

            lax.fori_loop(0, count // count, snaps, 0)
            done += count
        partial[chunk, 8:, :] = project(flat(deriv, first, CHUNK), flat_basis())
        return carry

    if chunks == 1:
        chunk_step(0, 0)
    else:
        lax.fori_loop(0, chunks, chunk_step, 0)


def eliminate(system, columns):
    row = iota(system.shape, 0)
    for j in columns:
        pivot = system[j : j + 1, :] / system[j : j + 1, j : j + 1]
        factor = jnp.where(row == j, 0.0, jnp.broadcast_to(system[:, j : j + 1], system.shape))
        system = jnp.where(row == j, pivot, system - factor * pivot)
    return system


highest = functools.partial(lax.dot_general, precision=HIGH, preferred_element_type=F32)
NN = (((1,), (0,)), ((), ()))


def system_kernel(ridge, modes, coords_ref, deriv, kernel_ref, system_ref, deriv_out, sem):
    write = pltpu.make_async_copy(deriv, deriv_out, sem)
    write.start()
    coords = unpack(coords_ref, modes)
    snaps = coords.shape[0]
    gram = highest(coords, coords, NT)
    squares = coords * coords
    kernel = gram + 0.5 * (gram * gram + highest(squares, squares, NT))
    kernel_ref[...] = kernel
    same = iota((snaps, snaps), 0) == iota((snaps, snaps), 1)
    eye = jnp.where(same, 1.0, 0.0)
    system = jnp.concatenate([kernel + ridge * eye, eye], axis=1)
    system_ref[...] = eliminate(system, range(snaps // 4))
    write.wait()


def invert_kernel(system_ref, out_ref):
    snaps = system_ref.shape[0]
    out_ref[...] = eliminate(system_ref[...], range(snaps // 4, snaps * 5 // 8))


def weight_kernel(
    coords_ref, kernel_ref, system_ref, first_ref, second_ref, lin_ref, weights, fit
):
    snaps = kernel_ref.shape[0]
    inverse = eliminate(system_ref[...], range(snaps * 5 // 8, snaps))[:, snaps:]
    coords = unpack(coords_ref, first_ref.shape[0])
    design = highest(coords, first_ref[...], NN)
    design = design * (highest(coords, second_ref[...], NN) + lin_ref[...])
    weights[...] = highest(inverse, design, NN)
    fit[...] = highest(kernel_ref[...], inverse, NN)


def fit_kernel(
    place, rates_ref, coords_ref, weights, fit, reduced, operator, fitted, full, red
):
    modes = operator.shape[0]
    rates = unpack(rates_ref, modes)
    operator[...] = highest(rates, weights[...], (((0,), (0,)), ((), ())))
    full[...] = highest(fit[...], rates, NN)
    red[...] = jnp.concatenate([unpack(coords_ref, modes), rates], axis=1)
    each = fitted.shape[0]
    for i in range(each):
        at = pl.ds(place[0] * each + i, 1)
        fitted[i : i + 1, :] = full[at, :]
        reduced[i : i + 1, :] = red[at, :]


def body(
    states,
    basis,
    snapshot_times,
    pert_ids,
    pert_table,
    cycle_ids,
    groove_kernel,
    groove_gain,
    speed,
    force_amp,
    viscosity,
    coupling,
):
    snaps = states.shape[0]
    modes = basis.shape[0]
    chunks = snaps // CHUNK
    passages = lax.axis_size("passage")
    rounds = passages.bit_length() - 1
    position = lax.axis_index("passage")
    place = position.reshape(1).astype(jnp.int32)
    angles = 2.0 * math.pi * np.arange(PERIOD) / PERIOD
    table = jnp.asarray(np.cos(angles).astype(np.float32))

    def swap(value, mask):
        pairs = [(i, i ^ mask) for i in range(passages)]
        return lax.ppermute(value, "passage", pairs)

    def swap_chip(value, mask):
        return swap(value, mask + 1)

    operands = (
        snapshot_times,
        pert_ids,
        viscosity,
        coupling,
        table,
        pert_table,
        cycle_ids,
        speed,
        force_amp,
        states,
        basis,
    )
    first, held, held_basis, cells, cosines, cos_lanes = pl.pallas_call(
        before_kernel,
        out_shape=(
            jax.ShapeDtypeStruct((chunks, ROWS, LANES), BF16),
            jax.ShapeDtypeStruct(states.shape, BF16),
            jax.ShapeDtypeStruct(basis.shape, BF16),
            jax.ShapeDtypeStruct((4, NX, LANES), F32),
            jax.ShapeDtypeStruct((snaps, LANES), F32),
            jax.ShapeDtypeStruct((chunks, 8, LANES), F32),
        ),
        in_specs=[HBM] * len(operands),
        out_specs=(VMEM,) * 6,
        scratch_shapes=[pltpu.SMEM(x.shape, x.dtype) for x in operands[:5]]
        + [pltpu.VMEM(x.shape, x.dtype) for x in operands[5:9]]
        + [
            pltpu.VMEM((3 * CHUNK * NX, LANES), BF16),
            pltpu.SemaphoreType.DMA((len(operands),)),
        ],
        compiler_params=pltpu.CompilerParams(vmem_limit_bytes=24 * 2**20),
        name="before",
    )(*(x if x is pert_ids else pltpu.with_memory_space_constraint(x, pltpu.HBM) for x in operands))
    near = swap(first, 1)
    bits = rounds - 1
    edges_shape = jax.ShapeDtypeStruct((chunks, 2 * EDGE, LANES), BF16)
    head = EDGE + COORD

    def glue(kernel, name, rows, *args, more=True):
        outs = (jax.ShapeDtypeStruct((chunks, rows, LANES), BF16), edges_shape)
        return pl.pallas_call(
            kernel,
            out_shape=outs if more else outs[:1],
            in_specs=[SMEM] + [VMEM] * len(args),
            out_specs=(VMEM, VMEM) if more else (VMEM,),
            compiler_params=pltpu.CompilerParams(vmem_limit_bytes=16 * 2**20),
            name=name,
        )(place, *args)

    hidden = pl.CostEstimate(flops=2 * 10**9, bytes_accessed=2**20, transcendentals=0)
    anywhere = pl.BlockSpec(memory_space=pl.ANY)
    tile = jax.ShapeDtypeStruct((chunks, 8, LANES), F32)
    coords = pl.pallas_call(
        coords_kernel,
        out_shape=tile,
        in_specs=[VMEM, VMEM, anywhere],
        out_specs=VMEM,
        cost_estimate=hidden,
        compiler_params=pltpu.CompilerParams(vmem_limit_bytes=24 * 2**20),
        name="coords",
    )(held, held_basis, first)
    near, coords = lax.optimization_barrier((near, coords))

    def local(offset, count, after):
        return pl.pallas_call(
            functools.partial(local_kernel, offset),
            out_shape=jax.ShapeDtypeStruct((count,) + states.shape[1:], F32),
            in_specs=[VMEM] * 6 + [anywhere],
            out_specs=VMEM,
            cost_estimate=hidden,
            compiler_params=pltpu.CompilerParams(vmem_limit_bytes=24 * 2**20),
            name="local",
        )(
            held,
            cells,
            cosines,
            mixer,
            east_coef,
            west_coef,
            after,
        )

    start = functools.partial(start_kernel, bits - 1)
    message, edges = glue(start, "start", head + 2 * BLOB, first, near, coords)
    mixer, east_coef, west_coef = pl.pallas_call(
        prepare_kernel,
        out_shape=(
            jax.ShapeDtypeStruct((NV * NX, 3 * NV * NX), BF16),
            jax.ShapeDtypeStruct((NV, NX, LANES), F32),
            jax.ShapeDtypeStruct((NV, NX, LANES), F32),
        ),
        in_specs=[SMEM] * 4 + [VMEM, anywhere],
        out_specs=(VMEM, VMEM, VMEM),
        cost_estimate=hidden,
        compiler_params=pltpu.CompilerParams(vmem_limit_bytes=16 * 2**20),
        name="prepare",
    )(viscosity, coupling, groove_kernel, groove_gain, cells, message)
    shares = [8, 8, 16] if chunks == 1 and bits == 3 else [snaps]
    bases, offset = [], 0
    for bit in range(bits - 1, -1, -1):
        got = swap_chip(message, 2 << bit)
        if shares:
            count = shares.pop(0)
            base = local(offset, count, message)
            got, base = lax.optimization_barrier((got, base))
            bases.append(base)
            offset += count
        if bit:
            rows = 2 * message.shape[1] - head
            step = functools.partial(next_kernel, bit - 1)
            message, *edges = glue(step, "next", rows, message, got, edges, more=bit > 1)
            edges = edges[0] if edges else None

    derivative, partial = pl.pallas_call(
        functools.partial(after_kernel, len(bases)),
        out_shape=(
            jax.ShapeDtypeStruct(states.shape, BF16),
            jax.ShapeDtypeStruct((chunks, 16, LANES), F32),
        ),
        in_specs=[SMEM] * 5 + [VMEM] * (7 + len(bases)),
        out_specs=(VMEM, VMEM),
        scratch_shapes=[
            pltpu.VMEM((passages * BLOB, 6 * LANES), F32),
            pltpu.VMEM((passages * BLOB, LANES), F32),
            pltpu.VMEM((passages * 8, LANES), F32),
            pltpu.VMEM((2, CHUNK * NX, LANES), F32),
            pltpu.VMEM((NV, NX, LANES), F32),
        ],
        compiler_params=pltpu.CompilerParams(vmem_limit_bytes=32 * 2**20),
        name="after",
    )(
        place,
        groove_kernel,
        groove_gain,
        viscosity,
        coupling,
        held_basis,
        cells,
        cos_lanes,
        first,
        near,
        message,
        got,
        *bases,
    )

    upper_first, upper_second = np.triu_indices(modes)
    features = modes + len(upper_first)
    pick_first = np.zeros((modes, features), np.float32)
    pick_second = np.zeros((modes, features), np.float32)
    linear = np.zeros((1, features), np.float32)
    pick_first[np.arange(modes), np.arange(modes)] = 1.0
    linear[0, :modes] = 1.0
    pick_first[upper_first, modes + np.arange(len(upper_first))] = 1.0
    pick_second[upper_second, modes + np.arange(len(upper_first))] = 1.0

    def small(kernel, name, outs, *args):
        return pl.pallas_call(
            kernel,
            out_shape=tuple(jax.ShapeDtypeStruct(shape, F32) for shape in outs),
            in_specs=[VMEM] * len(args),
            out_specs=tuple(VMEM for _ in outs),
            cost_estimate=hidden,
            compiler_params=pltpu.CompilerParams(vmem_limit_bytes=16 * 2**20),
            name=name,
        )(*args)

    total = partial + swap(partial, 1)
    coords, total, derivative = lax.optimization_barrier((total[:, :8], total[:, 8:], derivative))
    kernel, system, derivative = pl.pallas_call(
        functools.partial(system_kernel, RIDGE_FACTOR * snaps, modes),
        out_shape=(
            jax.ShapeDtypeStruct((snaps, snaps), F32),
            jax.ShapeDtypeStruct((snaps, 2 * snaps), F32),
            jax.ShapeDtypeStruct(states.shape, BF16),
        ),
        in_specs=[VMEM, VMEM],
        out_specs=(VMEM, VMEM, HBM),
        scratch_shapes=[pltpu.SemaphoreType.DMA],
        cost_estimate=hidden,
        compiler_params=pltpu.CompilerParams(vmem_limit_bytes=16 * 2**20),
        name="system",
    )(coords, derivative)
    for r in range(1, rounds):
        got = swap_chip(total, 1 << r)
        if r == 1:
            got, kernel, system = lax.optimization_barrier((got, kernel, system))
            total = total + got
            (inverse,) = small(invert_kernel, "invert", [(snaps, 2 * snaps)], system)
        elif r == 2:
            total, inverse = lax.optimization_barrier((total + got, inverse))
            weights, fit = small(
                weight_kernel,
                "weights",
                [(snaps, features), (snaps, snaps)],
                coords,
                kernel,
                inverse,
                jnp.asarray(pick_first),
                jnp.asarray(pick_second),
                jnp.asarray(linear),
            )
        else:
            total = total + got
    each = snaps // passages
    reduced, operator, fitted = pl.pallas_call(
        fit_kernel,
        out_shape=(
            jax.ShapeDtypeStruct((each, 2 * modes), F32),
            jax.ShapeDtypeStruct((modes, features), F32),
            jax.ShapeDtypeStruct((each, modes), F32),
        ),
        in_specs=[SMEM] + [VMEM] * 4,
        out_specs=(VMEM, VMEM, VMEM),
        scratch_shapes=[pltpu.VMEM((snaps, modes), F32), pltpu.VMEM((snaps, 2 * modes), F32)],
        compiler_params=pltpu.CompilerParams(vmem_limit_bytes=16 * 2**20),
        name="fit",
    )(place, total, coords, weights, fit)
    return derivative, reduced, operator.T, fitted


def solution(mesh):
    in_specs = (
        P("member", None, None, "passage"),
        P(None, None, None, "passage"),
        P("member"),
        P(("member", "passage")),
        P(),
        P(None, "passage"),
        P(),
        P(),
        P(None, "passage"),
        P(None, "passage"),
        P(),
        P(),
    )
    out_specs = (
        P("member", None, None, "passage"),
        P(("member", "passage"), None),
        P("member", None),
        P(("member", "passage"), None),
    )
    return jax.shard_map(body, mesh=mesh, in_specs=in_specs, out_specs=out_specs, check_vma=False)
```

```python
import functools
import math

import jax
import jax.numpy as jnp
import numpy as np
from jax import lax
from jax.experimental import pallas as pl
from jax.experimental.pallas import tpu as pltpu
from jax.sharding import PartitionSpec as P

F32 = jnp.float32
BF16 = jnp.bfloat16
NRING = 5
NV = 5
NX = 16
LANES = 128
PERIOD = 37
TIME_STEP = 0.2
RIDGE_FACTOR = 1.0
UNROLL = 4
CHUNK = 32
BLOB = 16
COORD = 16
EDGE = 48
ROWS = BLOB + 2 * EDGE
RIGHT = slice(BLOB, BLOB + EDGE)
LEFT = slice(BLOB + EDGE, ROWS)

HIGH = lax.Precision.HIGHEST
NT = (((1,), (1,)), ((), ()))
VMEM = pl.BlockSpec(memory_space=pltpu.VMEM)
HBM = pl.BlockSpec(memory_space=pltpu.HBM)
SMEM = pl.BlockSpec(memory_space=pltpu.SMEM)


def iota(shape, axis):
    return lax.broadcasted_iota(jnp.int32, shape, axis)


def roll(value, shift, axis):
    size = value.shape[axis]
    return pltpu.roll(value, shift % size if isinstance(shift, int) else shift, axis)


def split(value):
    high = value.astype(BF16).astype(F32)
    return high, (value - high).astype(BF16).astype(F32)


def north_south(u):
    row = iota(u.shape, 0)
    north = jnp.where(row == NX - 1, 0.0, roll(u, -1, 0))
    south = jnp.where(row == 0, 0.0, roll(u, 1, 0))
    return north + south


def cycle_masks(ids):
    return jnp.concatenate([jnp.where(ids == g, 1.0, 0.0) for g in range(NRING)], axis=0)


def lane_part():
    return iota((8, LANES), 1) % 4


def flat(ref, first, count):
    parts = [ref[pl.ds(first, count), v].reshape(count * NX, LANES) for v in range(NV)]
    return jnp.concatenate(parts, axis=1)


def project(rows, modes_flat):
    width = modes_flat.shape[0]
    size = rows.shape[0]
    pairs = lax.dot_general(rows, modes_flat, NT, preferred_element_type=F32)
    diagonal = iota((size, width), 0) % NX == iota((size, width), 1) % NX
    pairs = jnp.where(diagonal, pairs, 0.0)
    pairs = jnp.sum(pairs.reshape(size // NX, NX, width), axis=1)
    high, low = split(pairs)
    modes = width // NX
    mode_of = iota((width, LANES), 0) // NX
    column = iota((width, LANES), 1)
    total = jnp.zeros((8, LANES), F32)
    for j in range(CHUNK // 8):
        pick = jnp.where(mode_of + j * modes == column, 1.0, 0.0).astype(BF16)
        both = jnp.concatenate([high[8 * j : 8 * j + 8], low[8 * j : 8 * j + 8]], axis=0)
        both = jnp.dot(both.astype(BF16), pick, preferred_element_type=F32)
        total += both[:8] + both[8:]
    return total


def unpack(ref, modes):
    rows = []
    for chunk in range(ref.shape[0]):
        tile = ref[chunk]
        rows += [tile[:, j * modes : (j + 1) * modes] for j in range(CHUNK // 8)]
    return jnp.concatenate(rows, axis=0)


def before_kernel(*refs):
    count = 11
    sources = refs[:count]
    out, states, basis, cells, cosines, cos_lanes = refs[count : count + 6]
    targets = (*refs[count + 6 : 2 * count + 4], states, basis)
    fields, sems = refs[2 * count + 4 :]
    copies = [
        pltpu.make_async_copy(source, target, sems.at[i])
        for i, (source, target) in enumerate(zip(sources, targets))
    ]
    for copy in copies:
        copy.start()
    times, pert_ids, visc, coup, table, pert, ids_ref, speed_ref, force_ref = targets[:-2]
    for copy in copies[:-2]:
        copy.wait()
    chunks = out.shape[0]
    speed = speed_ref[...]
    force = force_ref[...]
    damping = pert[pert_ids[0]]
    ids = ids_ref[...]
    visc_p = visc[NV - 1]
    lane = iota((NX, LANES), 1)
    half_speed = 0.5 * speed
    coef_east = jnp.where(lane == LANES - 1, 0.0, visc_p - half_speed)
    coef_west = jnp.where(lane == 0, 0.0, visc_p + half_speed)
    coef_own = coup[NV - 1, NV - 1] - 4.0 * visc_p - damping
    masks = cycle_masks(ids)
    masks_half = masks.astype(BF16)
    c8 = lane_part()
    row8 = iota((8, LANES), 0)
    quad = iota((NX, LANES), 1) // 4
    for index, field in enumerate((speed, force, damping, ids.astype(F32))):
        cells[index] = field
    scale = 1.0 / math.sqrt(NX * LANES)

    def pieces(column):
        out16 = jnp.zeros((NX, LANES), F32)
        spot = 0
        for field in (speed, force, damping, ids.astype(F32)):
            for piece in split(field):
                moved = roll(piece, spot - column, 1)
                out16 = jnp.where(lane == spot, moved, out16)
                spot += 1
        return jnp.where(iota((8, LANES), 1) < 64, out16[:8], roll(out16[8:], 64, 1))

    params_right = pieces(LANES - 1)
    params_left = pieces(0)

    east_hi, east_lo = split(jnp.where(lane == LANES - 1, visc_p - half_speed, 0.0))
    west_hi, west_lo = split(jnp.where(lane == 0, visc_p + half_speed, 0.0))
    ids_f = ids.astype(F32)
    id_east = jnp.where(lane == LANES - 1, ids_f, 0.0)
    id_west = jnp.where(lane == 0, ids_f, 0.0)
    ones = jnp.ones((NX, LANES), BF16)
    filler = jnp.zeros((LANES - 32, LANES), F32)

    def as_rows(east, west):
        stacked = jnp.concatenate([east, west, filler], axis=0).astype(BF16)
        return lax.dot_general(ones, stacked, NT, preferred_element_type=F32)[:8]

    row_hi = as_rows(east_hi, west_hi)
    row_lo = as_rows(east_lo, west_lo)
    row_id = as_rows(id_east, id_west)
    counts = lax.dot_general(ones, masks_half, NT, preferred_element_type=F32)[:8]
    spread = jnp.where(
        iota((NRING * NX, LANES), 1) == 32 + iota((NRING * NX, LANES), 0) // NX, 1.0, 0.0
    )
    counts = jnp.dot(counts, spread, precision=HIGH, preferred_element_type=F32)
    count_hi, count_lo = split(counts)
    row_hi = row_hi + count_hi
    row_lo = row_lo + count_lo

    size = CHUNK * NX
    same_x = iota((NRING * NX, 3 * size), 0) % NX == iota((NRING * NX, 3 * size), 1) % NX
    snap_of_row = iota((size, LANES), 0) // NX == iota((size, LANES), 1) // 4
    part_of_lane = iota((size, LANES), 1) % 4
    to_start = jnp.where(snap_of_row & (part_of_lane < 2), scale, 0.0)
    to_rate = jnp.where(snap_of_row & (part_of_lane >= 2), scale, 0.0)
    copies[-2].wait()

    def chunk_step(chunk, carry):
        first = chunk * CHUNK

        def snap(k, carried):
            edges, cos_row = carried
            u = [states[first + k, v].astype(F32) for v in range(NV)]
            p = u[NV - 1]
            cosine = table[lax.rem(times[first + k], PERIOD)]
            cosines[pl.ds(first + k, 1), :] = jnp.full((1, LANES), cosine, F32)
            cos_row = jnp.where(quad[:8] == k, cosine, cos_row)
            rate = coef_east * roll(p, -1, 1) + coef_west * roll(p, 1, 1)
            rate = rate + visc_p * north_south(p) + coef_own * p + cosine * force
            for v in range(NV - 1):
                rate = rate + coup[NV - 1, v] * u[v]
            high, low = split(rate)
            at = pl.multiple_of(k * NX, NX)
            fields[pl.ds(at, NX), :] = p.astype(BF16)
            fields[pl.ds(pl.multiple_of(size + at, NX), NX), :] = high.astype(BF16)
            fields[pl.ds(pl.multiple_of(2 * size + at, NX), NX), :] = low.astype(BF16)
            edges = tuple(
                jnp.where(quad == k, roll(u[v], 4 * k + 2, 1), edges[v]) for v in range(NV)
            )
            return edges, cos_row

        carried = tuple(jnp.zeros((NX, LANES), F32) for _ in range(NV)), jnp.zeros((8, LANES), F32)
        if chunks == 1:
            for k in range(CHUNK):
                carried = snap(k, carried)
        else:
            carried = lax.fori_loop(0, CHUNK, snap, carried)
        edges, cos_lanes[chunk] = carried
        sums = lax.dot_general(masks_half, fields[...], NT, preferred_element_type=F32)
        sums = jnp.where(same_x, sums, 0.0)
        by_cycle = jnp.sum(sums.reshape(NRING, NX, 3 * size), axis=1)
        by_cycle = jnp.concatenate([by_cycle, jnp.zeros((3, 3 * size), F32)], axis=0)
        start = by_cycle[:, :size]
        rate = by_cycle[:, size : 2 * size] + by_cycle[:, 2 * size :]
        packed = jnp.dot(start, to_start, precision=HIGH, preferred_element_type=F32)
        packed += jnp.dot(rate, to_rate, precision=HIGH, preferred_element_type=F32)
        high, low = split(packed)
        packed = jnp.where(c8 % 2 == 0, high, low)
        packed = jnp.where(row8 < NRING, packed, 0.0)
        for at, row in ((5, row_hi), (6, row_lo), (7, row_id)):
            packed = jnp.where(row8 == at, row, packed)
        p_low, p_high = edges[NV - 1][:8], edges[NV - 1][8:]
        p_edges = jnp.where(
            (c8 == 1) | (c8 == 2), p_low, jnp.where(c8 == 3, roll(p_high, 1, 1), roll(p_high, -1, 1))
        )
        right = [jnp.where(c8 < 2, t[:8], roll(t[8:], 2, 1)) for t in edges]
        left = [jnp.where(c8 >= 2, t[:8], roll(t[8:], -2, 1)) for t in edges]
        rows = [packed, p_edges, *right, params_right, *left, params_left]
        out[chunk] = jnp.concatenate(rows, axis=0).astype(BF16)
        return carry

    if chunks == 1:
        chunk_step(0, 0)
    else:
        lax.fori_loop(0, chunks, chunk_step, 0)
    copies[-1].wait()


def coords_kernel(states, basis, after, out):
    flat_basis = flat(basis, 0, basis.shape[0])
    if out.shape[0] == 1:
        out[0] = project(flat(states, 0, CHUNK), flat_basis)
        return

    def chunk_step(chunk, carry):
        out[chunk] = project(flat(states, chunk * CHUNK, CHUNK), flat_basis)
        return carry

    lax.fori_loop(0, out.shape[0], chunk_step, 0)


def start_kernel(top, place, first, near, coords, out, edges):
    odd = place[0] % 2 == 1
    for chunk in range(out.shape[0]):
        mine, other = first[chunk].astype(F32), near[chunk].astype(F32)
        low, high = jnp.where(odd, other, mine), jnp.where(odd, mine, other)
        right, left = high[RIGHT], low[LEFT]
        edges[chunk] = jnp.concatenate([right, left], axis=0).astype(BF16)
        payload = jnp.where(goes_right(place[0], top), right, left)
        rows = [payload, *split(coords[chunk]), low[:BLOB], high[:BLOB]]
        out[chunk] = jnp.concatenate(rows, axis=0).astype(BF16)


def goes_right(me, bit):
    if bit == 0:
        return me % 2 == 1
    lower = jnp.bitwise_and(jnp.right_shift(me, 1), (1 << bit) - 1)
    return lower == (1 << bit) - 1


def goes_left(me, bit):
    lower = jnp.bitwise_and(jnp.right_shift(me, 1), (1 << bit) - 1)
    return lower == 0


def next_kernel(bit, place, sent, got, edges, out, new_edges=None):
    me = place[0]
    for chunk in range(out.shape[0]):
        mine, other = sent[chunk].astype(F32), got[chunk].astype(F32)
        both = edges[chunk].astype(F32)
        right = jnp.where(goes_right(me, bit + 1), other[:EDGE], both[:EDGE])
        left = jnp.where(goes_left(me, bit + 1), other[:EDGE], both[EDGE:])
        if new_edges is not None:
            new_edges[chunk] = jnp.concatenate([right, left], axis=0).astype(BF16)
        payload = jnp.where(goes_right(me, bit), right, left)
        total = mine[EDGE : EDGE + COORD] + other[EDGE : EDGE + COORD]
        rows = [payload, *split(total[:8] + total[8:]), mine[EDGE + COORD :], other[EDGE + COORD :]]
        out[chunk] = jnp.concatenate(rows, axis=0).astype(BF16)


def prepare_kernel(visc, coup, kern, gain, cells, after, mixer, east_coef, west_coef):
    half_speed = 0.5 * cells[0]
    lane = iota((NX, LANES), 1)
    for v in range(NV):
        east_coef[v] = jnp.where(lane == LANES - 1, 0.0, visc[v] - half_speed)
        west_coef[v] = jnp.where(lane == 0, 0.0, visc[v] + half_speed)
    deep = NV * NX
    col = iota((NX, 3 * deep), 1)
    col_var, col_x = col % deep // NX, col % NX
    row_x = iota((NX, 3 * deep), 0)
    beside = jnp.abs(row_x - col_x) == 1
    blocks = []
    for v in range(NV):
        weight = jnp.zeros((NX, 3 * deep), F32)
        for other in range(NV):
            value = coup[v, other] - (4.0 * visc[v] if other == v else 0.0)
            weight = jnp.where((col_var == other) & (row_x == col_x), value, weight)
        blocks.append(jnp.where((col_var == v) & beside, visc[v], weight))
    high, low = split(jnp.concatenate(blocks, axis=0))
    col = iota((deep, 3 * deep), 1)
    mixer[...] = jnp.where((col < deep) | (col >= 2 * deep), high, low).astype(BF16)


def local_kernel(
    offset,
    states,
    cells,
    cosines,
    mixer_ref,
    east_coef,
    west_coef,
    after,
    out,
):
    count = out.shape[0]
    deep = NV * NX
    force = cells[1]
    damping = cells[2]
    mixer = mixer_ref[...]

    def linear(u, mixed):
        result = []
        for v in range(NV):
            rate = mixed[NX * v : NX * v + NX] - damping * u[v]
            rate = rate + east_coef[v] * roll(u[v], -1, 1) + west_coef[v] * roll(u[v], 1, 1)
            result.append(rate)
        return result

    def snap(k):
        half = states[offset + k].reshape(deep, LANES)
        u = [states[offset + k, v].astype(F32) for v in range(NV)]
        drive = cosines[pl.ds(offset + k, 1), :] * force
        mixed = jnp.dot(
            mixer[:, : 2 * deep],
            jnp.concatenate([half, half], axis=0),
            preferred_element_type=F32,
        )
        rate = [r + drive for r in linear(u, mixed)]
        stack = jnp.concatenate(rate, axis=0)
        high = stack.astype(BF16)
        low = (stack - high.astype(F32)).astype(BF16)
        mixed = jnp.dot(
            mixer, jnp.concatenate([high, high, low], axis=0), preferred_element_type=F32
        )
        again = linear(rate, mixed)
        for v in range(NV):
            out[k, v] = rate[v] + 0.5 * TIME_STEP * again[v]

    def snaps(step, carry):
        for i in range(8):
            snap(step * 8 + i)
        return carry

    lax.fori_loop(0, count // 8, snaps, 0)


def after_kernel(parts, *refs):
    place, kern, gain, visc, coup, basis, cells, cos_lanes = refs[:8]
    own_ref, near_ref, sent_ref, last_ref = refs[8:12]
    bases = refs[12 : 12 + parts]
    deriv, partial, mixed, raw, cyc0, grooves, ends = refs[12 + parts :]
    chunks = own_ref.shape[0]
    passages = kern.shape[0]
    me = place[0]
    base = me - lax.rem(me, 2)
    bits = passages.bit_length() - 2
    odd = me % 2 == 1
    speed = cells[0]
    damping = cells[2]
    ids = cells[3]
    half_speed = 0.5 * speed
    lane = iota((NX, LANES), 1)
    c16 = lane % 4
    masks = cycle_masks(ids).astype(BF16)
    masks_twice = jnp.concatenate([masks, masks], axis=0)
    scale = 1.0 / math.sqrt(NX * LANES)
    size = CHUNK * NX

    src = iota((LANES, LANES), 0)
    dst = iota((LANES, LANES), 1) // 4 * 4
    mixers = [(src == dst) | (src == dst + 1), (src == dst + 2) | (src == dst + 3)]
    mixers += [src == dst + 2, src == dst + 1, src == dst + 3, src == dst]
    mix = jnp.concatenate([jnp.where(m, 1.0, 0.0).astype(BF16) for m in mixers], axis=1)
    pick_snap = jnp.where(iota((size, LANES), 1) == iota((size, LANES), 0) // NX * 4, 1.0, 0.0)
    pick_snap = pick_snap.astype(BF16)
    wide = 4 * NRING * NX
    same_x = iota((size, wide), 0) % NX == iota((size, wide), 1) % NX

    def flat_basis():
        return flat(basis, 0, basis.shape[0])

    def unpack_right(t):
        return jnp.concatenate([t, roll(t, -2, 1)], axis=0)

    def unpack_left(t):
        return jnp.concatenate([t, roll(t, 2, 1)], axis=0)

    def chunk_step(chunk, carry):
        first = chunk * CHUNK
        head = EDGE + COORD
        half = passages // 2 * BLOB
        raw[:half, :] = sent_ref[chunk, head:, :].astype(F32)
        raw[half:, :] = last_ref[chunk, head:, :].astype(F32)
        summed = sent_ref[chunk, EDGE:head, :].astype(F32)
        summed += last_ref[chunk, EDGE:head, :].astype(F32)
        partial[chunk, :8, :] = summed[:8] + summed[8:]
        mixed[...] = jnp.dot(raw[...].astype(BF16), mix, preferred_element_type=F32)

        def slot(offset):
            other = lax.rem(me + offset + passages, passages)
            flips = jnp.bitwise_xor(base, other)
            index = jnp.bitwise_and(flips, 1)
            for bit in range(bits):
                moved = jnp.bitwise_and(jnp.right_shift(flips, bit + 1), 1)
                index = index + jnp.left_shift(moved, bits - bit)
            return pl.multiple_of(index * BLOB, BLOB)

        def load(offset, carry):
            cyc0[pl.ds(pl.multiple_of(offset * 8, 8), 8), :] = mixed[pl.ds(slot(offset), 8), :LANES]
            return carry

        lax.fori_loop(0, passages, load, 0, unroll=passages <= 16)

        def plenum0(offset):
            total = jnp.zeros((8, LANES), F32)
            if passages <= 16 and isinstance(offset, int):
                for other in range(passages):
                    total += kern[(offset - other) % passages] * cyc0[other * 8 : other * 8 + 8, :]
                return total

            def add(other, total):
                weight = kern[lax.rem(offset - other + 2 * passages, passages)]
                return total + weight * cyc0[pl.ds(pl.multiple_of(other * 8, 8), 8), :]

            return lax.fori_loop(0, passages, add, total)

        row8 = iota((8, LANES), 0)
        lane8 = iota((8, LANES), 1)

        def second(offset, total):
            own = slot(offset)
            east, west = slot(offset + 1), slot(offset - 1)
            coefs = raw[pl.ds(own, 8), :]
            id_row = coefs[7:8, :].astype(jnp.int32)
            hit = (id_row == row8) & (lane8 < 32)
            left = jnp.concatenate(
                [jnp.where(hit, coefs[5:6, :], 0.0), jnp.where(hit, coefs[6:7, :], 0.0)], axis=0
            )
            right = jnp.concatenate(
                [
                    mixed[pl.ds(pl.multiple_of(east + 8, 8), 8), 2 * LANES : 3 * LANES],
                    mixed[pl.ds(pl.multiple_of(east + 8, 8), 8), 4 * LANES : 5 * LANES],
                    mixed[pl.ds(pl.multiple_of(west + 8, 8), 8), 3 * LANES : 4 * LANES],
                    mixed[pl.ds(pl.multiple_of(west + 8, 8), 8), 5 * LANES :],
                    jnp.zeros((LANES - 32, LANES), F32),
                ],
                axis=0,
            )
            edge = jnp.dot(left.astype(BF16), right.astype(BF16), preferred_element_type=F32)
            edge = (edge[:8] + edge[8:]) * scale
            count = jnp.where(lane8 == 32 + row8, coefs[5:6, :] + coefs[6:7, :], 0.0)
            count = jnp.sum(count, axis=1, keepdims=True) * (scale * gain[NV - 1])
            rate = mixed[pl.ds(own, 8), LANES : 2 * LANES] + edge + count * plenum0(offset)
            if isinstance(offset, int):
                start = cyc0[offset * 8 : offset * 8 + 8, :]
                weight = kern[-offset % passages]
            else:
                start = cyc0[pl.ds(pl.multiple_of(offset * 8, 8), 8), :]
                weight = kern[lax.rem(passages - offset, passages)]
            return total + weight * (start + TIME_STEP * rate)

        total = jnp.zeros((8, LANES), F32)
        if passages <= 16:
            for offset in range(passages):
                total = second(offset, total)
        else:
            total = lax.fori_loop(0, passages, second, total)
        own0, own1 = plenum0(0), total
        west0, east0 = plenum0(passages - 1), plenum0(1)

        stack = []
        for tile in (own0, own1):
            for piece in split(tile):
                stack += [jnp.broadcast_to(piece[g : g + 1], (NX, LANES)) for g in range(NRING)]
        stack = jnp.concatenate(stack, axis=0).astype(BF16)
        picked = lax.dot_general(pick_snap, stack, NT, preferred_element_type=F32)
        picked = jnp.where(same_x, picked, 0.0).astype(BF16)
        for stage in range(2):
            grooves[stage] = jnp.dot(
                picked[:, stage * wide // 2 : (stage + 1) * wide // 2],
                masks_twice,
                preferred_element_type=F32,
            )

        near = near_ref[chunk].astype(F32)
        own = own_ref[chunk].astype(F32)
        far = last_ref[chunk, :EDGE, :].astype(F32)
        west = jnp.where(odd, near[RIGHT], far)
        east = jnp.where(odd, far, near[LEFT])

        def param(side, index):
            t = side[40:48]
            low = t[:, index : index + 1] + t[:, index + 1 : index + 2]
            high = t[:, 64 + index : 65 + index] + t[:, 65 + index : 66 + index]
            return jnp.broadcast_to(jnp.concatenate([low, high], axis=0), (NX, LANES))

        speed_h, force_h, damp_h, ids_h = (
            jnp.where(c16 < 2, param(west, 2 * i), param(east, 2 * i)) for i in range(4)
        )
        groove_h = jnp.zeros((NX, LANES), F32)
        for g in range(NRING):
            value = jnp.where(c16 < 2, west0[g : g + 1], east0[g : g + 1])
            groove_h = jnp.where(ids_h == g, value, groove_h)
        cos_h = jnp.concatenate([cos_lanes[chunk]] * 2, axis=0)
        halo, ours, rates = [], [], []
        for v in range(NV):
            at = slice(8 * v, 8 * v + 8)
            halo.append(jnp.where(c16 < 2, unpack_right(west[at]), unpack_left(east[at])))
            ours.append(
                jnp.where(c16 < 2, unpack_right(own[RIGHT][at]), unpack_left(own[LEFT][at]))
            )
        for v in range(NV):
            h = halo[v]
            e = roll(jnp.where(c16 == 3, h, ours[v]), -1, 1)
            w = roll(jnp.where(c16 == 0, h, ours[v]), 1, 1)
            rate = visc[v] * (e + w + north_south(h) - 4.0 * h) - 0.5 * speed_h * (e - w)
            rate = rate - damp_h * h + gain[v] * groove_h + force_h * cos_h
            for other in range(NV):
                rate = rate + coup[v, other] * halo[other]
            rates.append(rate)

        def columns(field):
            tiles = [
                jnp.broadcast_to(field[:, c : c + 1], (NX, LANES))
                for c in (LANES - 2, LANES - 1, 0, 1)
            ]
            return jnp.where(
                c16 < 2,
                jnp.where(c16 == 0, tiles[0], tiles[1]),
                jnp.where(c16 == 2, tiles[2], tiles[3]),
            )

        def across(t):
            return jnp.where(c16 == 2, roll(t, 1, 1), roll(t, -1, 1))

        inner = (c16 == 1) | (c16 == 2)
        signed_speed = columns(half_speed) * jnp.where(c16 < 2, -1.0, 1.0)
        damp_e = columns(damping)
        half_step = 0.5 * TIME_STEP
        shifts = [
            jnp.where(inner, (visc[v] + signed_speed) * across(halo[v]), 0.0) for v in range(NV)
        ]
        for v in range(NV):
            change = shifts[v]
            rate = visc[v] * (north_south(change) - 4.0 * change) - damp_e * change
            for other in range(NV):
                rate = rate + coup[v, other] * shifts[other]
            rate = rate + (visc[v] + signed_speed) * across(rates[v])
            beside = jnp.where(c16 == 0, roll(change, -1, 1), roll(change, 1, 1))
            outer = (visc[v] + signed_speed) * beside
            ends[v] = jnp.where(inner, change + half_step * rate, half_step * outer)

        at_ends = (lane < 2) | (lane >= LANES - 2)
        damp_step = half_step * damping
        speed_step = half_step * half_speed
        diffuse = [half_step * visc[v] * gain[v] for v in range(NV)]
        couple = []
        for v in range(NV):
            total = coup[v, 0] * gain[0]
            for other in range(1, NV):
                total = total + coup[v, other] * gain[other]
            couple.append(half_step * total)

        def snap(k, share, index):
            at = pl.ds(pl.multiple_of(k * NX, NX), NX)
            m0, m1 = grooves[0, at, :], grooves[1, at, :]
            e = jnp.where(lane == LANES - 1, 0.0, roll(m0, -1, 1))
            w = jnp.where(lane == 0, 0.0, roll(m0, 1, 1))
            spread = LANES - 4 * k - 2
            lap = e + w + north_south(m0) - 4.0 * m0
            own = 0.5 * (m0 + m1) - speed_step * (e - w) - damp_step * m0
            for v in range(NV):
                total = share[index, v] + gain[v] * own + diffuse[v] * lap + couple[v] * m0
                total = total + jnp.where(at_ends, roll(ends[v], spread, 1), 0.0)
                deriv[first + k, v] = total.astype(BF16)

        done = 0
        for share in bases:
            count = share.shape[0] if chunks == 1 else CHUNK

            def snaps(step, carry, share=share, done=done):
                for i in range(count):
                    k = step * count + i
                    snap(done + k, share, k if chunks == 1 else first + k)
                return carry

            lax.fori_loop(0, count // count, snaps, 0)
            done += count
        partial[chunk, 8:, :] = project(flat(deriv, first, CHUNK), flat_basis())
        return carry

    if chunks == 1:
        chunk_step(0, 0)
    else:
        lax.fori_loop(0, chunks, chunk_step, 0)


def eliminate(system, columns):
    row = iota(system.shape, 0)
    for j in columns:
        pivot = system[j : j + 1, :] / system[j : j + 1, j : j + 1]
        factor = jnp.where(row == j, 0.0, jnp.broadcast_to(system[:, j : j + 1], system.shape))
        system = jnp.where(row == j, pivot, system - factor * pivot)
    return system


highest = functools.partial(lax.dot_general, precision=HIGH, preferred_element_type=F32)
NN = (((1,), (0,)), ((), ()))


def system_kernel(ridge, modes, coords_ref, deriv, kernel_ref, system_ref, deriv_out, sem):
    write = pltpu.make_async_copy(deriv, deriv_out, sem)
    write.start()
    coords = unpack(coords_ref, modes)
    snaps = coords.shape[0]
    gram = highest(coords, coords, NT)
    squares = coords * coords
    kernel = gram + 0.5 * (gram * gram + highest(squares, squares, NT))
    kernel_ref[...] = kernel
    same = iota((snaps, snaps), 0) == iota((snaps, snaps), 1)
    eye = jnp.where(same, 1.0, 0.0)
    system = jnp.concatenate([kernel + ridge * eye, eye], axis=1)
    system_ref[...] = eliminate(system, range(snaps // 4))
    write.wait()


def invert_kernel(system_ref, out_ref):
    snaps = system_ref.shape[0]
    out_ref[...] = eliminate(system_ref[...], range(snaps // 4, snaps * 5 // 8))


def weight_kernel(
    coords_ref, kernel_ref, system_ref, first_ref, second_ref, lin_ref, weights, fit
):
    snaps = kernel_ref.shape[0]
    inverse = eliminate(system_ref[...], range(snaps * 5 // 8, snaps))[:, snaps:]
    coords = unpack(coords_ref, first_ref.shape[0])
    design = highest(coords, first_ref[...], NN)
    design = design * (highest(coords, second_ref[...], NN) + lin_ref[...])
    weights[...] = highest(inverse, design, NN)
    fit[...] = highest(kernel_ref[...], inverse, NN)


def fit_kernel(
    place, rates_ref, coords_ref, weights, fit, reduced, operator, fitted, full, red
):
    modes = operator.shape[0]
    rates = unpack(rates_ref, modes)
    operator[...] = highest(rates, weights[...], (((0,), (0,)), ((), ())))
    full[...] = highest(fit[...], rates, NN)
    red[...] = jnp.concatenate([unpack(coords_ref, modes), rates], axis=1)
    each = fitted.shape[0]
    for i in range(each):
        at = pl.ds(place[0] * each + i, 1)
        fitted[i : i + 1, :] = full[at, :]
        reduced[i : i + 1, :] = red[at, :]


def body(
    states,
    basis,
    snapshot_times,
    pert_ids,
    pert_table,
    cycle_ids,
    groove_kernel,
    groove_gain,
    speed,
    force_amp,
    viscosity,
    coupling,
):
    snaps = states.shape[0]
    modes = basis.shape[0]
    chunks = snaps // CHUNK
    passages = lax.axis_size("passage")
    rounds = passages.bit_length() - 1
    position = lax.axis_index("passage")
    place = position.reshape(1).astype(jnp.int32)
    angles = 2.0 * math.pi * np.arange(PERIOD) / PERIOD
    table = jnp.asarray(np.cos(angles).astype(np.float32))

    def swap(value, mask):
        pairs = [(i, i ^ mask) for i in range(passages)]
        return lax.ppermute(value, "passage", pairs)

    def swap_chip(value, mask):
        return swap(value, mask + 1)

    operands = (
        snapshot_times,
        pert_ids,
        viscosity,
        coupling,
        table,
        pert_table,
        cycle_ids,
        speed,
        force_amp,
        states,
        basis,
    )
    first, held, held_basis, cells, cosines, cos_lanes = pl.pallas_call(
        before_kernel,
        out_shape=(
            jax.ShapeDtypeStruct((chunks, ROWS, LANES), BF16),
            jax.ShapeDtypeStruct(states.shape, BF16),
            jax.ShapeDtypeStruct(basis.shape, BF16),
            jax.ShapeDtypeStruct((4, NX, LANES), F32),
            jax.ShapeDtypeStruct((snaps, LANES), F32),
            jax.ShapeDtypeStruct((chunks, 8, LANES), F32),
        ),
        in_specs=[HBM] * len(operands),
        out_specs=(VMEM,) * 6,
        scratch_shapes=[pltpu.SMEM(x.shape, x.dtype) for x in operands[:5]]
        + [pltpu.VMEM(x.shape, x.dtype) for x in operands[5:9]]
        + [
            pltpu.VMEM((3 * CHUNK * NX, LANES), BF16),
            pltpu.SemaphoreType.DMA((len(operands),)),
        ],
        compiler_params=pltpu.CompilerParams(vmem_limit_bytes=24 * 2**20),
        name="before",
    )(*(x if x is pert_ids else pltpu.with_memory_space_constraint(x, pltpu.HBM) for x in operands))
    near = swap(first, 1)
    bits = rounds - 1
    edges_shape = jax.ShapeDtypeStruct((chunks, 2 * EDGE, LANES), BF16)
    head = EDGE + COORD

    def glue(kernel, name, rows, *args, more=True):
        outs = (jax.ShapeDtypeStruct((chunks, rows, LANES), BF16), edges_shape)
        return pl.pallas_call(
            kernel,
            out_shape=outs if more else outs[:1],
            in_specs=[SMEM] + [VMEM] * len(args),
            out_specs=(VMEM, VMEM) if more else (VMEM,),
            compiler_params=pltpu.CompilerParams(vmem_limit_bytes=16 * 2**20),
            name=name,
        )(place, *args)

    hidden = pl.CostEstimate(flops=2 * 10**9, bytes_accessed=2**20, transcendentals=0)
    anywhere = pl.BlockSpec(memory_space=pl.ANY)
    tile = jax.ShapeDtypeStruct((chunks, 8, LANES), F32)
    coords = pl.pallas_call(
        coords_kernel,
        out_shape=tile,
        in_specs=[VMEM, VMEM, anywhere],
        out_specs=VMEM,
        cost_estimate=hidden,
        compiler_params=pltpu.CompilerParams(vmem_limit_bytes=24 * 2**20),
        name="coords",
    )(held, held_basis, first)
    near, coords = lax.optimization_barrier((near, coords))

    def local(offset, count, after):
        return pl.pallas_call(
            functools.partial(local_kernel, offset),
            out_shape=jax.ShapeDtypeStruct((count,) + states.shape[1:], F32),
            in_specs=[VMEM] * 6 + [anywhere],
            out_specs=VMEM,
            cost_estimate=hidden,
            compiler_params=pltpu.CompilerParams(vmem_limit_bytes=24 * 2**20),
            name="local",
        )(
            held,
            cells,
            cosines,
            mixer,
            east_coef,
            west_coef,
            after,
        )

    start = functools.partial(start_kernel, bits - 1)
    message, edges = glue(start, "start", head + 2 * BLOB, first, near, coords)
    mixer, east_coef, west_coef = pl.pallas_call(
        prepare_kernel,
        out_shape=(
            jax.ShapeDtypeStruct((NV * NX, 3 * NV * NX), BF16),
            jax.ShapeDtypeStruct((NV, NX, LANES), F32),
            jax.ShapeDtypeStruct((NV, NX, LANES), F32),
        ),
        in_specs=[SMEM] * 4 + [VMEM, anywhere],
        out_specs=(VMEM, VMEM, VMEM),
        cost_estimate=hidden,
        compiler_params=pltpu.CompilerParams(vmem_limit_bytes=16 * 2**20),
        name="prepare",
    )(viscosity, coupling, groove_kernel, groove_gain, cells, message)
    shares = [8, 8, 16] if chunks == 1 and bits == 3 else [snaps]
    bases, offset = [], 0
    for bit in range(bits - 1, -1, -1):
        got = swap_chip(message, 2 << bit)
        if shares:
            count = shares.pop(0)
            base = local(offset, count, message)
            got, base = lax.optimization_barrier((got, base))
            bases.append(base)
            offset += count
        if bit:
            rows = 2 * message.shape[1] - head
            step = functools.partial(next_kernel, bit - 1)
            message, *edges = glue(step, "next", rows, message, got, edges, more=bit > 1)
            edges = edges[0] if edges else None

    derivative, partial = pl.pallas_call(
        functools.partial(after_kernel, len(bases)),
        out_shape=(
            jax.ShapeDtypeStruct(states.shape, BF16),
            jax.ShapeDtypeStruct((chunks, 16, LANES), F32),
        ),
        in_specs=[SMEM] * 5 + [VMEM] * (7 + len(bases)),
        out_specs=(VMEM, VMEM),
        scratch_shapes=[
            pltpu.VMEM((passages * BLOB, 6 * LANES), F32),
            pltpu.VMEM((passages * BLOB, LANES), F32),
            pltpu.VMEM((passages * 8, LANES), F32),
            pltpu.VMEM((2, CHUNK * NX, LANES), F32),
            pltpu.VMEM((NV, NX, LANES), F32),
        ],
        compiler_params=pltpu.CompilerParams(vmem_limit_bytes=32 * 2**20),
        name="after",
    )(
        place,
        groove_kernel,
        groove_gain,
        viscosity,
        coupling,
        held_basis,
        cells,
        cos_lanes,
        first,
        near,
        message,
        got,
        *bases,
    )

    upper_first, upper_second = np.triu_indices(modes)
    features = modes + len(upper_first)
    pick_first = np.zeros((modes, features), np.float32)
    pick_second = np.zeros((modes, features), np.float32)
    linear = np.zeros((1, features), np.float32)
    pick_first[np.arange(modes), np.arange(modes)] = 1.0
    linear[0, :modes] = 1.0
    pick_first[upper_first, modes + np.arange(len(upper_first))] = 1.0
    pick_second[upper_second, modes + np.arange(len(upper_first))] = 1.0

    def small(kernel, name, outs, *args):
        return pl.pallas_call(
            kernel,
            out_shape=tuple(jax.ShapeDtypeStruct(shape, F32) for shape in outs),
            in_specs=[VMEM] * len(args),
            out_specs=tuple(VMEM for _ in outs),
            cost_estimate=hidden,
            compiler_params=pltpu.CompilerParams(vmem_limit_bytes=16 * 2**20),
            name=name,
        )(*args)

    total = partial + swap(partial, 1)
    coords, total, derivative = lax.optimization_barrier((total[:, :8], total[:, 8:], derivative))
    kernel, system, derivative = pl.pallas_call(
        functools.partial(system_kernel, RIDGE_FACTOR * snaps, modes),
        out_shape=(
            jax.ShapeDtypeStruct((snaps, snaps), F32),
            jax.ShapeDtypeStruct((snaps, 2 * snaps), F32),
            jax.ShapeDtypeStruct(states.shape, BF16),
        ),
        in_specs=[VMEM, VMEM],
        out_specs=(VMEM, VMEM, HBM),
        scratch_shapes=[pltpu.SemaphoreType.DMA],
        cost_estimate=hidden,
        compiler_params=pltpu.CompilerParams(vmem_limit_bytes=16 * 2**20),
        name="system",
    )(coords, derivative)
    for r in range(1, rounds):
        got = swap_chip(total, 1 << r)
        if r == 1:
            got, kernel, system = lax.optimization_barrier((got, kernel, system))
            total = total + got
            (inverse,) = small(invert_kernel, "invert", [(snaps, 2 * snaps)], system)
        elif r == 2:
            total, inverse = lax.optimization_barrier((total + got, inverse))
            weights, fit = small(
                weight_kernel,
                "weights",
                [(snaps, features), (snaps, snaps)],
                coords,
                kernel,
                inverse,
                jnp.asarray(pick_first),
                jnp.asarray(pick_second),
                jnp.asarray(linear),
            )
        else:
            total = total + got
    each = snaps // passages
    reduced, operator, fitted = pl.pallas_call(
        fit_kernel,
        out_shape=(
            jax.ShapeDtypeStruct((each, 2 * modes), F32),
            jax.ShapeDtypeStruct((modes, features), F32),
            jax.ShapeDtypeStruct((each, modes), F32),
        ),
        in_specs=[SMEM] + [VMEM] * 4,
        out_specs=(VMEM, VMEM, VMEM),
        scratch_shapes=[pltpu.VMEM((snaps, modes), F32), pltpu.VMEM((snaps, 2 * modes), F32)],
        compiler_params=pltpu.CompilerParams(vmem_limit_bytes=16 * 2**20),
        name="fit",
    )(place, total, coords, weights, fit)
    return derivative, reduced, operator.T, fitted


def solution(mesh):
    in_specs = (
        P("member", None, None, "passage"),
        P(None, None, None, "passage"),
        P("member"),
        P(("member", "passage")),
        P(),
        P(None, "passage"),
        P(),
        P(),
        P(None, "passage"),
        P(None, "passage"),
        P(),
        P(),
    )
    out_specs = (
        P("member", None, None, "passage"),
        P(("member", "passage"), None),
        P("member", None),
        P(("member", "passage"), None),
    )
    return jax.shard_map(body, mesh=mesh, in_specs=in_specs, out_specs=out_specs, check_vma=False)
```

```python
import functools
import math

import jax
import jax.numpy as jnp
import numpy as np
from jax import lax
from jax.experimental import pallas as pl
from jax.experimental.pallas import tpu as pltpu
from jax.sharding import PartitionSpec as P

F32 = jnp.float32
BF16 = jnp.bfloat16
NRING = 5
NV = 5
NX = 16
LANES = 128
PERIOD = 37
TIME_STEP = 0.2
RIDGE_FACTOR = 1.0
UNROLL = 4
CHUNK = 32
BLOB = 16
COORD = 16
EDGE = 48
ROWS = BLOB + 2 * EDGE
RIGHT = slice(BLOB, BLOB + EDGE)
LEFT = slice(BLOB + EDGE, ROWS)

HIGH = lax.Precision.HIGHEST
NT = (((1,), (1,)), ((), ()))
VMEM = pl.BlockSpec(memory_space=pltpu.VMEM)
HBM = pl.BlockSpec(memory_space=pltpu.HBM)
SMEM = pl.BlockSpec(memory_space=pltpu.SMEM)


def iota(shape, axis):
    return lax.broadcasted_iota(jnp.int32, shape, axis)


def roll(value, shift, axis):
    size = value.shape[axis]
    return pltpu.roll(value, shift % size if isinstance(shift, int) else shift, axis)


def split(value):
    high = value.astype(BF16).astype(F32)
    return high, (value - high).astype(BF16).astype(F32)


def north_south(u):
    row = iota(u.shape, 0)
    north = jnp.where(row == NX - 1, 0.0, roll(u, -1, 0))
    south = jnp.where(row == 0, 0.0, roll(u, 1, 0))
    return north + south


def cycle_masks(ids):
    return jnp.concatenate([jnp.where(ids == g, 1.0, 0.0) for g in range(NRING)], axis=0)


def lane_part():
    return iota((8, LANES), 1) % 4


def flat(ref, first, count):
    parts = [ref[pl.ds(first, count), v].reshape(count * NX, LANES) for v in range(NV)]
    return jnp.concatenate(parts, axis=1)


def project(rows, modes_flat):
    width = modes_flat.shape[0]
    size = rows.shape[0]
    pairs = lax.dot_general(rows, modes_flat, NT, preferred_element_type=F32)
    diagonal = iota((size, width), 0) % NX == iota((size, width), 1) % NX
    pairs = jnp.where(diagonal, pairs, 0.0)
    pairs = jnp.sum(pairs.reshape(size // NX, NX, width), axis=1)
    high, low = split(pairs)
    modes = width // NX
    mode_of = iota((width, LANES), 0) // NX
    column = iota((width, LANES), 1)
    total = jnp.zeros((8, LANES), F32)
    for j in range(CHUNK // 8):
        pick = jnp.where(mode_of + j * modes == column, 1.0, 0.0).astype(BF16)
        both = jnp.concatenate([high[8 * j : 8 * j + 8], low[8 * j : 8 * j + 8]], axis=0)
        both = jnp.dot(both.astype(BF16), pick, preferred_element_type=F32)
        total += both[:8] + both[8:]
    return total


def unpack(ref, modes):
    rows = []
    for chunk in range(ref.shape[0]):
        tile = ref[chunk]
        rows += [tile[:, j * modes : (j + 1) * modes] for j in range(CHUNK // 8)]
    return jnp.concatenate(rows, axis=0)


def before_kernel(*refs):
    count = 11
    sources = refs[:count]
    out, states, basis, cells, cosines, cos_lanes = refs[count : count + 6]
    targets = (*refs[count + 6 : 2 * count + 4], states, basis)
    fields, sems = refs[2 * count + 4 :]
    copies = [
        pltpu.make_async_copy(source, target, sems.at[i])
        for i, (source, target) in enumerate(zip(sources, targets))
    ]
    for copy in copies:
        copy.start()
    times, pert_ids, visc, coup, table, pert, ids_ref, speed_ref, force_ref = targets[:-2]
    for copy in copies[:-2]:
        copy.wait()
    chunks = out.shape[0]
    speed = speed_ref[...]
    force = force_ref[...]
    damping = pert[pert_ids[0]]
    ids = ids_ref[...]
    visc_p = visc[NV - 1]
    lane = iota((NX, LANES), 1)
    half_speed = 0.5 * speed
    coef_east = jnp.where(lane == LANES - 1, 0.0, visc_p - half_speed)
    coef_west = jnp.where(lane == 0, 0.0, visc_p + half_speed)
    coef_own = coup[NV - 1, NV - 1] - 4.0 * visc_p - damping
    masks = cycle_masks(ids)
    masks_half = masks.astype(BF16)
    c8 = lane_part()
    row8 = iota((8, LANES), 0)
    quad = iota((NX, LANES), 1) // 4
    for index, field in enumerate((speed, force, damping, ids.astype(F32))):
        cells[index] = field
    scale = 1.0 / math.sqrt(NX * LANES)

    def pieces(column):
        out16 = jnp.zeros((NX, LANES), F32)
        spot = 0
        for field in (speed, force, damping, ids.astype(F32)):
            for piece in split(field):
                moved = roll(piece, spot - column, 1)
                out16 = jnp.where(lane == spot, moved, out16)
                spot += 1
        return jnp.where(iota((8, LANES), 1) < 64, out16[:8], roll(out16[8:], 64, 1))

    params_right = pieces(LANES - 1)
    params_left = pieces(0)

    east_hi, east_lo = split(jnp.where(lane == LANES - 1, visc_p - half_speed, 0.0))
    west_hi, west_lo = split(jnp.where(lane == 0, visc_p + half_speed, 0.0))
    ids_f = ids.astype(F32)
    id_east = jnp.where(lane == LANES - 1, ids_f, 0.0)
    id_west = jnp.where(lane == 0, ids_f, 0.0)
    ones = jnp.ones((NX, LANES), BF16)
    filler = jnp.zeros((LANES - 32, LANES), F32)

    def as_rows(east, west):
        stacked = jnp.concatenate([east, west, filler], axis=0).astype(BF16)
        return lax.dot_general(ones, stacked, NT, preferred_element_type=F32)[:8]

    row_hi = as_rows(east_hi, west_hi)
    row_lo = as_rows(east_lo, west_lo)
    row_id = as_rows(id_east, id_west)
    counts = lax.dot_general(ones, masks_half, NT, preferred_element_type=F32)[:8]
    spread = jnp.where(
        iota((NRING * NX, LANES), 1) == 32 + iota((NRING * NX, LANES), 0) // NX, 1.0, 0.0
    )
    counts = jnp.dot(counts, spread, precision=HIGH, preferred_element_type=F32)
    count_hi, count_lo = split(counts)
    row_hi = row_hi + count_hi
    row_lo = row_lo + count_lo

    size = CHUNK * NX
    same_x = iota((NRING * NX, 3 * size), 0) % NX == iota((NRING * NX, 3 * size), 1) % NX
    snap_of_row = iota((size, LANES), 0) // NX == iota((size, LANES), 1) // 4
    part_of_lane = iota((size, LANES), 1) % 4
    to_start = jnp.where(snap_of_row & (part_of_lane < 2), scale, 0.0)
    to_rate = jnp.where(snap_of_row & (part_of_lane >= 2), scale, 0.0)
    copies[-2].wait()

    def chunk_step(chunk, carry):
        first = chunk * CHUNK

        def snap(k, carried):
            edges, cos_row = carried
            u = [states[first + k, v].astype(F32) for v in range(NV)]
            p = u[NV - 1]
            cosine = table[lax.rem(times[first + k], PERIOD)]
            cosines[pl.ds(first + k, 1), :] = jnp.full((1, LANES), cosine, F32)
            cos_row = jnp.where(quad[:8] == k, cosine, cos_row)
            rate = coef_east * roll(p, -1, 1) + coef_west * roll(p, 1, 1)
            rate = rate + visc_p * north_south(p) + coef_own * p + cosine * force
            for v in range(NV - 1):
                rate = rate + coup[NV - 1, v] * u[v]
            high, low = split(rate)
            at = pl.multiple_of(k * NX, NX)
            fields[pl.ds(at, NX), :] = p.astype(BF16)
            fields[pl.ds(pl.multiple_of(size + at, NX), NX), :] = high.astype(BF16)
            fields[pl.ds(pl.multiple_of(2 * size + at, NX), NX), :] = low.astype(BF16)
            edges = tuple(
                jnp.where(quad == k, roll(u[v], 4 * k + 2, 1), edges[v]) for v in range(NV)
            )
            return edges, cos_row

        carried = tuple(jnp.zeros((NX, LANES), F32) for _ in range(NV)), jnp.zeros((8, LANES), F32)
        if chunks == 1:
            for k in range(CHUNK):
                carried = snap(k, carried)
        else:
            carried = lax.fori_loop(0, CHUNK, snap, carried)
        edges, cos_lanes[chunk] = carried
        sums = lax.dot_general(masks_half, fields[...], NT, preferred_element_type=F32)
        sums = jnp.where(same_x, sums, 0.0)
        by_cycle = jnp.sum(sums.reshape(NRING, NX, 3 * size), axis=1)
        by_cycle = jnp.concatenate([by_cycle, jnp.zeros((3, 3 * size), F32)], axis=0)
        start = by_cycle[:, :size]
        rate = by_cycle[:, size : 2 * size] + by_cycle[:, 2 * size :]
        packed = jnp.dot(start, to_start, precision=HIGH, preferred_element_type=F32)
        packed += jnp.dot(rate, to_rate, precision=HIGH, preferred_element_type=F32)
        high, low = split(packed)
        packed = jnp.where(c8 % 2 == 0, high, low)
        packed = jnp.where(row8 < NRING, packed, 0.0)
        for at, row in ((5, row_hi), (6, row_lo), (7, row_id)):
            packed = jnp.where(row8 == at, row, packed)
        p_low, p_high = edges[NV - 1][:8], edges[NV - 1][8:]
        p_edges = jnp.where(
            (c8 == 1) | (c8 == 2), p_low, jnp.where(c8 == 3, roll(p_high, 1, 1), roll(p_high, -1, 1))
        )
        right = [jnp.where(c8 < 2, t[:8], roll(t[8:], 2, 1)) for t in edges]
        left = [jnp.where(c8 >= 2, t[:8], roll(t[8:], -2, 1)) for t in edges]
        rows = [packed, p_edges, *right, params_right, *left, params_left]
        out[chunk] = jnp.concatenate(rows, axis=0).astype(BF16)
        return carry

    if chunks == 1:
        chunk_step(0, 0)
    else:
        lax.fori_loop(0, chunks, chunk_step, 0)
    copies[-1].wait()


def coords_kernel(states, basis, after, out):
    flat_basis = flat(basis, 0, basis.shape[0])
    if out.shape[0] == 1:
        out[0] = project(flat(states, 0, CHUNK), flat_basis)
        return

    def chunk_step(chunk, carry):
        out[chunk] = project(flat(states, chunk * CHUNK, CHUNK), flat_basis)
        return carry

    lax.fori_loop(0, out.shape[0], chunk_step, 0)


def start_kernel(top, place, first, near, coords, out, edges):
    odd = place[0] % 2 == 1
    for chunk in range(out.shape[0]):
        mine, other = first[chunk].astype(F32), near[chunk].astype(F32)
        low, high = jnp.where(odd, other, mine), jnp.where(odd, mine, other)
        right, left = high[RIGHT], low[LEFT]
        edges[chunk] = jnp.concatenate([right, left], axis=0).astype(BF16)
        payload = jnp.where(goes_right(place[0], top), right, left)
        rows = [payload, *split(coords[chunk]), low[:BLOB], high[:BLOB]]
        out[chunk] = jnp.concatenate(rows, axis=0).astype(BF16)


def goes_right(me, bit):
    if bit == 0:
        return me % 2 == 1
    lower = jnp.bitwise_and(jnp.right_shift(me, 1), (1 << bit) - 1)
    return lower == (1 << bit) - 1


def goes_left(me, bit):
    lower = jnp.bitwise_and(jnp.right_shift(me, 1), (1 << bit) - 1)
    return lower == 0


def next_kernel(bit, place, sent, got, edges, out, new_edges=None):
    me = place[0]
    for chunk in range(out.shape[0]):
        mine, other = sent[chunk].astype(F32), got[chunk].astype(F32)
        both = edges[chunk].astype(F32)
        right = jnp.where(goes_right(me, bit + 1), other[:EDGE], both[:EDGE])
        left = jnp.where(goes_left(me, bit + 1), other[:EDGE], both[EDGE:])
        if new_edges is not None:
            new_edges[chunk] = jnp.concatenate([right, left], axis=0).astype(BF16)
        payload = jnp.where(goes_right(me, bit), right, left)
        total = mine[EDGE : EDGE + COORD] + other[EDGE : EDGE + COORD]
        rows = [payload, *split(total[:8] + total[8:]), mine[EDGE + COORD :], other[EDGE + COORD :]]
        out[chunk] = jnp.concatenate(rows, axis=0).astype(BF16)


def prepare_kernel(visc, coup, kern, gain, cells, after, mixer, east_coef, west_coef, splats):
    scalars = [gain[v] for v in range(NV)] + [visc[v] for v in range(NV)]
    scalars += [coup[v, other] for v in range(NV) for other in range(NV)]
    scalars += [kern[p] for p in range(kern.shape[0])]
    for i, value in enumerate(scalars):
        splats[i : i + 1, :] = jnp.full((1, LANES), value, F32)
    half_speed = 0.5 * cells[0]
    lane = iota((NX, LANES), 1)
    for v in range(NV):
        east_coef[v] = jnp.where(lane == LANES - 1, 0.0, visc[v] - half_speed)
        west_coef[v] = jnp.where(lane == 0, 0.0, visc[v] + half_speed)
    deep = NV * NX
    col = iota((NX, 3 * deep), 1)
    col_var, col_x = col % deep // NX, col % NX
    row_x = iota((NX, 3 * deep), 0)
    beside = jnp.abs(row_x - col_x) == 1
    blocks = []
    for v in range(NV):
        weight = jnp.zeros((NX, 3 * deep), F32)
        for other in range(NV):
            value = coup[v, other] - (4.0 * visc[v] if other == v else 0.0)
            weight = jnp.where((col_var == other) & (row_x == col_x), value, weight)
        blocks.append(jnp.where((col_var == v) & beside, visc[v], weight))
    high, low = split(jnp.concatenate(blocks, axis=0))
    col = iota((deep, 3 * deep), 1)
    mixer[...] = jnp.where((col < deep) | (col >= 2 * deep), high, low).astype(BF16)


def local_kernel(
    offset,
    states,
    cells,
    cosines,
    mixer_ref,
    east_coef,
    west_coef,
    after,
    out,
):
    count = out.shape[0]
    deep = NV * NX
    force = cells[1]
    damping = cells[2]
    mixer = mixer_ref[...]

    def linear(u, mixed):
        result = []
        for v in range(NV):
            rate = mixed[NX * v : NX * v + NX] - damping * u[v]
            rate = rate + east_coef[v] * roll(u[v], -1, 1) + west_coef[v] * roll(u[v], 1, 1)
            result.append(rate)
        return result

    def snap(k):
        half = states[offset + k].reshape(deep, LANES)
        u = [states[offset + k, v].astype(F32) for v in range(NV)]
        drive = cosines[pl.ds(offset + k, 1), :] * force
        mixed = jnp.dot(
            mixer[:, : 2 * deep],
            jnp.concatenate([half, half], axis=0),
            preferred_element_type=F32,
        )
        rate = [r + drive for r in linear(u, mixed)]
        stack = jnp.concatenate(rate, axis=0)
        high = stack.astype(BF16)
        low = (stack - high.astype(F32)).astype(BF16)
        mixed = jnp.dot(
            mixer, jnp.concatenate([high, high, low], axis=0), preferred_element_type=F32
        )
        again = linear(rate, mixed)
        for v in range(NV):
            out[k, v] = rate[v] + 0.5 * TIME_STEP * again[v]

    def snaps(step, carry):
        for i in range(8):
            snap(step * 8 + i)
        return carry

    lax.fori_loop(0, count // 8, snaps, 0)


class Splats:
    def __init__(self, ref, first, shape):
        self.ref, self.first, self.shape = ref, first, shape

    def __getitem__(self, index):
        if isinstance(index, tuple):
            index = index[0] * self.shape[1] + index[1]
        return self.ref[pl.ds(self.first + index, 1), :]


def after_kernel(parts, *refs):
    place, splats, basis, cells, cos_lanes = refs[:5]
    own_ref, near_ref, sent_ref, last_ref = refs[5:9]
    bases = refs[9 : 9 + parts]
    deriv, partial, mixed, raw, cyc0, grooves, ends = refs[9 + parts :]
    gain, visc = Splats(splats, 0, (NV,)), Splats(splats, NV, (NV,))
    coup = Splats(splats, 2 * NV, (NV, NV))
    scalars = 2 * NV + NV * NV
    kern = Splats(splats, scalars, (splats.shape[0] - scalars,))
    chunks = own_ref.shape[0]
    passages = kern.shape[0]
    me = place[0]
    base = me - lax.rem(me, 2)
    bits = passages.bit_length() - 2
    odd = me % 2 == 1
    speed = cells[0]
    damping = cells[2]
    ids = cells[3]
    half_speed = 0.5 * speed
    lane = iota((NX, LANES), 1)
    c16 = lane % 4
    masks = cycle_masks(ids).astype(BF16)
    masks_twice = jnp.concatenate([masks, masks], axis=0)
    scale = 1.0 / math.sqrt(NX * LANES)
    size = CHUNK * NX

    src = iota((LANES, LANES), 0)
    dst = iota((LANES, LANES), 1) // 4 * 4
    mixers = [(src == dst) | (src == dst + 1), (src == dst + 2) | (src == dst + 3)]
    mixers += [src == dst + 2, src == dst + 1, src == dst + 3, src == dst]
    mix = jnp.concatenate([jnp.where(m, 1.0, 0.0).astype(BF16) for m in mixers], axis=1)
    pick_snap = jnp.where(iota((size, LANES), 1) == iota((size, LANES), 0) // NX * 4, 1.0, 0.0)
    pick_snap = pick_snap.astype(BF16)
    wide = 4 * NRING * NX
    same_x = iota((size, wide), 0) % NX == iota((size, wide), 1) % NX

    def flat_basis():
        return flat(basis, 0, basis.shape[0])

    def unpack_right(t):
        return jnp.concatenate([t, roll(t, -2, 1)], axis=0)

    def unpack_left(t):
        return jnp.concatenate([t, roll(t, 2, 1)], axis=0)

    def chunk_step(chunk, carry):
        first = chunk * CHUNK
        head = EDGE + COORD
        half = passages // 2 * BLOB
        raw[:half, :] = sent_ref[chunk, head:, :].astype(F32)
        raw[half:, :] = last_ref[chunk, head:, :].astype(F32)
        summed = sent_ref[chunk, EDGE:head, :].astype(F32)
        summed += last_ref[chunk, EDGE:head, :].astype(F32)
        partial[chunk, :8, :] = summed[:8] + summed[8:]
        mixed[...] = jnp.dot(raw[...].astype(BF16), mix, preferred_element_type=F32)

        def slot(offset):
            other = lax.rem(me + offset + passages, passages)
            flips = jnp.bitwise_xor(base, other)
            index = jnp.bitwise_and(flips, 1)
            for bit in range(bits):
                moved = jnp.bitwise_and(jnp.right_shift(flips, bit + 1), 1)
                index = index + jnp.left_shift(moved, bits - bit)
            return pl.multiple_of(index * BLOB, BLOB)

        def load(offset, carry):
            cyc0[pl.ds(pl.multiple_of(offset * 8, 8), 8), :] = mixed[pl.ds(slot(offset), 8), :LANES]
            return carry

        lax.fori_loop(0, passages, load, 0, unroll=passages <= 16)

        def plenum0(offset):
            total = jnp.zeros((8, LANES), F32)
            if passages <= 16 and isinstance(offset, int):
                for other in range(passages):
                    total += kern[(offset - other) % passages] * cyc0[other * 8 : other * 8 + 8, :]
                return total

            def add(other, total):
                weight = kern[lax.rem(offset - other + 2 * passages, passages)]
                return total + weight * cyc0[pl.ds(pl.multiple_of(other * 8, 8), 8), :]

            return lax.fori_loop(0, passages, add, total)

        row8 = iota((8, LANES), 0)
        lane8 = iota((8, LANES), 1)

        def second(offset, total):
            own = slot(offset)
            east, west = slot(offset + 1), slot(offset - 1)
            coefs = raw[pl.ds(own, 8), :]
            id_row = coefs[7:8, :].astype(jnp.int32)
            hit = (id_row == row8) & (lane8 < 32)
            left = jnp.concatenate(
                [jnp.where(hit, coefs[5:6, :], 0.0), jnp.where(hit, coefs[6:7, :], 0.0)], axis=0
            )
            right = jnp.concatenate(
                [
                    mixed[pl.ds(pl.multiple_of(east + 8, 8), 8), 2 * LANES : 3 * LANES],
                    mixed[pl.ds(pl.multiple_of(east + 8, 8), 8), 4 * LANES : 5 * LANES],
                    mixed[pl.ds(pl.multiple_of(west + 8, 8), 8), 3 * LANES : 4 * LANES],
                    mixed[pl.ds(pl.multiple_of(west + 8, 8), 8), 5 * LANES :],
                    jnp.zeros((LANES - 32, LANES), F32),
                ],
                axis=0,
            )
            edge = jnp.dot(left.astype(BF16), right.astype(BF16), preferred_element_type=F32)
            edge = (edge[:8] + edge[8:]) * scale
            count = jnp.where(lane8 == 32 + row8, coefs[5:6, :] + coefs[6:7, :], 0.0)
            count = jnp.sum(count, axis=1, keepdims=True) * (scale * gain[NV - 1])
            rate = mixed[pl.ds(own, 8), LANES : 2 * LANES] + edge + count * plenum0(offset)
            if isinstance(offset, int):
                start = cyc0[offset * 8 : offset * 8 + 8, :]
                weight = kern[-offset % passages]
            else:
                start = cyc0[pl.ds(pl.multiple_of(offset * 8, 8), 8), :]
                weight = kern[lax.rem(passages - offset, passages)]
            return total + weight * (start + TIME_STEP * rate)

        total = jnp.zeros((8, LANES), F32)
        if passages <= 16:
            for offset in range(passages):
                total = second(offset, total)
        else:
            total = lax.fori_loop(0, passages, second, total)
        own0, own1 = plenum0(0), total
        west0, east0 = plenum0(passages - 1), plenum0(1)

        stack = []
        for tile in (own0, own1):
            for piece in split(tile):
                stack += [jnp.broadcast_to(piece[g : g + 1], (NX, LANES)) for g in range(NRING)]
        stack = jnp.concatenate(stack, axis=0).astype(BF16)
        picked = lax.dot_general(pick_snap, stack, NT, preferred_element_type=F32)
        picked = jnp.where(same_x, picked, 0.0).astype(BF16)
        for stage in range(2):
            grooves[stage] = jnp.dot(
                picked[:, stage * wide // 2 : (stage + 1) * wide // 2],
                masks_twice,
                preferred_element_type=F32,
            )

        near = near_ref[chunk].astype(F32)
        own = own_ref[chunk].astype(F32)
        far = last_ref[chunk, :EDGE, :].astype(F32)
        west = jnp.where(odd, near[RIGHT], far)
        east = jnp.where(odd, far, near[LEFT])

        def param(side, index):
            t = side[40:48]
            low = t[:, index : index + 1] + t[:, index + 1 : index + 2]
            high = t[:, 64 + index : 65 + index] + t[:, 65 + index : 66 + index]
            return jnp.broadcast_to(jnp.concatenate([low, high], axis=0), (NX, LANES))

        speed_h, force_h, damp_h, ids_h = (
            jnp.where(c16 < 2, param(west, 2 * i), param(east, 2 * i)) for i in range(4)
        )
        groove_h = jnp.zeros((NX, LANES), F32)
        for g in range(NRING):
            value = jnp.where(c16 < 2, west0[g : g + 1], east0[g : g + 1])
            groove_h = jnp.where(ids_h == g, value, groove_h)
        cos_h = jnp.concatenate([cos_lanes[chunk]] * 2, axis=0)
        halo, ours, rates = [], [], []
        for v in range(NV):
            at = slice(8 * v, 8 * v + 8)
            halo.append(jnp.where(c16 < 2, unpack_right(west[at]), unpack_left(east[at])))
            ours.append(
                jnp.where(c16 < 2, unpack_right(own[RIGHT][at]), unpack_left(own[LEFT][at]))
            )
        for v in range(NV):
            h = halo[v]
            e = roll(jnp.where(c16 == 3, h, ours[v]), -1, 1)
            w = roll(jnp.where(c16 == 0, h, ours[v]), 1, 1)
            rate = visc[v] * (e + w + north_south(h) - 4.0 * h) - 0.5 * speed_h * (e - w)
            rate = rate - damp_h * h + gain[v] * groove_h + force_h * cos_h
            for other in range(NV):
                rate = rate + coup[v, other] * halo[other]
            rates.append(rate)

        def columns(field):
            tiles = [
                jnp.broadcast_to(field[:, c : c + 1], (NX, LANES))
                for c in (LANES - 2, LANES - 1, 0, 1)
            ]
            return jnp.where(
                c16 < 2,
                jnp.where(c16 == 0, tiles[0], tiles[1]),
                jnp.where(c16 == 2, tiles[2], tiles[3]),
            )

        def across(t):
            return jnp.where(c16 == 2, roll(t, 1, 1), roll(t, -1, 1))

        inner = (c16 == 1) | (c16 == 2)
        signed_speed = columns(half_speed) * jnp.where(c16 < 2, -1.0, 1.0)
        damp_e = columns(damping)
        half_step = 0.5 * TIME_STEP
        shifts = [
            jnp.where(inner, (visc[v] + signed_speed) * across(halo[v]), 0.0) for v in range(NV)
        ]
        for v in range(NV):
            change = shifts[v]
            rate = visc[v] * (north_south(change) - 4.0 * change) - damp_e * change
            for other in range(NV):
                rate = rate + coup[v, other] * shifts[other]
            rate = rate + (visc[v] + signed_speed) * across(rates[v])
            beside = jnp.where(c16 == 0, roll(change, -1, 1), roll(change, 1, 1))
            outer = (visc[v] + signed_speed) * beside
            ends[v] = jnp.where(inner, change + half_step * rate, half_step * outer)

        at_ends = (lane < 2) | (lane >= LANES - 2)
        damp_step = half_step * damping
        speed_step = half_step * half_speed
        diffuse = [half_step * visc[v] * gain[v] for v in range(NV)]
        couple = []
        for v in range(NV):
            total = coup[v, 0] * gain[0]
            for other in range(1, NV):
                total = total + coup[v, other] * gain[other]
            couple.append(half_step * total)

        def snap(k, share, index):
            at = pl.ds(pl.multiple_of(k * NX, NX), NX)
            m0, m1 = grooves[0, at, :], grooves[1, at, :]
            e = jnp.where(lane == LANES - 1, 0.0, roll(m0, -1, 1))
            w = jnp.where(lane == 0, 0.0, roll(m0, 1, 1))
            spread = LANES - 4 * k - 2
            lap = e + w + north_south(m0) - 4.0 * m0
            own = 0.5 * (m0 + m1) - speed_step * (e - w) - damp_step * m0
            for v in range(NV):
                total = share[index, v] + gain[v] * own + diffuse[v] * lap + couple[v] * m0
                total = total + jnp.where(at_ends, roll(ends[v], spread, 1), 0.0)
                deriv[first + k, v] = total.astype(BF16)

        done = 0
        for share in bases:
            count = share.shape[0] if chunks == 1 else CHUNK

            def snaps(step, carry, share=share, done=done):
                for i in range(count):
                    k = step * count + i
                    snap(done + k, share, k if chunks == 1 else first + k)
                return carry

            lax.fori_loop(0, count // count, snaps, 0)
            done += count
        partial[chunk, 8:, :] = project(flat(deriv, first, CHUNK), flat_basis())
        return carry

    if chunks == 1:
        chunk_step(0, 0)
    else:
        lax.fori_loop(0, chunks, chunk_step, 0)


def eliminate(system, columns):
    row = iota(system.shape, 0)
    for j in columns:
        pivot = system[j : j + 1, :] / system[j : j + 1, j : j + 1]
        factor = jnp.where(row == j, 0.0, jnp.broadcast_to(system[:, j : j + 1], system.shape))
        system = jnp.where(row == j, pivot, system - factor * pivot)
    return system


highest = functools.partial(lax.dot_general, precision=HIGH, preferred_element_type=F32)
NN = (((1,), (0,)), ((), ()))


def system_kernel(ridge, modes, coords_ref, deriv, kernel_ref, system_ref, deriv_out, sem):
    write = pltpu.make_async_copy(deriv, deriv_out, sem)
    write.start()
    coords = unpack(coords_ref, modes)
    snaps = coords.shape[0]
    gram = highest(coords, coords, NT)
    squares = coords * coords
    kernel = gram + 0.5 * (gram * gram + highest(squares, squares, NT))
    kernel_ref[...] = kernel
    same = iota((snaps, snaps), 0) == iota((snaps, snaps), 1)
    eye = jnp.where(same, 1.0, 0.0)
    system = jnp.concatenate([kernel + ridge * eye, eye], axis=1)
    system_ref[...] = eliminate(system, range(snaps // 4))
    write.wait()


def invert_kernel(system_ref, out_ref):
    snaps = system_ref.shape[0]
    out_ref[...] = eliminate(system_ref[...], range(snaps // 4, snaps * 5 // 8))


def weight_kernel(
    coords_ref, kernel_ref, system_ref, first_ref, second_ref, lin_ref, weights, fit
):
    snaps = kernel_ref.shape[0]
    inverse = eliminate(system_ref[...], range(snaps * 5 // 8, snaps))[:, snaps:]
    coords = unpack(coords_ref, first_ref.shape[0])
    design = highest(coords, first_ref[...], NN)
    design = design * (highest(coords, second_ref[...], NN) + lin_ref[...])
    weights[...] = highest(inverse, design, NN)
    fit[...] = highest(kernel_ref[...], inverse, NN)


def fit_kernel(
    place, rates_ref, coords_ref, weights, fit, reduced, operator, fitted, full, red
):
    modes = operator.shape[0]
    rates = unpack(rates_ref, modes)
    operator[...] = highest(rates, weights[...], (((0,), (0,)), ((), ())))
    full[...] = highest(fit[...], rates, NN)
    red[...] = jnp.concatenate([unpack(coords_ref, modes), rates], axis=1)
    each = fitted.shape[0]
    for i in range(each):
        at = pl.ds(place[0] * each + i, 1)
        fitted[i : i + 1, :] = full[at, :]
        reduced[i : i + 1, :] = red[at, :]


def body(
    states,
    basis,
    snapshot_times,
    pert_ids,
    pert_table,
    cycle_ids,
    groove_kernel,
    groove_gain,
    speed,
    force_amp,
    viscosity,
    coupling,
):
    snaps = states.shape[0]
    modes = basis.shape[0]
    chunks = snaps // CHUNK
    passages = lax.axis_size("passage")
    rounds = passages.bit_length() - 1
    position = lax.axis_index("passage")
    place = position.reshape(1).astype(jnp.int32)
    angles = 2.0 * math.pi * np.arange(PERIOD) / PERIOD
    table = jnp.asarray(np.cos(angles).astype(np.float32))

    def swap(value, mask):
        pairs = [(i, i ^ mask) for i in range(passages)]
        return lax.ppermute(value, "passage", pairs)

    def swap_chip(value, mask):
        return swap(value, mask + 1)

    operands = (
        snapshot_times,
        pert_ids,
        viscosity,
        coupling,
        table,
        pert_table,
        cycle_ids,
        speed,
        force_amp,
        states,
        basis,
    )
    first, held, held_basis, cells, cosines, cos_lanes = pl.pallas_call(
        before_kernel,
        out_shape=(
            jax.ShapeDtypeStruct((chunks, ROWS, LANES), BF16),
            jax.ShapeDtypeStruct(states.shape, BF16),
            jax.ShapeDtypeStruct(basis.shape, BF16),
            jax.ShapeDtypeStruct((4, NX, LANES), F32),
            jax.ShapeDtypeStruct((snaps, LANES), F32),
            jax.ShapeDtypeStruct((chunks, 8, LANES), F32),
        ),
        in_specs=[HBM] * len(operands),
        out_specs=(VMEM,) * 6,
        scratch_shapes=[pltpu.SMEM(x.shape, x.dtype) for x in operands[:5]]
        + [pltpu.VMEM(x.shape, x.dtype) for x in operands[5:9]]
        + [
            pltpu.VMEM((3 * CHUNK * NX, LANES), BF16),
            pltpu.SemaphoreType.DMA((len(operands),)),
        ],
        compiler_params=pltpu.CompilerParams(vmem_limit_bytes=24 * 2**20),
        name="before",
    )(*(x if x is pert_ids else pltpu.with_memory_space_constraint(x, pltpu.HBM) for x in operands))
    near = swap(first, 1)
    bits = rounds - 1
    edges_shape = jax.ShapeDtypeStruct((chunks, 2 * EDGE, LANES), BF16)
    head = EDGE + COORD

    def glue(kernel, name, rows, *args, more=True):
        outs = (jax.ShapeDtypeStruct((chunks, rows, LANES), BF16), edges_shape)
        return pl.pallas_call(
            kernel,
            out_shape=outs if more else outs[:1],
            in_specs=[SMEM] + [VMEM] * len(args),
            out_specs=(VMEM, VMEM) if more else (VMEM,),
            compiler_params=pltpu.CompilerParams(vmem_limit_bytes=16 * 2**20),
            name=name,
        )(place, *args)

    hidden = pl.CostEstimate(flops=2 * 10**9, bytes_accessed=2**20, transcendentals=0)
    anywhere = pl.BlockSpec(memory_space=pl.ANY)
    tile = jax.ShapeDtypeStruct((chunks, 8, LANES), F32)
    coords = pl.pallas_call(
        coords_kernel,
        out_shape=tile,
        in_specs=[VMEM, VMEM, anywhere],
        out_specs=VMEM,
        cost_estimate=hidden,
        compiler_params=pltpu.CompilerParams(vmem_limit_bytes=24 * 2**20),
        name="coords",
    )(held, held_basis, first)
    near, coords = lax.optimization_barrier((near, coords))

    def local(offset, count, after):
        return pl.pallas_call(
            functools.partial(local_kernel, offset),
            out_shape=jax.ShapeDtypeStruct((count,) + states.shape[1:], F32),
            in_specs=[VMEM] * 6 + [anywhere],
            out_specs=VMEM,
            cost_estimate=hidden,
            compiler_params=pltpu.CompilerParams(vmem_limit_bytes=24 * 2**20),
            name="local",
        )(
            held,
            cells,
            cosines,
            mixer,
            east_coef,
            west_coef,
            after,
        )

    start = functools.partial(start_kernel, bits - 1)
    message, edges = glue(start, "start", head + 2 * BLOB, first, near, coords)
    mixer, east_coef, west_coef, splats = pl.pallas_call(
        prepare_kernel,
        out_shape=(
            jax.ShapeDtypeStruct((NV * NX, 3 * NV * NX), BF16),
            jax.ShapeDtypeStruct((NV, NX, LANES), F32),
            jax.ShapeDtypeStruct((NV, NX, LANES), F32),
            jax.ShapeDtypeStruct((2 * NV + NV * NV + passages, LANES), F32),
        ),
        in_specs=[SMEM] * 4 + [VMEM, anywhere],
        out_specs=(VMEM,) * 4,
        cost_estimate=hidden,
        compiler_params=pltpu.CompilerParams(vmem_limit_bytes=16 * 2**20),
        name="prepare",
    )(viscosity, coupling, groove_kernel, groove_gain, cells, message)
    shares = [8, 8, 16] if chunks == 1 and bits == 3 else [snaps]
    bases, offset = [], 0
    for bit in range(bits - 1, -1, -1):
        got = swap_chip(message, 2 << bit)
        if shares:
            count = shares.pop(0)
            base = local(offset, count, message)
            got, base = lax.optimization_barrier((got, base))
            bases.append(base)
            offset += count
        if bit:
            rows = 2 * message.shape[1] - head
            step = functools.partial(next_kernel, bit - 1)
            message, *edges = glue(step, "next", rows, message, got, edges, more=bit > 1)
            edges = edges[0] if edges else None

    derivative, partial = pl.pallas_call(
        functools.partial(after_kernel, len(bases)),
        out_shape=(
            jax.ShapeDtypeStruct(states.shape, BF16),
            jax.ShapeDtypeStruct((chunks, 16, LANES), F32),
        ),
        in_specs=[SMEM] + [VMEM] * (8 + len(bases)),
        out_specs=(VMEM, VMEM),
        scratch_shapes=[
            pltpu.VMEM((passages * BLOB, 6 * LANES), F32),
            pltpu.VMEM((passages * BLOB, LANES), F32),
            pltpu.VMEM((passages * 8, LANES), F32),
            pltpu.VMEM((2, CHUNK * NX, LANES), F32),
            pltpu.VMEM((NV, NX, LANES), F32),
        ],
        compiler_params=pltpu.CompilerParams(vmem_limit_bytes=32 * 2**20),
        name="after",
    )(
        place,
        splats,
        held_basis,
        cells,
        cos_lanes,
        first,
        near,
        message,
        got,
        *bases,
    )

    upper_first, upper_second = np.triu_indices(modes)
    features = modes + len(upper_first)
    pick_first = np.zeros((modes, features), np.float32)
    pick_second = np.zeros((modes, features), np.float32)
    linear = np.zeros((1, features), np.float32)
    pick_first[np.arange(modes), np.arange(modes)] = 1.0
    linear[0, :modes] = 1.0
    pick_first[upper_first, modes + np.arange(len(upper_first))] = 1.0
    pick_second[upper_second, modes + np.arange(len(upper_first))] = 1.0

    def small(kernel, name, outs, *args):
        return pl.pallas_call(
            kernel,
            out_shape=tuple(jax.ShapeDtypeStruct(shape, F32) for shape in outs),
            in_specs=[VMEM] * len(args),
            out_specs=tuple(VMEM for _ in outs),
            cost_estimate=hidden,
            compiler_params=pltpu.CompilerParams(vmem_limit_bytes=16 * 2**20),
            name=name,
        )(*args)

    total = partial + swap(partial, 1)
    coords, total, derivative = lax.optimization_barrier((total[:, :8], total[:, 8:], derivative))
    kernel, system, derivative = pl.pallas_call(
        functools.partial(system_kernel, RIDGE_FACTOR * snaps, modes),
        out_shape=(
            jax.ShapeDtypeStruct((snaps, snaps), F32),
            jax.ShapeDtypeStruct((snaps, 2 * snaps), F32),
            jax.ShapeDtypeStruct(states.shape, BF16),
        ),
        in_specs=[VMEM, VMEM],
        out_specs=(VMEM, VMEM, HBM),
        scratch_shapes=[pltpu.SemaphoreType.DMA],
        cost_estimate=hidden,
        compiler_params=pltpu.CompilerParams(vmem_limit_bytes=16 * 2**20),
        name="system",
    )(coords, derivative)
    for r in range(1, rounds):
        got = swap_chip(total, 1 << r)
        if r == 1:
            got, kernel, system = lax.optimization_barrier((got, kernel, system))
            total = total + got
            (inverse,) = small(invert_kernel, "invert", [(snaps, 2 * snaps)], system)
        elif r == 2:
            total, inverse = lax.optimization_barrier((total + got, inverse))
            weights, fit = small(
                weight_kernel,
                "weights",
                [(snaps, features), (snaps, snaps)],
                coords,
                kernel,
                inverse,
                jnp.asarray(pick_first),
                jnp.asarray(pick_second),
                jnp.asarray(linear),
            )
        else:
            total = total + got
    each = snaps // passages
    reduced, operator, fitted = pl.pallas_call(
        fit_kernel,
        out_shape=(
            jax.ShapeDtypeStruct((each, 2 * modes), F32),
            jax.ShapeDtypeStruct((modes, features), F32),
            jax.ShapeDtypeStruct((each, modes), F32),
        ),
        in_specs=[SMEM] + [VMEM] * 4,
        out_specs=(VMEM, VMEM, VMEM),
        scratch_shapes=[pltpu.VMEM((snaps, modes), F32), pltpu.VMEM((snaps, 2 * modes), F32)],
        compiler_params=pltpu.CompilerParams(vmem_limit_bytes=16 * 2**20),
        name="fit",
    )(place, total, coords, weights, fit)
    return derivative, reduced, operator.T, fitted


def solution(mesh):
    in_specs = (
        P("member", None, None, "passage"),
        P(None, None, None, "passage"),
        P("member"),
        P(("member", "passage")),
        P(),
        P(None, "passage"),
        P(),
        P(),
        P(None, "passage"),
        P(None, "passage"),
        P(),
        P(),
    )
    out_specs = (
        P("member", None, None, "passage"),
        P(("member", "passage"), None),
        P("member", None),
        P(("member", "passage"), None),
    )
    return jax.shard_map(body, mesh=mesh, in_specs=in_specs, out_specs=out_specs, check_vma=False)
```
